32 devices in a mesh: sp: 8 (over z, y), fsdp: 4 (over x, core).
Axes of the slice: x: 2, y: 2, z: 4, core: 2. Of those that a mesh axis runs over, the one named last changes fastest.
Arguments:
- tokens: bfloat16 [4, 2048, 2048], P('fsdp', 'sp'), may hold values from -6 to 6
- doc_lengths: int32 [4, 4], P('fsdp'), may hold values from 1 to 1536, 2048 in all within a row
- expert_ids: int32 [4, 2048, 8], P('fsdp', 'sp'), may hold values from 0 to 63, all different within a row; in each aligned block of 256 rows (0 to 255, 256 to 511, ..., all dimensions but the last counted through in order) at most 64 rows name the same one
- norm_attn: bfloat16 [2048], P('fsdp'), may hold values from 0.5 to 1.5
- norm_query: bfloat16 [2048], P('fsdp'), may hold values from 0.5 to 1.5
- norm_key: bfloat16 [2048], P('fsdp'), may hold values from 0.5 to 1.5
- norm_ffn: bfloat16 [2048], P('fsdp'), may hold values from 0.5 to 1.5
- w_query: bfloat16 [2048, 2048], P('fsdp'), may hold values from -0.125 to 0.125
- w_key: bfloat16 [2048, 2048], P('fsdp'), may hold values from -0.125 to 0.125
- w_value: bfloat16 [2048, 2048], P('fsdp'), may hold values from -0.125 to 0.125
- w_out: bfloat16 [2048, 2048], P('fsdp'), may hold values from -4 to 4
- w_router: bfloat16 [2048, 64], P('fsdp'), may hold values from -0.0625 to 0.0625
- w_gate: bfloat16 [64, 2048, 1024], P('sp', None, 'fsdp'), may hold values from -0.125 to 0.125
- w_up: bfloat16 [64, 2048, 1024], P('sp', None, 'fsdp'), may hold values from -0.125 to 0.125
- w_down: bfloat16 [64, 2048, 1024], P('sp', None, 'fsdp'), may hold values from -6 to 6
- cotangent: bfloat16 [4, 2048, 2048], P('fsdp', 'sp'), may hold values from -6 to 6
Outputs:
- mixed: bfloat16 [4, 2048, 2048], P('fsdp', 'sp')
- grad_tokens: float32 [4, 2048, 2048], P('fsdp', 'sp')
- grad_norm_attn: float32 [2048], P('fsdp')
- grad_norm_query: float32 [2048], P('fsdp')
- grad_norm_key: float32 [2048], P('fsdp')
- grad_norm_ffn: float32 [2048], P('fsdp')
- grad_query: float32 [2048, 2048], P('fsdp')
- grad_key: float32 [2048, 2048], P('fsdp')
- grad_value: float32 [2048, 2048], P('fsdp')
- grad_out: float32 [2048, 2048], P('fsdp')
- grad_router: float32 [2048, 64], P('fsdp')
- grad_gate: float32 [64, 2048, 1024], P('sp', None, 'fsdp')
- grad_up: float32 [64, 2048, 1024], P('sp', None, 'fsdp')
- grad_down: float32 [64, 2048, 1024], P('sp', None, 'fsdp')
The draws below stay inside these ranges and needn't reach their ends.
Inputs may be any that keep to these rules, and one draw needn't show every extreme that they name: `expert_ids`: in the rows of one device, no expert is named by more than 64 of them, and in every draw some expert is named by exactly 64 rows of some device.
All inputs are finite; a program needn't handle non-finite values.
Results may differ from the reference program's by a relative error of at most 0.024.
Values may be sent and summed in bfloat16 or wider, within the bound.
A program may use at most 512 MiB of HBM per device.

```python
import math
from functools import partial
import jax
import jax.numpy as jnp
import numpy as np
from jax import lax

D = 2048
HEADS = 16
HEAD_DIM = 128
FF = 1024
EXPERTS = 64
TOPK = 8
WINDOW = 1024
NDOC = 4
SEQ_LEN = 2048
TOK_DEV = 256
SEQS = 4
MOST = 64
CAP = 1280


def block_scale(own_key, dims, shards, least, high):
    level = 1.0
    for dim, shards_of in shards:
        steps = jax.random.uniform(jax.random.fold_in(jax.random.fold_in(own_key, 6), dim), (shards_of,), jnp.float32, least / len(shards), high / len(shards))
        level = level * jnp.repeat(jnp.exp(steps), dims[dim] // shards_of).reshape((-1,) + (1,) * (len(dims) - 1 - dim))
    return level


def length_profile(amount, total, reach, lean):
    loads = [(1 << 20) // math.isqrt(grade ** lean) + 1 for grade in range(2, amount + 1)]
    rest, given = total - reach - (amount - 1), [1] * (amount - 1)
    while rest > 0:
        free = [i for i in range(amount - 1) if given[i] < reach]
        pool, left = sum([loads[i] for i in free]), rest
        for i in free:
            addition = min(reach - given[i], max(1, left * loads[i] // pool), rest)
            given[i] = given[i] + addition
            rest = rest - addition
    return np.array([reach] + given)


def uneven_parts(rng, amount, total, reach, slope):
    if amount == 2:
        one = jax.random.randint(rng, (), max(1, total - reach), min(reach, total - 1) + 1)
        return jnp.stack([one, total - one])
    lengths = jnp.asarray(length_profile(amount, total, reach, slope), jnp.int32)
    pairs = (amount - 1) // 2
    giver, receiver = lengths[1:1 + 2 * pairs:2], lengths[2:2 + 2 * pairs:2]
    room = jnp.minimum(giver - 1, reach - receiver)
    shifted = jax.random.randint(jax.random.fold_in(rng, 1), (pairs,), 0, 1 << 20) % (room + 1)
    lengths = lengths.at[1:1 + 2 * pairs:2].set(giver - shifted).at[2:2 + 2 * pairs:2].set(receiver + shifted)
    return lengths[jax.random.permutation(jax.random.fold_in(rng, 2), amount)]


def shared_out(key, own, number, rows, amount, top, bound, lean):
    ranking = jax.random.permutation(key, amount)
    heavy_load, usual = shares(amount, rows * top, bound, lean, True), shares(amount, rows * top, bound, lean, False)
    places = jnp.arange(amount)

    def named(lengths, rotation):
        used = int((lengths > 0).sum())
        fixed = max(1, used // 4)
        moved = fixed + (places - fixed + rotation * (used - fixed)) % max(1, amount - fixed)
        return jnp.zeros((amount,), jnp.int32).at[ranking[jnp.where(places < fixed, places, moved)]].set(jnp.asarray(lengths, jnp.int32))

    lengths = jnp.where(number % 4 == 0, named(heavy_load, number // 4), named(usual, number - number // 4 - 1))
    mixed = jax.random.permutation(jax.random.fold_in(own, 3), amount)
    giver, sink = mixed[0:amount // 2 * 2:2], mixed[1:amount // 2 * 2:2]
    room = jnp.minimum(lengths[giver] - 1, bound - lengths[sink]) // 2
    room = jnp.where((giver == ranking[0]) | (sink == ranking[0]) | (lengths[sink] == 0), 0, jnp.maximum(room, 0))
    moved = jax.random.randint(jax.random.fold_in(own, 4), (amount // 2,), 0, 1 << 20) % (room + 1)
    lengths = lengths.at[giver].add(-moved).at[sink].add(moved)
    members = jnp.searchsorted(jnp.cumsum(lengths), jnp.arange(rows * top), side="right").astype(jnp.int32)
    grid = members.reshape(top, rows).T
    grid = grid[jax.random.permutation(jax.random.fold_in(own, 1), rows)]
    rotation = jax.random.randint(jax.random.fold_in(own, 2), (rows, 1), 0, top)
    return jnp.take_along_axis(grid, (jnp.arange(top)[None, :] + rotation) % top, axis=1)


def shares(number_of, total, reach, lean, full):
    loads = [(1 << 20) // math.isqrt(grade ** lean) + 1 for grade in range(1, number_of + 1)]
    largest = reach if full else min(reach, max(-(-total // number_of), total * loads[0] // sum(loads)))
    least = 1 if total - largest >= number_of - 1 else 0
    counts, surplus = [largest] + [least] * (number_of - 1), total - largest - least * (number_of - 1)
    while surplus > 0:
        candidates = [i for i in range(1, number_of) if counts[i] < largest] or [i for i in range(1, number_of) if counts[i] < reach]
        whole, budget = sum([loads[i] for i in candidates]), surplus
        for i in candidates:
            more = min(reach - counts[i], max(1, budget * loads[i] // whole), surplus)
            counts[i] = counts[i] + more
            surplus = surplus - more
    return np.array(counts)


def noise(own_key, extent, deviation, most, cuts=(), held_as=jnp.bfloat16):
    values = deviation * jax.random.normal(own_key, extent, jnp.float32)
    if cuts:
        values = values * block_scale(own_key, extent, cuts, -0.22, 0.18)
    return jnp.clip(values, -most, most).astype(held_as)


def setup_inputs(seed: int = 0) -> dict:
    splits = jax.random.split(jax.random.key(seed), 17)
    tokens = noise(splits[0], (SEQS, SEQ_LEN, D), 1.0, 6.0, ((0, 4), (1, 8)))
    doc_lengths = jax.vmap(lambda own: uneven_parts(own, NDOC, SEQ_LEN, (3 * SEQ_LEN) // 4, 2))(jax.random.split(splits[1], SEQS)).reshape((SEQS, NDOC)).astype(jnp.int32)
    expert_ids_keys = jax.random.split(jax.random.fold_in(splits[2], 1), SEQS * SEQ_LEN // TOK_DEV)
    expert_ids_turns = jax.random.permutation(jax.random.fold_in(splits[2], 3), SEQS * SEQ_LEN // TOK_DEV)
    expert_ids = jax.vmap(lambda own, number: shared_out(jax.random.fold_in(splits[2], 2), own, number, TOK_DEV, EXPERTS, TOPK, MOST, 2))(expert_ids_keys, expert_ids_turns).reshape((SEQS, SEQ_LEN, TOPK))
    norm_attn = jnp.clip(1.0 + 0.1 * jax.random.normal(splits[3], (D,), jnp.float32), 0.5, 1.5).astype(jnp.bfloat16)
    norm_query = jnp.clip(1.0 + 0.1 * jax.random.normal(splits[4], (D,), jnp.float32), 0.5, 1.5).astype(jnp.bfloat16)
    norm_key = jnp.clip(1.0 + 0.1 * jax.random.normal(splits[5], (D,), jnp.float32), 0.5, 1.5).astype(jnp.bfloat16)
    norm_ffn = jnp.clip(1.0 + 0.1 * jax.random.normal(splits[6], (D,), jnp.float32), 0.5, 1.5).astype(jnp.bfloat16)
    w_query = noise(splits[7], (D, D), D ** -0.5, 0.125, ((0, 4),))
    w_key = noise(splits[8], (D, D), D ** -0.5, 0.125, ((0, 4),))
    w_value = noise(splits[9], (D, D), D ** -0.5, 0.125, ((0, 4),))
    w_out = noise(splits[10], (D, D), (max(1, D // WINDOW)) ** -0.5, 4.0, ((0, 4),))
    w_router = noise(splits[11], (D, EXPERTS), (4 * D) ** -0.5, 0.0625, ((0, 4),))
    w_gate = noise(splits[12], (EXPERTS, D, FF), D ** -0.5, 0.125, ((0, 8), (2, 4)))
    w_up = noise(splits[13], (EXPERTS, D, FF), D ** -0.5, 0.125, ((0, 8), (2, 4)))
    w_down = noise(splits[14], (EXPERTS, D, FF), (2 * EXPERTS / (TOPK * FF) ** 0.5), 6.0, ((0, 8), (2, 4)))
    cotangent = noise(splits[15], (SEQS, SEQ_LEN, D), 1.0, 6.0, ((0, 4), (1, 8)))
    return {"tokens": tokens, "doc_lengths": doc_lengths, "expert_ids": expert_ids, "norm_attn": norm_attn, "norm_query": norm_query, "norm_key": norm_key, "norm_ffn": norm_ffn, "w_query": w_query, "w_key": w_key, "w_value": w_value, "w_out": w_out, "w_router": w_router, "w_gate": w_gate, "w_up": w_up, "w_down": w_down, "cotangent": cotangent}


eps = 1e-05
rope_base = 10000.0
masked_score = -1e+30

@jax.custom_vjp
def low(v):
    return lax.optimization_barrier(v.astype(jnp.bfloat16)).astype(jnp.float32)

@jax.custom_vjp
def low_back(v):
    return v

def low_keep(v):
    return (low(v), None)

def low_pass(kept, grad):
    return (grad,)

def back_keep(v):
    return (v, None)

def back_low(kept, grad):
    return (low(grad),)
low.defvjp(low_keep, low_pass)
low_back.defvjp(back_keep, back_low)

def matmul_high(left, right):
    return jnp.dot(left, right, precision=lax.Precision.HIGHEST, preferred_element_type=jnp.float32)

def rms_scale(values, gain_vec):
    return values * lax.rsqrt(lax.optimization_barrier(jnp.mean(values * values, axis=-1, keepdims=True)) + eps) * gain_vec

def rotate_pairs(values, cosine, sine):
    half_dim = values.shape[-1] // 2
    turned = jnp.concatenate([-values[..., half_dim:], values[..., :half_dim]], axis=-1)
    return values * cosine + turned * sine

def rope_tables(positions, head_size):
    inv_freq = rope_base ** (-jnp.arange(0, head_size, 2, dtype=jnp.float32) / head_size)
    phase_half = positions.astype(jnp.float32)[:, None] * inv_freq[None, :]
    phase_all = jnp.concatenate([phase_half, phase_half], axis=-1)
    return (jnp.cos(phase_all)[:, None, :], jnp.sin(phase_all)[:, None, :])

def segment_ids(lengths_row, seq_rows):
    doc_ends = jnp.cumsum(lengths_row)
    positions = jnp.arange(seq_rows, dtype=jnp.int32)
    return lax.optimization_barrier(jnp.sum((positions[:, None] >= doc_ends[None, :]).astype(jnp.int32), axis=1))

def window_geometry(seq_rows):
    block_rows = min(512, seq_rows)
    key_blocks = 1 + (WINDOW - 1 + block_rows - 1) // block_rows
    return (block_rows, seq_rows // block_rows, key_blocks * block_rows, (key_blocks - 1) * block_rows)

def window_allowed(segments, seg_padded, first_row, block_rows, key_rows, pad_rows):
    query_pos = first_row + jnp.arange(block_rows, dtype=jnp.int32)
    key_pos = first_row - pad_rows + jnp.arange(key_rows, dtype=jnp.int32)
    query_seg = lax.dynamic_slice_in_dim(segments, first_row, block_rows)
    key_seg = lax.dynamic_slice_in_dim(seg_padded, first_row, key_rows)
    distance = query_pos[:, None] - key_pos[None, :]
    return (query_seg[:, None] == key_seg[None, :]) & (distance >= 0) & (distance < WINDOW)

def attend_sequence(pieces):
    query_seq, key_seq, value_seq, lengths_row = pieces
    seq_rows = query_seq.shape[0]
    block_rows, block_count, key_rows, pad_rows = window_geometry(seq_rows)
    segments = segment_ids(lengths_row, seq_rows)
    seg_padded = jnp.concatenate([jnp.full((pad_rows,), -1, jnp.int32), segments])
    pad_zero = jnp.zeros((pad_rows,) + key_seq.shape[1:], jnp.float32)
    key_padded = jnp.concatenate([pad_zero, key_seq], axis=0)
    value_padded = jnp.concatenate([pad_zero, value_seq], axis=0)
    score_scale = HEAD_DIM ** (-0.5)

    def one_block(block_index):
        first_row = block_index * block_rows
        query_block = lax.dynamic_slice_in_dim(query_seq, first_row, block_rows)
        key_block = lax.dynamic_slice_in_dim(key_padded, first_row, key_rows)
        value_block = lax.dynamic_slice_in_dim(value_padded, first_row, key_rows)
        scores = low_back(jnp.einsum('qhd,khd->hqk', query_block, key_block, precision=lax.Precision.HIGHEST) * score_scale)
        allowed = window_allowed(segments, seg_padded, first_row, block_rows, key_rows, pad_rows)
        scores = jnp.where(allowed[None], scores, masked_score)
        weights = low(jax.nn.softmax(scores, axis=-1))
        return low_back(low(jnp.einsum('hqk,khd->qhd', weights, value_block, precision=lax.Precision.HIGHEST)))
    blocks = lax.map(jax.checkpoint(one_block), jnp.arange(block_count, dtype=jnp.int32))
    return blocks.reshape(query_seq.shape)

def forward(hidden, norm_attn, norm_query, norm_key, norm_ffn, w_query, w_key, w_value, w_out, w_router, w_gate, w_up, w_down, doc_lengths, expert_ids):
    seqs, seq_rows, width = hidden.shape
    flat_in = hidden.reshape(-1, width)
    attn_in = low(rms_scale(flat_in, norm_attn))
    query_raw = low_back(matmul_high(attn_in, w_query))
    key_raw = low_back(matmul_high(attn_in, w_key))
    value_all = low_back(low(matmul_high(attn_in, w_value))).reshape(seqs, seq_rows, HEADS, HEAD_DIM)
    cosine, sine = rope_tables(jnp.arange(seq_rows, dtype=jnp.int32), HEAD_DIM)

    def rotated(raw_proj, gain_vec):
        shaped = rms_scale(raw_proj, gain_vec).reshape(seqs, seq_rows, HEADS, HEAD_DIM)
        return low_back(low(rotate_pairs(shaped, cosine, sine)))
    attended = lax.map(attend_sequence, (rotated(query_raw, norm_query), rotated(key_raw, norm_key), value_all, doc_lengths))
    after_attn = flat_in + low_back(matmul_high(attended.reshape(-1, width), w_out))
    ffn_in = low(rms_scale(after_attn, norm_ffn))
    logits = low_back(matmul_high(ffn_in, w_router))
    router = jax.nn.softmax(logits, axis=-1)
    ids_flat = expert_ids.reshape(-1, TOPK)
    gate_flat = jnp.take_along_axis(router, ids_flat, axis=1).reshape(-1)
    expert_flat = ids_flat.reshape(-1)
    pair_count = expert_flat.shape[0]
    onehot_pairs = (expert_flat[:, None] == jnp.arange(EXPERTS, dtype=jnp.int32)[None, :]).astype(jnp.int32)
    place = lax.optimization_barrier(jnp.sum((jnp.cumsum(onehot_pairs, axis=0) - 1) * onehot_pairs, axis=1))
    pair_numbers = jnp.arange(pair_count, dtype=jnp.int32)
    slot_pair = jnp.zeros((EXPERTS, CAP), jnp.int32).at[expert_flat, place].set(pair_numbers, mode='drop')
    slot_live = jnp.zeros((EXPERTS, CAP), jnp.float32).at[expert_flat, place].set(1.0, mode='drop')

    def one_expert(pieces):
        pairs_one, live_one, gate_mat, up_mat, down_mat = pieces
        token_rows = pairs_one // TOPK
        rows_in = low_back(ffn_in[token_rows])
        gate_pre = low_back(matmul_high(rows_in, gate_mat))
        up_pre = low_back(matmul_high(rows_in, up_mat))
        act_rows = low(jax.nn.silu(gate_pre) * up_pre)
        expert_out = low_back(low(matmul_high(act_rows, down_mat.T)))
        return expert_out * (gate_flat[pairs_one] * live_one)[:, None]
    weighted = lax.map(jax.checkpoint(one_expert), (slot_pair, slot_live, w_gate, w_up, w_down))
    moe_sum = jnp.zeros_like(after_attn).at[(slot_pair // TOPK).reshape(-1)].add(weighted.reshape(-1, width))
    return (after_attn + moe_sum).reshape(hidden.shape)

def reference(tokens, doc_lengths, expert_ids, norm_attn, norm_query, norm_key, norm_ffn, w_query, w_key, w_value, w_out, w_router, w_gate, w_up, w_down, cotangent):
    closed = partial(forward, doc_lengths=doc_lengths, expert_ids=expert_ids)
    result, pullback = jax.vjp(closed, tokens.astype(jnp.float32), norm_attn.astype(jnp.float32), norm_query.astype(jnp.float32), norm_key.astype(jnp.float32), norm_ffn.astype(jnp.float32), w_query.astype(jnp.float32), w_key.astype(jnp.float32), w_value.astype(jnp.float32), w_out.astype(jnp.float32), w_router.astype(jnp.float32), w_gate.astype(jnp.float32), w_up.astype(jnp.float32), w_down.astype(jnp.float32))
    grads = pullback(cotangent.astype(jnp.float32))
    return (result.astype(jnp.bfloat16), grads[0], grads[1], grads[2], grads[3], grads[4], grads[5], grads[6], grads[7], grads[8], grads[9], grads[10], grads[11], grads[12])
```

```python
import jax
import jax.numpy as jnp
from jax import lax
from jax.experimental import pallas as pl
from jax.experimental.pallas import tpu as pltpu
from jax.sharding import PartitionSpec as P

HEADS = 16
HEAD_DIM = 128
EXPERTS = 64
TOPK = 8
WINDOW = 1024


eps = 1e-05
rope_base = 10000.0
masked_score = -1e30


def rms_scale(values, gain_vec):
    return values * lax.rsqrt(jnp.mean(values * values, axis=-1, keepdims=True) + eps) * gain_vec


def rotate_pairs(values, cosine, sine):
    half_dim = values.shape[-1] // 2
    turned = jnp.concatenate([-values[..., half_dim:], values[..., :half_dim]], axis=-1)
    return values * cosine + turned * sine


def rope_tables(positions, head_size):
    inv_freq = rope_base ** (-jnp.arange(0, head_size, 2, dtype=jnp.float32) / head_size)
    phase_half = positions.astype(jnp.float32)[:, None] * inv_freq[None, :]
    phase_all = jnp.concatenate([phase_half, phase_half], axis=-1)
    return (jnp.cos(phase_all)[:, None, :], jnp.sin(phase_all)[:, None, :])


def segment_ids(lengths_row, seq_rows):
    doc_ends = jnp.cumsum(lengths_row)
    positions = jnp.arange(seq_rows, dtype=jnp.int32)
    return jnp.sum((positions[:, None] >= doc_ends[None, :]).astype(jnp.int32), axis=1)


def window_geometry(seq_rows):
    block_rows = min(512, seq_rows)
    key_blocks = 1 + (WINDOW - 1 + block_rows - 1) // block_rows
    return (
        block_rows,
        seq_rows // block_rows,
        key_blocks * block_rows,
        (key_blocks - 1) * block_rows,
    )


def window_allowed(segments, seg_padded, first_row, block_rows, key_rows, pad_rows):
    query_pos = first_row + jnp.arange(block_rows, dtype=jnp.int32)
    key_pos = first_row - pad_rows + jnp.arange(key_rows, dtype=jnp.int32)
    query_seg = lax.dynamic_slice_in_dim(segments, first_row, block_rows)
    key_seg = lax.dynamic_slice_in_dim(seg_padded, first_row, key_rows)
    distance = query_pos[:, None] - key_pos[None, :]
    return (query_seg[:, None] == key_seg[None, :]) & (distance >= 0) & (distance < WINDOW)


def pad_front(values, pad_rows, filler):
    return jnp.concatenate(
        [jnp.full((pad_rows,) + values.shape[1:], filler, values.dtype), values], axis=0
    )


BLOCK = 256
SLOTS = 64
STEP = 16
TILE = 256


def exclusive_sum(values):
    count = values.shape[0]
    lower = (jnp.arange(count)[:, None] > jnp.arange(count)[None, :]).astype(jnp.float32)
    total = jnp.dot(lower, values.astype(jnp.float32), precision=lax.Precision.HIGHEST)
    return total.astype(jnp.int32)


def route_plan(own_ids, sp_count, fs_count):
    local_experts = EXPERTS // sp_count
    ids = lax.all_gather(own_ids, ("fsdp", "sp"), axis=0, tiled=True)
    tokens = ids.shape[0]
    blocks = tokens // BLOCK
    capacity = 5 * tokens * TOPK // (4 * EXPERTS)
    first = lax.axis_index("sp") * local_experts
    mine = first + jnp.arange(local_experts, dtype=jnp.int32)
    named = jnp.any(ids[:, None, :] == mine[None, :, None], axis=-1)
    named = named.reshape(blocks, BLOCK, local_experts)
    upto = (jnp.arange(BLOCK)[:, None] >= jnp.arange(BLOCK)[None, :]).astype(jnp.bfloat16)
    running = jnp.einsum(
        "ts,bse->bte", upto, named.astype(jnp.bfloat16), preferred_element_type=jnp.float32
    ).astype(jnp.int32)
    earlier = exclusive_sum(running[:, -1])
    keep = named & (earlier[:, None, :] + running - 1 < capacity)
    rank = jnp.where(keep, running - 1, -1).transpose(0, 2, 1)
    steps = (jnp.sum(keep.astype(jnp.int32), axis=1) + STEP - 1) // STEP
    starts = exclusive_sum(steps)
    used = starts[-1] + steps[-1]
    slots_all = min(blocks * SLOTS, capacity + blocks * (STEP - 1))
    slots_all = (slots_all + TILE - 1) // TILE * TILE
    return rank, starts.reshape(-1), steps.reshape(-1), used, slots_all


def steps_copy(count, make, act):
    for size in range(1, SLOTS // STEP + 1):

        @pl.when(count == size)
        def _(size=size):
            act(make(size * STEP))


def start_copy(copy):
    copy.start()


def wait_copy(copy):
    copy.wait()


def pick_matrix(rank):
    experts = rank.shape[0]
    slot = lax.broadcasted_iota(jnp.int32, (SLOTS, BLOCK), 0)
    parts = [slot == rank[e : e + 1, :] for e in range(experts)]
    return parts


def dispatch_kernel(
    starts, steps, used, rank_ref, weight_ref, x_ref, out_ref, wout_ref, buf, wbuf, zeros,
    sems, wsems, zsems,
):
    experts = rank_ref.shape[1]
    width = x_ref.shape[1]
    b = pl.program_id(0)
    blocks = pl.num_programs(0)
    slot = lax.rem(b, 2)

    def make(which, e, place):
        first = starts[which * experts + e] * STEP

        def rows(size):
            return pltpu.make_async_copy(
                buf.at[place, pl.ds(e * SLOTS, size)],
                out_ref.at[e, pl.ds(pl.multiple_of(first, STEP), size)],
                sems.at[place, e],
            )

        def weights(size):
            return pltpu.make_async_copy(
                wbuf.at[place, pl.ds(e * SLOTS, size)],
                wout_ref.at[e, pl.ds(pl.multiple_of(first, STEP), size)],
                wsems.at[place, e],
            )

        return rows, weights

    def each(which, place, act):
        for e in range(experts):
            rows, weights = make(which, e, place)
            steps_copy(steps[which * experts + e], rows, act)
            if weight_ref is not None:
                steps_copy(steps[which * experts + e], weights, act)

    def fill(act):
        for e in range(experts):
            rest = lax.rem(TILE // STEP - lax.rem(used[e], TILE // STEP), TILE // STEP)
            done = used[e]
            for k, size in enumerate((8, 4, 2, 1)):
                take = lax.rem(rest // size, 2)

                @pl.when(take == 1)
                def _(e=e, k=k, size=size, done=done):
                    act(
                        pltpu.make_async_copy(
                            zeros.at[pl.ds(0, size * STEP)],
                            out_ref.at[e, pl.ds(pl.multiple_of(done * STEP, STEP), size * STEP)],
                            zsems.at[e, k],
                        )
                    )

                done = done + take * size

    @pl.when(b == 0)
    def _():
        zeros[...] = jnp.zeros_like(zeros)
        fill(start_copy)

    @pl.when(b >= 2)
    def _():
        each(b - 2, slot, wait_copy)

    parts = pick_matrix(rank_ref[0])
    if weight_ref is not None:
        for e in range(experts):
            column = jnp.sum(
                jnp.where(parts[e], weight_ref[0, e : e + 1, :], 0.0), axis=1, keepdims=True
            )
            wbuf[slot, pl.ds(e * SLOTS, SLOTS), :] = jnp.broadcast_to(column, (SLOTS, 128))
    pick = jnp.concatenate([p.astype(jnp.bfloat16) for p in parts], axis=0)
    span = 512
    for n in range(width // span):
        cols = pl.ds(n * span, span)
        buf[slot, :, cols] = jnp.dot(
            pick, x_ref[:, cols], preferred_element_type=jnp.float32
        ).astype(jnp.bfloat16)
    each(b, slot, start_copy)

    @pl.when(b == blocks - 1)
    def _():
        each(b - 1, 1 - slot, wait_copy)
        each(b, slot, wait_copy)
        fill(wait_copy)


def dispatch_rows(table, routing, weights):
    rank, starts, steps, used, slots_all = routing
    blocks, experts, _ = rank.shape
    width = table.shape[1]
    wide = pl.BlockSpec((1, experts, BLOCK), lambda b, *_: (b, 0, 0))
    anywhere = pl.BlockSpec(memory_space=pl.ANY)
    rows_shape = jax.ShapeDtypeStruct((experts, slots_all, width), jnp.bfloat16)
    scratch = [
        pltpu.VMEM((2, experts * SLOTS, width), jnp.bfloat16),
        pltpu.VMEM((2, experts * SLOTS, 128), jnp.float32),
        pltpu.VMEM((8 * STEP, width), jnp.bfloat16),
        pltpu.SemaphoreType.DMA((2, experts)),
        pltpu.SemaphoreType.DMA((2, experts)),
        pltpu.SemaphoreType.DMA((experts, 4)),
    ]
    flops = 2 * blocks * experts * SLOTS * BLOCK * width
    params = dict(
        compiler_params=pltpu.CompilerParams(
            dimension_semantics=("arbitrary",), vmem_limit_bytes=48 * 2**20
        ),
        cost_estimate=pl.CostEstimate(
            flops=flops, bytes_accessed=6 * blocks * BLOCK * width, transcendentals=0
        ),
    )
    x_spec = pl.BlockSpec((BLOCK, width), lambda b, *_: (b, 0))
    if weights is None:

        def plain(starts, steps, used, rank_ref, x_ref, out_ref, *rest):
            dispatch_kernel(
                starts, steps, used, rank_ref, None, x_ref, out_ref, None, *rest
            )

        rows = pl.pallas_call(
            plain,
            grid_spec=pltpu.PrefetchScalarGridSpec(
                num_scalar_prefetch=3,
                grid=(blocks,),
                in_specs=[wide, x_spec],
                out_specs=anywhere,
                scratch_shapes=scratch,
            ),
            out_shape=rows_shape,
            name="dispatch_cotangent",
            **params,
        )(starts, steps, used, rank, table)
        return rows, None
    return pl.pallas_call(
        dispatch_kernel,
        grid_spec=pltpu.PrefetchScalarGridSpec(
            num_scalar_prefetch=3,
            grid=(blocks,),
            in_specs=[wide, wide, x_spec],
            out_specs=[anywhere, anywhere],
            scratch_shapes=scratch,
        ),
        out_shape=[
            rows_shape,
            jax.ShapeDtypeStruct((experts, slots_all, 128), jnp.float32),
        ],
        name="dispatch_tokens",
        **params,
    )(starts, steps, used, rank, weights, table)


def contract(left, right, left_dim, right_dim):
    return lax.dot_general(
        left, right, (((left_dim,), (right_dim,)), ((), ())), preferred_element_type=jnp.float32
    )


def expert_kernel(
    used, first, x_ref, c_ref, w_ref, gate_ref, up_ref, down_ref, y_ref, dx_ref, gg_ref, gu_ref,
    gd_ref, acc_g, acc_u, acc_d,
):
    e = pl.program_id(0)
    t = pl.program_id(1)
    rows_used = used[e] * STEP
    width = x_ref.shape[2]

    @pl.when(t == 0)
    def _():
        acc_g[...] = jnp.zeros_like(acc_g)
        acc_u[...] = jnp.zeros_like(acc_u)
        acc_d[...] = jnp.zeros_like(acc_d)

    @pl.when(t * TILE < rows_used)
    def _():
        x = x_ref[0]
        c = c_ref[0]
        gate_mat = gate_ref[0]
        up_mat = up_ref[0]
        down_mat = down_ref[0]
        row = t * TILE + lax.broadcasted_iota(jnp.int32, (TILE, 1), 0)
        weight = jnp.where(row < rows_used, w_ref[0][:, 0:1], 0.0)
        gate_pre = jnp.dot(x, gate_mat, preferred_element_type=jnp.float32)
        up_pre = jnp.dot(x, up_mat, preferred_element_type=jnp.float32)
        up_act = jnp.dot(c, down_mat, preferred_element_type=jnp.float32)
        sig = 1.0 / (1.0 + jnp.exp(-gate_pre))
        silu = gate_pre * sig
        act = silu * up_pre
        gate_grad = jnp.sum(up_act * act, axis=1, keepdims=True)
        act_low = (act * weight).astype(jnp.bfloat16)
        act_grad = up_act * weight
        dgate = (act_grad * up_pre * sig * (1.0 + gate_pre * (1.0 - sig))).astype(jnp.bfloat16)
        dup = (act_grad * silu).astype(jnp.bfloat16)
        y_ref[0] = contract(act_low, down_mat, 1, 1).astype(jnp.bfloat16)
        dx_ref[0, :, 0:width] = (
            contract(dgate, gate_mat, 1, 1) + contract(dup, up_mat, 1, 1)
        ).astype(jnp.bfloat16)
        column = lax.broadcasted_iota(jnp.int32, (TILE, 128), 1)
        dx_ref[0, :, width : width + 128] = jnp.where(
            column == first[0] + e, gate_grad, 0.0
        ).astype(jnp.bfloat16)
        acc_g[...] += contract(dgate, x, 0, 0)
        acc_u[...] += contract(dup, x, 0, 0)
        acc_d[...] += contract(act_low, c, 0, 0)

    @pl.when(t == pl.num_programs(1) - 1)
    def _():
        gg_ref[0] = acc_g[...].T
        gu_ref[0] = acc_u[...].T
        gd_ref[0] = acc_d[...].T


def run_experts(x_rows, c_rows, w_rows, w_gate, w_up, w_down, used, first):
    experts, slots_all, width = x_rows.shape
    hidden = w_gate.shape[2]

    def tile_map(e, t, used, first):
        last = jnp.maximum((used[e] * STEP + TILE - 1) // TILE - 1, 0)
        return (e, jnp.minimum(t, last), 0)

    def mat_map(e, t, used, first):
        return (e, 0, 0)

    mat = pl.BlockSpec((1, width, hidden), mat_map)
    return pl.pallas_call(
        expert_kernel,
        grid_spec=pltpu.PrefetchScalarGridSpec(
            num_scalar_prefetch=2,
            grid=(experts, slots_all // TILE),
            in_specs=[
                pl.BlockSpec((1, TILE, width), tile_map),
                pl.BlockSpec((1, TILE, width), tile_map),
                pl.BlockSpec((1, TILE, 128), tile_map),
                mat,
                mat,
                mat,
            ],
            out_specs=[
                pl.BlockSpec((1, TILE, width), tile_map),
                pl.BlockSpec((1, TILE, width + 128), tile_map),
                mat,
                mat,
                mat,
            ],
            scratch_shapes=[pltpu.VMEM((hidden, width), jnp.float32)] * 3,
        ),
        out_shape=[
            jax.ShapeDtypeStruct((experts, slots_all, width), jnp.bfloat16),
            jax.ShapeDtypeStruct((experts, slots_all, width + 128), jnp.bfloat16),
        ]
        + [jax.ShapeDtypeStruct((experts, width, hidden), jnp.float32)] * 3,
        compiler_params=pltpu.CompilerParams(
            dimension_semantics=("arbitrary", "arbitrary"), vmem_limit_bytes=60 * 2**20
        ),
        cost_estimate=pl.CostEstimate(
            flops=18 * experts * slots_all * width * hidden,
            bytes_accessed=8 * experts * slots_all * width,
            transcendentals=experts * slots_all * hidden,
        ),
        name="experts",
    )(used, first, x_rows, c_rows, w_rows, w_gate, w_up, w_down)


def combine_kernel(starts, steps, rank_ref, y_ref, out_ref, buf, sems):
    experts = rank_ref.shape[1]
    width = out_ref.shape[1]
    b = pl.program_id(0)
    blocks = pl.num_programs(0)
    slot = lax.rem(b, 2)

    def each(which, place, act):
        for e in range(experts):
            first = starts[which * experts + e] * STEP

            def rows(size, e=e, first=first):
                return pltpu.make_async_copy(
                    y_ref.at[e, pl.ds(pl.multiple_of(first, STEP), size)],
                    buf.at[place, pl.ds(e * SLOTS, size)],
                    sems.at[place, e],
                )

            steps_copy(steps[which * experts + e], rows, act)

    @pl.when(b == 0)
    def _():
        buf[...] = jnp.zeros_like(buf)
        each(0, 0, start_copy)

    @pl.when(b + 1 < blocks)
    def _():
        each(b + 1, 1 - slot, start_copy)

    pick = jnp.concatenate([p.astype(jnp.bfloat16) for p in pick_matrix(rank_ref[0])], axis=0)
    each(b, slot, wait_copy)
    done = 0
    while done < width:
        span = min(512, width - done)
        cols = pl.ds(done, span)
        out_ref[:, cols] = contract(pick, buf[slot, :, cols], 0, 0).astype(jnp.bfloat16)
        done += span


def combine_rows(rows, routing, name):
    rank, starts, steps, used, slots_all = routing
    blocks, experts, _ = rank.shape
    width = rows.shape[2]
    return pl.pallas_call(
        combine_kernel,
        grid_spec=pltpu.PrefetchScalarGridSpec(
            num_scalar_prefetch=2,
            grid=(blocks,),
            in_specs=[
                pl.BlockSpec((1, experts, BLOCK), lambda b, *_: (b, 0, 0)),
                pl.BlockSpec(memory_space=pl.ANY),
            ],
            out_specs=pl.BlockSpec((BLOCK, width), lambda b, *_: (b, 0)),
            scratch_shapes=[
                pltpu.VMEM((2, experts * SLOTS, width), jnp.bfloat16),
                pltpu.SemaphoreType.DMA((2, experts)),
            ],
        ),
        out_shape=jax.ShapeDtypeStruct((blocks * BLOCK, width), jnp.bfloat16),
        compiler_params=pltpu.CompilerParams(
            dimension_semantics=("arbitrary",), vmem_limit_bytes=48 * 2**20
        ),
        cost_estimate=pl.CostEstimate(
            flops=2 * blocks * experts * SLOTS * BLOCK * width,
            bytes_accessed=6 * blocks * BLOCK * width,
            transcendentals=0,
        ),
        name=name,
    )(starts, steps, rank, rows)


def reduce_tokens(partial):
    partial = lax.psum_scatter(partial, "fsdp", scatter_dimension=0, tiled=True)
    return lax.psum_scatter(partial, "sp", scatter_dimension=0, tiled=True)


def local(
    tokens,
    doc_lengths,
    expert_ids,
    norm_attn,
    norm_query,
    norm_key,
    norm_ffn,
    w_query,
    w_key,
    w_value,
    w_out,
    w_router,
    w_gate,
    w_up,
    w_down,
    cotangent,
):
    sp_count = lax.axis_size("sp")
    fs_count = lax.axis_size("fsdp")
    hidden_in = tokens[0].astype(jnp.float32)
    tok_rows = hidden_in.shape[0]
    width = hidden_in.shape[1]
    head_local = HEADS // sp_count
    seq_rows = tok_rows * sp_count
    gathered = (
        lax.all_gather(norm_attn, "fsdp", axis=0, tiled=True),
        lax.all_gather(norm_query, "fsdp", axis=0, tiled=True),
        lax.all_gather(norm_key, "fsdp", axis=0, tiled=True),
        lax.all_gather(norm_ffn, "fsdp", axis=0, tiled=True),
        lax.all_gather(w_query, "fsdp", axis=0, tiled=True),
        lax.all_gather(w_key, "fsdp", axis=0, tiled=True),
        lax.all_gather(w_value, "fsdp", axis=0, tiled=True),
        lax.all_gather(w_out, "fsdp", axis=0, tiled=True),
        lax.all_gather(w_router, "fsdp", axis=0, tiled=True),
    )
    (
        gain_attn,
        gain_query,
        gain_key,
        gain_ffn,
        query_mat,
        key_mat,
        value_mat,
        out_mat,
        router_mat,
    ) = gathered
    cot_all = lax.all_gather(cotangent[0], ("fsdp", "sp"), axis=0, tiled=True)
    routing = route_plan(expert_ids[0], sp_count, fs_count)
    cot_rows, _ = dispatch_rows(cot_all, routing, None)
    attn_normed, attn_pull = jax.vjp(rms_scale, hidden_in, gain_attn.astype(jnp.float32))
    attn_in = attn_normed.astype(jnp.bfloat16)
    query_raw = jnp.dot(attn_in, query_mat, preferred_element_type=jnp.float32)
    key_raw = jnp.dot(attn_in, key_mat, preferred_element_type=jnp.float32)
    value_rows = jnp.dot(attn_in, value_mat, preferred_element_type=jnp.float32).astype(
        jnp.bfloat16
    )
    cosine, sine = rope_tables(
        lax.axis_index("sp") * tok_rows + jnp.arange(tok_rows, dtype=jnp.int32), HEAD_DIM
    )

    def head_path(raw_proj, gain_vec):
        return rotate_pairs(
            rms_scale(raw_proj, gain_vec).reshape(tok_rows, HEADS, HEAD_DIM), cosine, sine
        )

    query_rot, query_pull = jax.vjp(head_path, query_raw, gain_query.astype(jnp.float32))
    key_rot, key_pull = jax.vjp(head_path, key_raw, gain_key.astype(jnp.float32))
    query_heads, key_heads, value_heads = (
        lax.all_to_all(
            query_rot.astype(jnp.bfloat16), "sp", split_axis=1, concat_axis=0, tiled=True
        ),
        lax.all_to_all(key_rot.astype(jnp.bfloat16), "sp", split_axis=1, concat_axis=0, tiled=True),
        lax.all_to_all(
            value_rows.reshape(tok_rows, HEADS, HEAD_DIM),
            "sp",
            split_axis=1,
            concat_axis=0,
            tiled=True,
        ),
    )
    block_rows, block_count, key_rows, pad_rows = window_geometry(seq_rows)
    segments = segment_ids(doc_lengths[0], seq_rows)
    seg_padded = pad_front(segments, pad_rows, -1)
    key_padded = pad_front(key_heads, pad_rows, 0.0)
    value_padded = pad_front(value_heads, pad_rows, 0.0)
    score_scale = HEAD_DIM ** (-0.5)
    block_numbers = jnp.arange(block_count, dtype=jnp.int32)

    def block_scores(first_row):
        query_block = lax.dynamic_slice_in_dim(query_heads, first_row, block_rows)
        key_block = lax.dynamic_slice_in_dim(key_padded, first_row, key_rows)
        scores = (
            jnp.einsum("qhd,khd->hqk", query_block, key_block, preferred_element_type=jnp.float32)
            * score_scale
        )
        allowed = window_allowed(segments, seg_padded, first_row, block_rows, key_rows, pad_rows)
        return (jnp.where(allowed[None], scores, masked_score), query_block, key_block)

    def forward_block(carry_in, block_index):
        first_row = block_index * block_rows
        scores, query_block, key_block = block_scores(first_row)
        value_block = lax.dynamic_slice_in_dim(value_padded, first_row, key_rows)
        row_max = jnp.max(scores, axis=-1, keepdims=True)
        weights = jnp.exp(scores - row_max)
        row_total = jnp.sum(weights, axis=-1, keepdims=True)
        probs = (weights / row_total).astype(jnp.bfloat16)
        attended = jnp.einsum(
            "hqk,khd->qhd", probs, value_block, preferred_element_type=jnp.float32
        )
        return (carry_in, (attended.astype(jnp.bfloat16), (row_max + jnp.log(row_total))[..., 0]))

    _, (attended_blocks, lse_blocks) = lax.scan(forward_block, 0, block_numbers)
    attended_heads = attended_blocks.reshape(seq_rows, head_local, HEAD_DIM)
    attended_tok = lax.all_to_all(
        attended_heads, "sp", split_axis=0, concat_axis=1, tiled=True
    ).reshape(tok_rows, width)
    after_attn = hidden_in + jnp.dot(attended_tok, out_mat, preferred_element_type=jnp.float32)
    ffn_normed, ffn_pull = jax.vjp(rms_scale, after_attn, gain_ffn.astype(jnp.float32))
    ffn_in = ffn_normed.astype(jnp.bfloat16)
    logits = jnp.dot(ffn_in, router_mat, preferred_element_type=jnp.float32)
    router = jax.nn.softmax(logits, axis=-1)
    rank = routing[0]
    ffn_all = lax.all_gather(ffn_in, ("fsdp", "sp"), axis=0, tiled=True)
    router_all = jax.nn.softmax(
        jnp.dot(ffn_all, router_mat, preferred_element_type=jnp.float32), axis=-1
    )
    expert_local = EXPERTS // sp_count
    first_expert = lax.axis_index("sp") * expert_local
    gate_rows = (
        lax.dynamic_slice_in_dim(router_all, first_expert, expert_local, axis=1)
        .reshape(-1, BLOCK, expert_local)
        .transpose(0, 2, 1)
    )
    ffn_rows, gate_slots = dispatch_rows(ffn_all, routing, gate_rows)
    out_rows, in_grad_rows, grad_gate, grad_up, grad_down = run_experts(
        ffn_rows, cot_rows, gate_slots, w_gate, w_up, w_down, routing[3], first_expert[None]
    )
    in_grad_sum = reduce_tokens(combine_rows(in_grad_rows, routing, "combine_grads"))
    moe_sum = reduce_tokens(combine_rows(out_rows, routing, "combine_outputs"))
    mixed = (after_attn + moe_sum.astype(jnp.float32)).astype(jnp.bfloat16)
    upstream = cotangent[0].astype(jnp.float32)
    ffn_in_grad = in_grad_sum[:, :width].astype(jnp.float32)
    router_grad = in_grad_sum[:, width : width + EXPERTS].astype(jnp.float32)
    logit_grad = (
        router * (router_grad - jnp.sum(router * router_grad, axis=-1, keepdims=True))
    ).astype(jnp.bfloat16)
    ffn_in_grad = ffn_in_grad + jnp.dot(
        logit_grad, router_mat.T, preferred_element_type=jnp.float32
    )
    router_term = jnp.dot(ffn_in.T, logit_grad, preferred_element_type=jnp.float32)
    ffn_hidden_grad, ffn_gain_term = ffn_pull(ffn_in_grad)
    after_grad = upstream + ffn_hidden_grad
    attn_out_grad = after_grad.astype(jnp.bfloat16)
    out_term = jnp.dot(attended_tok.T, attn_out_grad, preferred_element_type=jnp.float32)
    attended_grad = jnp.dot(attn_out_grad, out_mat.T, preferred_element_type=jnp.float32).astype(
        jnp.bfloat16
    )
    attended_grad_heads = lax.all_to_all(
        attended_grad.reshape(tok_rows, HEADS, HEAD_DIM),
        "sp",
        split_axis=1,
        concat_axis=0,
        tiled=True,
    )

    def backward_block(carry_in, block_index):
        key_total, value_total = carry_in
        first_row = block_index * block_rows
        scores, query_block, key_block = block_scores(first_row)
        value_block = lax.dynamic_slice_in_dim(value_padded, first_row, key_rows)
        grad_block = lax.dynamic_slice_in_dim(attended_grad_heads, first_row, block_rows)
        probs = jnp.exp(scores - lse_blocks[block_index][..., None])
        prob_grad = jnp.einsum(
            "qhd,khd->hqk", grad_block, value_block, preferred_element_type=jnp.float32
        )
        row_delta = jnp.sum(probs * prob_grad, axis=-1, keepdims=True)
        score_grad = (probs * (prob_grad - row_delta)).astype(jnp.bfloat16)
        query_part = (
            jnp.einsum("hqk,khd->qhd", score_grad, key_block, preferred_element_type=jnp.float32)
            * score_scale
        )
        key_part = (
            jnp.einsum("hqk,qhd->khd", score_grad, query_block, preferred_element_type=jnp.float32)
            * score_scale
        )
        value_part = jnp.einsum(
            "hqk,qhd->khd",
            probs.astype(jnp.bfloat16),
            grad_block,
            preferred_element_type=jnp.float32,
        )
        key_total = lax.dynamic_update_slice_in_dim(
            key_total,
            lax.dynamic_slice_in_dim(key_total, first_row, key_rows) + key_part,
            first_row,
            0,
        )
        value_total = lax.dynamic_update_slice_in_dim(
            value_total,
            lax.dynamic_slice_in_dim(value_total, first_row, key_rows) + value_part,
            first_row,
            0,
        )
        return ((key_total, value_total), query_part.astype(jnp.bfloat16))

    zero_keys = jnp.zeros((pad_rows + seq_rows, head_local, HEAD_DIM), jnp.float32)
    (key_total, value_total), query_blocks = lax.scan(
        backward_block, (zero_keys, zero_keys), block_numbers
    )
    query_grad_heads = query_blocks.reshape(seq_rows, head_local, HEAD_DIM)
    key_grad_heads = key_total[pad_rows:].astype(jnp.bfloat16)
    value_grad_heads = value_total[pad_rows:].astype(jnp.bfloat16)
    query_back, key_back, value_back = (
        lax.all_to_all(query_grad_heads, "sp", split_axis=0, concat_axis=1, tiled=True),
        lax.all_to_all(key_grad_heads, "sp", split_axis=0, concat_axis=1, tiled=True),
        lax.all_to_all(value_grad_heads, "sp", split_axis=0, concat_axis=1, tiled=True),
    )
    query_raw_grad, query_gain_term = query_pull(query_back.astype(jnp.float32))
    key_raw_grad, key_gain_term = key_pull(key_back.astype(jnp.float32))
    query_low = query_raw_grad.astype(jnp.bfloat16)
    key_low = key_raw_grad.astype(jnp.bfloat16)
    value_low = value_back.reshape(tok_rows, width)
    attn_in_grad = jnp.dot(query_low, query_mat.T, preferred_element_type=jnp.float32)
    attn_in_grad = attn_in_grad + jnp.dot(key_low, key_mat.T, preferred_element_type=jnp.float32)
    attn_in_grad = attn_in_grad + jnp.dot(
        value_low, value_mat.T, preferred_element_type=jnp.float32
    )
    query_term = jnp.dot(attn_in.T, query_low, preferred_element_type=jnp.float32)
    key_term = jnp.dot(attn_in.T, key_low, preferred_element_type=jnp.float32)
    value_term = jnp.dot(attn_in.T, value_low, preferred_element_type=jnp.float32)
    attn_hidden_grad, attn_gain_term = attn_pull(attn_in_grad)
    grad_tokens = after_grad + attn_hidden_grad
    scattered = (
        lax.psum_scatter(
            attn_gain_term.astype(jnp.bfloat16), "fsdp", scatter_dimension=0, tiled=True
        ).astype(jnp.float32),
        lax.psum_scatter(
            query_gain_term.astype(jnp.bfloat16), "fsdp", scatter_dimension=0, tiled=True
        ).astype(jnp.float32),
        lax.psum_scatter(
            key_gain_term.astype(jnp.bfloat16), "fsdp", scatter_dimension=0, tiled=True
        ).astype(jnp.float32),
        lax.psum_scatter(
            ffn_gain_term.astype(jnp.bfloat16), "fsdp", scatter_dimension=0, tiled=True
        ).astype(jnp.float32),
        lax.psum_scatter(
            query_term.astype(jnp.bfloat16), "fsdp", scatter_dimension=0, tiled=True
        ).astype(jnp.float32),
        lax.psum_scatter(
            key_term.astype(jnp.bfloat16), "fsdp", scatter_dimension=0, tiled=True
        ).astype(jnp.float32),
        lax.psum_scatter(
            value_term.astype(jnp.bfloat16), "fsdp", scatter_dimension=0, tiled=True
        ).astype(jnp.float32),
        lax.psum_scatter(
            out_term.astype(jnp.bfloat16), "fsdp", scatter_dimension=0, tiled=True
        ).astype(jnp.float32),
        lax.psum_scatter(
            router_term.astype(jnp.bfloat16), "fsdp", scatter_dimension=0, tiled=True
        ).astype(jnp.float32),
    )
    summed = (
        lax.psum(scattered[0].astype(jnp.bfloat16), "sp").astype(jnp.float32),
        lax.psum(scattered[1].astype(jnp.bfloat16), "sp").astype(jnp.float32),
        lax.psum(scattered[2].astype(jnp.bfloat16), "sp").astype(jnp.float32),
        lax.psum(scattered[3].astype(jnp.bfloat16), "sp").astype(jnp.float32),
        lax.psum(scattered[4].astype(jnp.bfloat16), "sp").astype(jnp.float32),
        lax.psum(scattered[5].astype(jnp.bfloat16), "sp").astype(jnp.float32),
        lax.psum(scattered[6].astype(jnp.bfloat16), "sp").astype(jnp.float32),
        lax.psum(scattered[7].astype(jnp.bfloat16), "sp").astype(jnp.float32),
        lax.psum(scattered[8].astype(jnp.bfloat16), "sp").astype(jnp.float32),
    )
    return (
        mixed[None],
        grad_tokens[None],
        summed[0],
        summed[1],
        summed[2],
        summed[3],
        summed[4],
        summed[5],
        summed[6],
        summed[7],
        summed[8],
        grad_gate,
        grad_up,
        grad_down,
    )


def solution(mesh):
    in_specs = (
        P("fsdp", "sp", None),
        P("fsdp", None),
        P("fsdp", "sp", None),
        P("fsdp"),
        P("fsdp"),
        P("fsdp"),
        P("fsdp"),
        P("fsdp", None),
        P("fsdp", None),
        P("fsdp", None),
        P("fsdp", None),
        P("fsdp", None),
        P("sp", None, "fsdp"),
        P("sp", None, "fsdp"),
        P("sp", None, "fsdp"),
        P("fsdp", "sp", None),
    )
    out_specs = (
        P("fsdp", "sp", None),
        P("fsdp", "sp", None),
        P("fsdp"),
        P("fsdp"),
        P("fsdp"),
        P("fsdp"),
        P("fsdp", None),
        P("fsdp", None),
        P("fsdp", None),
        P("fsdp", None),
        P("fsdp", None),
        P("sp", None, "fsdp"),
        P("sp", None, "fsdp"),
        P("sp", None, "fsdp"),
    )
    return jax.shard_map(local, mesh=mesh, in_specs=in_specs, out_specs=out_specs, check_vma=False)
```

```python
import functools

import jax
import jax.numpy as jnp
from jax import lax
from jax.experimental import pallas as pl
from jax.experimental.pallas import tpu as pltpu
from jax.sharding import PartitionSpec as P

HEADS = 16
HEAD_DIM = 128
EXPERTS = 64
TOPK = 8
WINDOW = 1024


eps = 1e-05
rope_base = 10000.0
masked_score = -1e30


def rms_scale(values, gain_vec):
    return values * lax.rsqrt(jnp.mean(values * values, axis=-1, keepdims=True) + eps) * gain_vec


def rotate_pairs(values, cosine, sine):
    half_dim = values.shape[-1] // 2
    turned = jnp.concatenate([-values[..., half_dim:], values[..., :half_dim]], axis=-1)
    return values * cosine + turned * sine


def rope_tables(positions, head_size):
    inv_freq = rope_base ** (-jnp.arange(0, head_size, 2, dtype=jnp.float32) / head_size)
    phase_half = positions.astype(jnp.float32)[:, None] * inv_freq[None, :]
    phase_all = jnp.concatenate([phase_half, phase_half], axis=-1)
    return (jnp.cos(phase_all)[:, None, :], jnp.sin(phase_all)[:, None, :])


def segment_ids(lengths_row, seq_rows):
    doc_ends = jnp.cumsum(lengths_row)
    positions = jnp.arange(seq_rows, dtype=jnp.int32)
    return jnp.sum((positions[:, None] >= doc_ends[None, :]).astype(jnp.int32), axis=1)


def window_geometry(seq_rows):
    block_rows = min(512, seq_rows)
    key_blocks = 1 + (WINDOW - 1 + block_rows - 1) // block_rows
    return (
        block_rows,
        seq_rows // block_rows,
        key_blocks * block_rows,
        (key_blocks - 1) * block_rows,
    )


def window_allowed(segments, seg_padded, first_row, block_rows, key_rows, pad_rows):
    query_pos = first_row + jnp.arange(block_rows, dtype=jnp.int32)
    key_pos = first_row - pad_rows + jnp.arange(key_rows, dtype=jnp.int32)
    query_seg = lax.dynamic_slice_in_dim(segments, first_row, block_rows)
    key_seg = lax.dynamic_slice_in_dim(seg_padded, first_row, key_rows)
    distance = query_pos[:, None] - key_pos[None, :]
    return (query_seg[:, None] == key_seg[None, :]) & (distance >= 0) & (distance < WINDOW)


def pad_front(values, pad_rows, filler):
    return jnp.concatenate(
        [jnp.full((pad_rows,) + values.shape[1:], filler, values.dtype), values], axis=0
    )


BLOCK = 256
SLOTS = 64
STEP = 16
TILE = 256


def exclusive_sum(values):
    count = values.shape[0]
    lower = (jnp.arange(count)[:, None] > jnp.arange(count)[None, :]).astype(jnp.float32)
    total = jnp.dot(lower, values.astype(jnp.float32), precision=lax.Precision.HIGHEST)
    return total.astype(jnp.int32)


def route_plan(own_ids, sp_count, fs_count):
    local_experts = EXPERTS // sp_count
    ids = lax.all_gather(own_ids, ("fsdp", "sp"), axis=0, tiled=True)
    tokens = ids.shape[0]
    blocks = tokens // BLOCK
    capacity = 5 * tokens * TOPK // (4 * EXPERTS)
    first = lax.axis_index("sp") * local_experts
    mine = first + jnp.arange(local_experts, dtype=jnp.int32)
    named = jnp.any(ids[:, None, :] == mine[None, :, None], axis=-1)
    named = named.reshape(blocks, BLOCK, local_experts)
    upto = (jnp.arange(BLOCK)[:, None] >= jnp.arange(BLOCK)[None, :]).astype(jnp.bfloat16)
    running = jnp.einsum(
        "ts,bse->bte", upto, named.astype(jnp.bfloat16), preferred_element_type=jnp.float32
    ).astype(jnp.int32)
    earlier = exclusive_sum(running[:, -1])
    keep = named & (earlier[:, None, :] + running - 1 < capacity)
    rank = jnp.where(keep, running - 1, -1).transpose(0, 2, 1)
    steps = (jnp.sum(keep.astype(jnp.int32), axis=1) + STEP - 1) // STEP
    starts = exclusive_sum(steps)
    used = starts[-1] + steps[-1]
    slots_all = min(blocks * SLOTS, capacity + blocks * (STEP - 1))
    slots_all = (slots_all + TILE - 1) // TILE * TILE
    return rank, starts.reshape(-1), steps.reshape(-1), used, slots_all


def steps_copy(count, make, act):
    for size in range(1, SLOTS // STEP + 1):

        @pl.when(count == size)
        def _(size=size):
            act(make(size * STEP))


def start_copy(copy):
    copy.start()


def wait_copy(copy):
    copy.wait()


def pick_matrix(rank):
    experts = rank.shape[0]
    slot = lax.broadcasted_iota(jnp.int32, (SLOTS, BLOCK), 0)
    parts = [slot == rank[e : e + 1, :] for e in range(experts)]
    return parts


def dispatch_kernel(
    starts, steps, used, rank_ref, weight_ref, x_ref, out_ref, wout_ref, buf, wbuf, zeros,
    sems, wsems, zsems,
):
    experts = rank_ref.shape[1]
    width = x_ref.shape[1]
    b = pl.program_id(0)
    blocks = pl.num_programs(0)
    slot = lax.rem(b, 2)

    def make(which, e, place):
        first = starts[which * experts + e] * STEP

        def rows(size):
            return pltpu.make_async_copy(
                buf.at[place, pl.ds(e * SLOTS, size)],
                out_ref.at[e, pl.ds(pl.multiple_of(first, STEP), size)],
                sems.at[place, e],
            )

        def weights(size):
            return pltpu.make_async_copy(
                wbuf.at[place, pl.ds(e * SLOTS, size)],
                wout_ref.at[e, pl.ds(pl.multiple_of(first, STEP), size)],
                wsems.at[place, e],
            )

        return rows, weights

    def each(which, place, act):
        for e in range(experts):
            rows, weights = make(which, e, place)
            steps_copy(steps[which * experts + e], rows, act)
            if weight_ref is not None:
                steps_copy(steps[which * experts + e], weights, act)

    def fill(act):
        for e in range(experts):
            rest = lax.rem(TILE // STEP - lax.rem(used[e], TILE // STEP), TILE // STEP)
            done = used[e]
            for k, size in enumerate((8, 4, 2, 1)):
                take = lax.rem(rest // size, 2)

                @pl.when(take == 1)
                def _(e=e, k=k, size=size, done=done):
                    act(
                        pltpu.make_async_copy(
                            zeros.at[pl.ds(0, size * STEP)],
                            out_ref.at[e, pl.ds(pl.multiple_of(done * STEP, STEP), size * STEP)],
                            zsems.at[e, k],
                        )
                    )

                done = done + take * size

    @pl.when(b == 0)
    def _():
        zeros[...] = jnp.zeros_like(zeros)
        fill(start_copy)

    @pl.when(b >= 2)
    def _():
        each(b - 2, slot, wait_copy)

    parts = pick_matrix(rank_ref[0])
    if weight_ref is not None:
        for e in range(experts):
            column = jnp.sum(
                jnp.where(parts[e], weight_ref[0, e : e + 1, :], 0.0), axis=1, keepdims=True
            )
            wbuf[slot, pl.ds(e * SLOTS, SLOTS), :] = jnp.broadcast_to(column, (SLOTS, 128))
    pick = jnp.concatenate([p.astype(jnp.bfloat16) for p in parts], axis=0)
    span = 512
    for n in range(width // span):
        cols = pl.ds(n * span, span)
        buf[slot, :, cols] = jnp.dot(
            pick, x_ref[:, cols], preferred_element_type=jnp.float32
        ).astype(jnp.bfloat16)
    each(b, slot, start_copy)

    @pl.when(b == blocks - 1)
    def _():
        each(b - 1, 1 - slot, wait_copy)
        each(b, slot, wait_copy)
        fill(wait_copy)


def dispatch_rows(table, routing, weights):
    rank, starts, steps, used, slots_all = routing
    blocks, experts, _ = rank.shape
    width = table.shape[1]
    wide = pl.BlockSpec((1, experts, BLOCK), lambda b, *_: (b, 0, 0))
    anywhere = pl.BlockSpec(memory_space=pl.ANY)
    rows_shape = jax.ShapeDtypeStruct((experts, slots_all, width), jnp.bfloat16)
    scratch = [
        pltpu.VMEM((2, experts * SLOTS, width), jnp.bfloat16),
        pltpu.VMEM((2, experts * SLOTS, 128), jnp.float32),
        pltpu.VMEM((8 * STEP, width), jnp.bfloat16),
        pltpu.SemaphoreType.DMA((2, experts)),
        pltpu.SemaphoreType.DMA((2, experts)),
        pltpu.SemaphoreType.DMA((experts, 4)),
    ]
    flops = 2 * blocks * experts * SLOTS * BLOCK * width
    params = dict(
        compiler_params=pltpu.CompilerParams(
            dimension_semantics=("arbitrary",), vmem_limit_bytes=48 * 2**20
        ),
        cost_estimate=pl.CostEstimate(
            flops=flops, bytes_accessed=6 * blocks * BLOCK * width, transcendentals=0
        ),
    )
    x_spec = pl.BlockSpec((BLOCK, width), lambda b, *_: (b, 0))
    if weights is None:

        def plain(starts, steps, used, rank_ref, x_ref, out_ref, *rest):
            dispatch_kernel(
                starts, steps, used, rank_ref, None, x_ref, out_ref, None, *rest
            )

        rows = pl.pallas_call(
            plain,
            grid_spec=pltpu.PrefetchScalarGridSpec(
                num_scalar_prefetch=3,
                grid=(blocks,),
                in_specs=[wide, x_spec],
                out_specs=anywhere,
                scratch_shapes=scratch,
            ),
            out_shape=rows_shape,
            name="dispatch_cotangent",
            **params,
        )(starts, steps, used, rank, table)
        return rows, None
    return pl.pallas_call(
        dispatch_kernel,
        grid_spec=pltpu.PrefetchScalarGridSpec(
            num_scalar_prefetch=3,
            grid=(blocks,),
            in_specs=[wide, wide, x_spec],
            out_specs=[anywhere, anywhere],
            scratch_shapes=scratch,
        ),
        out_shape=[
            rows_shape,
            jax.ShapeDtypeStruct((experts, slots_all, 128), jnp.float32),
        ],
        name="dispatch_tokens",
        **params,
    )(starts, steps, used, rank, weights, table)


def contract(left, right, left_dim, right_dim):
    return lax.dot_general(
        left, right, (((left_dim,), (right_dim,)), ((), ())), preferred_element_type=jnp.float32
    )


def expert_kernel(
    used, first, x_ref, c_ref, w_ref, gate_ref, up_ref, down_ref, y_ref, dx_ref, gg_ref, gu_ref,
    gd_ref, acc_g, acc_u, acc_d,
):
    e = pl.program_id(0)
    t = pl.program_id(1)
    rows_used = used[e] * STEP
    width = x_ref.shape[2]

    @pl.when(t == 0)
    def _():
        acc_g[...] = jnp.zeros_like(acc_g)
        acc_u[...] = jnp.zeros_like(acc_u)
        acc_d[...] = jnp.zeros_like(acc_d)

    @pl.when(t * TILE < rows_used)
    def _():
        x = x_ref[0]
        c = c_ref[0]
        gate_mat = gate_ref[0]
        up_mat = up_ref[0]
        down_mat = down_ref[0]
        row = t * TILE + lax.broadcasted_iota(jnp.int32, (TILE, 1), 0)
        weight = jnp.where(row < rows_used, w_ref[0][:, 0:1], 0.0)
        gate_pre = jnp.dot(x, gate_mat, preferred_element_type=jnp.float32)
        up_pre = jnp.dot(x, up_mat, preferred_element_type=jnp.float32)
        up_act = jnp.dot(c, down_mat, preferred_element_type=jnp.float32)
        sig = 1.0 / (1.0 + jnp.exp(-gate_pre))
        silu = gate_pre * sig
        act = silu * up_pre
        gate_grad = jnp.sum(up_act * act, axis=1, keepdims=True)
        act_low = (act * weight).astype(jnp.bfloat16)
        act_grad = up_act * weight
        dgate = (act_grad * up_pre * sig * (1.0 + gate_pre * (1.0 - sig))).astype(jnp.bfloat16)
        dup = (act_grad * silu).astype(jnp.bfloat16)
        y_ref[0] = contract(act_low, down_mat, 1, 1).astype(jnp.bfloat16)
        dx_ref[0, :, 0:width] = (
            contract(dgate, gate_mat, 1, 1) + contract(dup, up_mat, 1, 1)
        ).astype(jnp.bfloat16)
        column = lax.broadcasted_iota(jnp.int32, (TILE, 128), 1)
        dx_ref[0, :, width : width + 128] = jnp.where(
            column == first[0] + e, gate_grad, 0.0
        ).astype(jnp.bfloat16)
        acc_g[...] += contract(dgate, x, 0, 0)
        acc_u[...] += contract(dup, x, 0, 0)
        acc_d[...] += contract(act_low, c, 0, 0)

    @pl.when(t == pl.num_programs(1) - 1)
    def _():
        gg_ref[0] = acc_g[...].T
        gu_ref[0] = acc_u[...].T
        gd_ref[0] = acc_d[...].T


def run_experts(x_rows, c_rows, w_rows, w_gate, w_up, w_down, used, first):
    experts, slots_all, width = x_rows.shape
    hidden = w_gate.shape[2]

    def tile_map(e, t, used, first):
        last = jnp.maximum((used[e] * STEP + TILE - 1) // TILE - 1, 0)
        return (e, jnp.minimum(t, last), 0)

    def mat_map(e, t, used, first):
        return (e, 0, 0)

    mat = pl.BlockSpec((1, width, hidden), mat_map)
    return pl.pallas_call(
        expert_kernel,
        grid_spec=pltpu.PrefetchScalarGridSpec(
            num_scalar_prefetch=2,
            grid=(experts, slots_all // TILE),
            in_specs=[
                pl.BlockSpec((1, TILE, width), tile_map),
                pl.BlockSpec((1, TILE, width), tile_map),
                pl.BlockSpec((1, TILE, 128), tile_map),
                mat,
                mat,
                mat,
            ],
            out_specs=[
                pl.BlockSpec((1, TILE, width), tile_map),
                pl.BlockSpec((1, TILE, width + 128), tile_map),
                mat,
                mat,
                mat,
            ],
            scratch_shapes=[pltpu.VMEM((hidden, width), jnp.float32)] * 3,
        ),
        out_shape=[
            jax.ShapeDtypeStruct((experts, slots_all, width), jnp.bfloat16),
            jax.ShapeDtypeStruct((experts, slots_all, width + 128), jnp.bfloat16),
        ]
        + [jax.ShapeDtypeStruct((experts, width, hidden), jnp.float32)] * 3,
        input_output_aliases={2: 0},
        compiler_params=pltpu.CompilerParams(
            dimension_semantics=("arbitrary", "arbitrary"), vmem_limit_bytes=60 * 2**20
        ),
        cost_estimate=pl.CostEstimate(
            flops=18 * experts * slots_all * width * hidden,
            bytes_accessed=8 * experts * slots_all * width,
            transcendentals=experts * slots_all * hidden,
        ),
        name="experts",
    )(used, first, x_rows, c_rows, w_rows, w_gate, w_up, w_down)


def combine_kernel(starts, steps, rank_ref, y_ref, out_ref, buf, sems):
    experts = rank_ref.shape[1]
    width = out_ref.shape[1]
    b = pl.program_id(0)
    blocks = pl.num_programs(0)
    slot = lax.rem(b, 2)

    def each(which, place, act):
        for e in range(experts):
            first = starts[which * experts + e] * STEP

            def rows(size, e=e, first=first):
                return pltpu.make_async_copy(
                    y_ref.at[e, pl.ds(pl.multiple_of(first, STEP), size)],
                    buf.at[place, pl.ds(e * SLOTS, size)],
                    sems.at[place, e],
                )

            steps_copy(steps[which * experts + e], rows, act)

    @pl.when(b == 0)
    def _():
        buf[...] = jnp.zeros_like(buf)
        each(0, 0, start_copy)

    @pl.when(b + 1 < blocks)
    def _():
        each(b + 1, 1 - slot, start_copy)

    pick = jnp.concatenate([p.astype(jnp.bfloat16) for p in pick_matrix(rank_ref[0])], axis=0)
    each(b, slot, wait_copy)
    done = 0
    while done < width:
        span = min(512, width - done)
        cols = pl.ds(done, span)
        out_ref[:, cols] = contract(pick, buf[slot, :, cols], 0, 0).astype(jnp.bfloat16)
        done += span


def combine_rows(rows, routing, name):
    rank, starts, steps, used, slots_all = routing
    blocks, experts, _ = rank.shape
    width = rows.shape[2]
    return pl.pallas_call(
        combine_kernel,
        grid_spec=pltpu.PrefetchScalarGridSpec(
            num_scalar_prefetch=2,
            grid=(blocks,),
            in_specs=[
                pl.BlockSpec((1, experts, BLOCK), lambda b, *_: (b, 0, 0)),
                pl.BlockSpec(memory_space=pl.ANY),
            ],
            out_specs=pl.BlockSpec((BLOCK, width), lambda b, *_: (b, 0)),
            scratch_shapes=[
                pltpu.VMEM((2, experts * SLOTS, width), jnp.bfloat16),
                pltpu.SemaphoreType.DMA((2, experts)),
            ],
        ),
        out_shape=jax.ShapeDtypeStruct((blocks * BLOCK, width), jnp.bfloat16),
        compiler_params=pltpu.CompilerParams(
            dimension_semantics=("arbitrary",), vmem_limit_bytes=48 * 2**20
        ),
        cost_estimate=pl.CostEstimate(
            flops=2 * blocks * experts * SLOTS * BLOCK * width,
            bytes_accessed=6 * blocks * BLOCK * width,
            transcendentals=0,
        ),
        name=name,
    )(starts, steps, rank, rows)


MESH = pl.DeviceIdType.MESH


class Place:
    def __init__(self, counts, fsdp_too):
        self.n_hi, self.n_lo, self.n_x, self.n_core = counts
        sp = lax.axis_index("sp")
        self.hi, self.lo = sp // self.n_lo, sp % self.n_lo
        if fsdp_too:
            fs = lax.axis_index("fsdp")
            self.x, self.core = fs // self.n_core, fs % self.n_core
        else:
            self.x, self.core = 0, 0

    def peer(self, dim, ahead):
        if dim == "core":
            return {"fsdp": self.x * self.n_core + (self.core + ahead) % self.n_core}
        if dim == "x":
            return {"fsdp": (self.x + ahead) % self.n_x * self.n_core + self.core}
        if dim == "lo":
            return {"sp": self.hi * self.n_lo + (self.lo + ahead) % self.n_lo}
        return {"sp": (self.hi + ahead) % self.n_hi * self.n_lo + self.lo}

    def sizes(self):
        return {"core": self.n_core, "x": self.n_x, "lo": self.n_lo, "hi": self.n_hi}

    def meet(self):
        barrier = pltpu.get_barrier_semaphore()
        met = 0
        for dim, size in self.sizes().items():
            for ahead in range(1, size):
                pl.semaphore_signal(
                    barrier, inc=1, device_id=self.peer(dim, ahead), device_id_type=MESH
                )
                met += 1
        pl.semaphore_wait(barrier, met)


def mesh_counts(sp_count, fs_count):
    low = 2
    while low * low < sp_count // 2:
        low *= 2
    low = min(low, sp_count)
    core = 2 if fs_count % 2 == 0 else 1
    return sp_count // low, low, fs_count // core, core


def scatter_kernel(
    counts, parts, fsdp_too, part_ref, out_ref, own, buf, first, second, third, own_sem, s0, r0,
    s1, r1, s2, r2, s3, r3,
):
    at = Place(counts, fsdp_too)
    n_hi, n_lo, n_x, n_core = counts
    rows = out_ref.shape[0] // parts
    pairs = parts // 2
    steps = n_hi * pairs
    lag = 1
    orders = [[d for d in o if at.sizes()[d] > 1] for o in (("x", "lo"), ("lo", "x"))]

    def remote(src, dst, send, recv, dim, ahead):
        return pltpu.make_async_remote_copy(
            src_ref=src, dst_ref=dst, send_sem=send, recv_sem=recv,
            device_id=at.peer(dim, ahead), device_id_type=MESH,
        )

    def where(t, v):
        return (at.hi + 1 + t // pairs) % n_hi, t % pairs * 2 + v

    def mine(t, v, core):
        hi, q = where(t, v)
        return part_ref.at[:, core, hi, :, pl.ds(pl.multiple_of(q * rows, 16), rows), :]

    def load_own(t, v):
        place = own.at[t % 2, v] if n_core > 1 else buf.at[2 * t + v]
        return pltpu.make_async_copy(mine(t, v, at.core), place, own_sem.at[t % 2, v])

    def core_copy(t, v):
        return remote(
            mine(t, v, (at.core + 1) % 2), buf.at[2 * t + v], s0.at[2 * t + v], r0.at[2 * t + v],
            "core", 1,
        )

    def mid_copy(t, v, stage, ahead):
        u = 2 * t + v
        dim = orders[v][stage]
        size = at.sizes()[dim]
        to = ((at.x if dim == "x" else at.lo) + ahead) % size
        if stage == 0:
            src = buf.at[u, to] if dim == "x" else buf.at[u, :, to]
            dst = first.at[u, size - ahead - 1, pl.ds(0, n_lo if dim == "x" else n_x)]
            return remote(
                src, dst, s1.at[u, ahead - 1], r1.at[u, size - ahead - 1], dim, ahead
            )
        return remote(
            first.at[u, 0, to], second.at[u, size - ahead - 1],
            s2.at[u, ahead - 1], r2.at[u, size - ahead - 1], dim, ahead,
        )

    def wait_in(t, v, stage):
        size = at.sizes()[orders[v][stage]]
        for ahead in range(1, size):
            mid_copy(t, v, stage, ahead).wait_recv()

    def start_out(t, v, stage):
        size = at.sizes()[orders[v][stage]]
        for ahead in range(1, size):
            mid_copy(t, v, stage, ahead).start()

    def wide(ref):
        return ref[...].astype(jnp.float32)

    def result(t, v):
        u = 2 * t + v
        if len(orders[v]) == 2:
            return second.at[u, 0]
        if len(orders[v]) == 1:
            return first.at[u, 0, 0]
        return buf.at[u, 0, 0]

    def last_copy(t, v, ahead):
        _, q = where(t, v)
        return remote(
            result(t, v), third.at[n_hi - ahead - 1, q],
            s3.at[2 * t + v], r3.at[n_hi - ahead - 1, q], "hi", ahead,
        )

    def send_last(t, v):
        for k in range(n_hi - 1):

            @pl.when(t // pairs == k)
            def _(k=k):
                last_copy(t, v, k + 1).start()

    def stage_core(t, v):
        u = 2 * t + v
        load_own(t, v).wait()
        if n_core > 1:
            core_copy(t, v).wait_recv()

            @pl.loop(0, n_x * n_lo)
            def _(j):
                x, lo = j // n_lo, j % n_lo
                place = buf.at[u, x, lo]
                place[...] = (wide(place) + wide(own.at[t % 2, v, x, lo])).astype(jnp.bfloat16)

        if orders[v]:
            start_out(t, v, 0)
        else:
            send_last(t, v)

    def stage_mid(t, v, stage):
        u = 2 * t + v
        wait_in(t, v, stage)
        dim = orders[v][stage]
        size = at.sizes()[dim]
        if stage == 0:
            keep = n_lo if dim == "x" else n_x

            @pl.loop(0, keep)
            def _(j):
                base = buf.at[u, at.x, j] if dim == "x" else buf.at[u, j, at.lo]
                total = wide(base)
                for s in range(size - 1):
                    total = total + wide(first.at[u, s, j])
                first.at[u, 0, j][...] = total.astype(jnp.bfloat16)

        else:
            base = first.at[u, 0, at.x if dim == "x" else at.lo]
            total = wide(base)
            for s in range(size - 1):
                total = total + wide(second.at[u, s])
            second.at[u, 0][...] = total.astype(jnp.bfloat16)
        if stage + 1 < len(orders[v]):
            start_out(t, v, stage + 1)
        else:
            send_last(t, v)

    at.meet()
    if n_core > 1:

        @pl.loop(0, steps)
        def _(t):
            for v in range(2):
                core_copy(t, v).start()

    for v in range(2):
        load_own(0, v).start()

    depth = len(orders[0])

    @pl.loop(0, steps + depth * lag)
    def _(t):
        @pl.when(t + 1 < steps)
        def _():
            for v in range(2):
                load_own(t + 1, v).start()

        @pl.when(t < steps)
        def _():
            for v in range(2):
                stage_core(t, v)

        for stage in range(depth):
            back = (stage + 1) * lag

            @pl.when((t >= back) & (t < steps + back))
            def _(stage=stage, back=back):
                for v in range(2):
                    stage_mid(t - back, v, stage)

    for g in range(pairs):
        t = (n_hi - 1) * pairs + g
        for v in range(2):
            q = g * 2 + v
            total = wide(result(t, v))
            for s in range(n_hi - 1):
                last_copy(g, v, n_hi - 1 - s).wait_recv()
                total = total + wide(third.at[s, q])
            out_ref[pl.ds(q * rows, rows), :] = total.astype(out_ref.dtype)

    @pl.loop(0, steps)
    def _(t):
        for v in range(2):
            if n_core > 1:
                core_copy(t, v).wait_send()
            for stage in range(depth):
                for ahead in range(1, at.sizes()[orders[v][stage]]):
                    mid_copy(t, v, stage, ahead).wait_send()

            @pl.when(t // pairs < n_hi - 1)
            def _(v=v):
                last_copy(t, v, 1).wait_send()


def scatter_sum(partial, counts, fsdp_too, parts, out_dtype, ident, name):
    n_hi, n_lo, n_x, n_core = counts
    rows, width = partial.shape[4:]
    r = rows // parts
    units = n_hi * parts
    keep = max(n_x, n_lo)
    peers = max(n_x, n_lo, 2) - 1
    b16 = jnp.bfloat16
    own_shape = (2, 2, n_x, n_lo, r, width) if n_core > 1 else (1, 1, 1, 1, 16, 128)
    scratch = [
        pltpu.VMEM(own_shape, b16),
        pltpu.VMEM((units, n_x, n_lo, r, width), b16),
        pltpu.VMEM((units, peers, keep, r, width), b16),
        pltpu.VMEM((units, peers, r, width), b16),
        pltpu.VMEM((max(n_hi - 1, 1), parts, r, width), b16),
        pltpu.SemaphoreType.DMA((2, 2)),
        pltpu.SemaphoreType.DMA((units,)),
        pltpu.SemaphoreType.DMA((units,)),
        pltpu.SemaphoreType.DMA((units, peers)),
        pltpu.SemaphoreType.DMA((units, peers)),
        pltpu.SemaphoreType.DMA((units, peers)),
        pltpu.SemaphoreType.DMA((units, peers)),
        pltpu.SemaphoreType.DMA((units,)),
        pltpu.SemaphoreType.DMA((max(n_hi - 1, 1), parts)),
    ]
    return pl.pallas_call(
        functools.partial(scatter_kernel, counts, parts, fsdp_too),
        in_specs=[pl.BlockSpec(memory_space=pl.ANY)],
        out_specs=pl.BlockSpec(memory_space=pltpu.VMEM),
        out_shape=jax.ShapeDtypeStruct((rows, width), out_dtype),
        scratch_shapes=scratch,
        compiler_params=pltpu.CompilerParams(
            collective_id=ident, has_side_effects=True, vmem_limit_bytes=60 * 2**20
        ),
        cost_estimate=pl.CostEstimate(
            flops=partial.size, bytes_accessed=2 * partial.size, transcendentals=0
        ),
        name=name,
    )(partial)


def gather_kernel(
    counts, parts, fsdp_too, in_ref, out_ref, own_sem, s0, r0, s1, r1, s2, r2, s3, r3
):
    at = Place(counts, fsdp_too)
    n_hi, n_lo, n_x, n_core = counts
    rows = in_ref.shape[0] // parts
    pairs = parts // 2
    steps = n_hi * pairs
    orders = [[d for d in o if at.sizes()[d] > 1] for o in (("lo", "x"), ("x", "lo"))]
    depth = len(orders[0])

    def remote(src, dst, send, recv, dim, ahead):
        return pltpu.make_async_remote_copy(
            src_ref=src, dst_ref=dst, send_sem=send, recv_sem=recv,
            device_id=at.peer(dim, ahead), device_id_type=MESH,
        )

    def span(q):
        return pl.ds(pl.multiple_of(q * rows, 16), rows)

    def hi_copy(q, ahead):
        return remote(
            in_ref.at[span(q)], out_ref.at[at.x, at.core, at.hi, at.lo, span(q)],
            s0.at[ahead - 1, q], r0.at[n_hi - ahead - 1, q], "hi", ahead,
        )

    def where(t, v):
        return (at.hi + n_hi - t // pairs) % n_hi, t % pairs * 2 + v

    def mid_copy(t, v, stage, ahead):
        u = 2 * t + v
        hi, q = where(t, v)
        dim = orders[v][stage]
        size = at.sizes()[dim]
        if stage == 0:
            ref = out_ref.at[at.x, at.core, hi, at.lo, span(q)]
            if_own = in_ref.at[span(q)]
            del if_own
            return remote(
                ref, ref, s1.at[u, ahead - 1], r1.at[u, size - ahead - 1], dim, ahead
            )
        if dim == "x":
            ref = out_ref.at[at.x, at.core, hi, :, span(q)]
        else:
            ref = out_ref.at[:, at.core, hi, at.lo, span(q)]
        return remote(ref, ref, s2.at[u, ahead - 1], r2.at[u, size - ahead - 1], dim, ahead)

    def core_copy(t, v):
        u = 2 * t + v
        hi, q = where(t, v)
        ref = out_ref.at[:, at.core, hi, :, span(q)]
        return remote(ref, ref, s3.at[u], r3.at[u], "core", 1)

    def each_mid(t, v, stage, act):
        size = at.sizes()[orders[v][stage]]
        for ahead in range(1, size):
            act(mid_copy(t, v, stage, ahead))

    keep = pltpu.make_async_copy(
        in_ref, out_ref.at[at.x, at.core, at.hi, at.lo], own_sem
    )
    keep.start()
    at.meet()
    for ahead in range(1, n_hi):
        for q in range(parts):
            hi_copy(q, ahead).start()
    keep.wait()

    @pl.loop(0, steps + depth)
    def _(t):
        @pl.when(t < steps)
        def _():
            for v in range(2):
                _, q = where(t, v)
                for k in range(1, n_hi):

                    @pl.when(t // pairs == k)
                    def _(k=k, q=q):
                        hi_copy(q, k).wait_recv()

                if depth > 0:
                    each_mid(t, v, 0, lambda c: c.start())
                elif n_core > 1:
                    core_copy(t, v).start()

        for stage in range(depth):
            back = stage + 1

            @pl.when((t >= back) & (t < steps + back))
            def _(stage=stage, back=back):
                for v in range(2):
                    each_mid(t - back, v, stage, lambda c: c.wait_recv())
                    if stage + 1 < depth:
                        each_mid(t - back, v, stage + 1, lambda c: c.start())
                    elif n_core > 1:
                        core_copy(t - back, v).start()

    @pl.loop(0, steps)
    def _(t):
        for v in range(2):
            if n_core > 1:
                core_copy(t, v).wait_recv()
                core_copy(t, v).wait_send()
            for stage in range(depth):
                each_mid(t, v, stage, lambda c: c.wait_send())

    for q in range(parts):
        for ahead in range(1, n_hi):
            hi_copy(q, ahead).wait_send()


def gather_rows(own, counts, fsdp_too, parts, ident, name):
    n_hi, n_lo, n_x, n_core = counts
    rows, width = own.shape
    units = n_hi * parts
    peers = max(n_x, n_lo, 2) - 1
    ahead = max(n_hi - 1, 1)
    scratch = [
        pltpu.SemaphoreType.DMA,
        pltpu.SemaphoreType.DMA((ahead, parts)),
        pltpu.SemaphoreType.DMA((ahead, parts)),
        pltpu.SemaphoreType.DMA((units, peers)),
        pltpu.SemaphoreType.DMA((units, peers)),
        pltpu.SemaphoreType.DMA((units, peers)),
        pltpu.SemaphoreType.DMA((units, peers)),
        pltpu.SemaphoreType.DMA((units,)),
        pltpu.SemaphoreType.DMA((units,)),
    ]
    total = rows * n_hi * n_lo * n_x * n_core
    out = pl.pallas_call(
        functools.partial(gather_kernel, counts, parts, fsdp_too),
        in_specs=[pl.BlockSpec(memory_space=pl.ANY)],
        out_specs=pl.BlockSpec(memory_space=pl.ANY),
        out_shape=jax.ShapeDtypeStruct((n_x, n_core, n_hi, n_lo, rows, width), own.dtype),
        scratch_shapes=scratch,
        compiler_params=pltpu.CompilerParams(collective_id=ident, has_side_effects=True),
        cost_estimate=pl.CostEstimate(
            flops=0, bytes_accessed=4 * total * width, transcendentals=0
        ),
        name=name,
    )(own)
    return out.reshape(total, width)


def attend(query_heads, key_heads, value_heads, lengths):
    seq_rows, head_local, _ = query_heads.shape
    block_rows, block_count, key_rows, pad_rows = window_geometry(seq_rows)
    segments = segment_ids(lengths, seq_rows)
    seg_padded = pad_front(segments, pad_rows, -1)
    key_padded = pad_front(key_heads, pad_rows, 0.0)
    value_padded = pad_front(value_heads, pad_rows, 0.0)
    score_scale = HEAD_DIM ** (-0.5)
    block_numbers = jnp.arange(block_count, dtype=jnp.int32)

    def block_scores(first_row):
        query_block = lax.dynamic_slice_in_dim(query_heads, first_row, block_rows)
        key_block = lax.dynamic_slice_in_dim(key_padded, first_row, key_rows)
        scores = (
            jnp.einsum("qhd,khd->hqk", query_block, key_block, preferred_element_type=jnp.float32)
            * score_scale
        )
        allowed = window_allowed(segments, seg_padded, first_row, block_rows, key_rows, pad_rows)
        return (jnp.where(allowed[None], scores, masked_score), query_block, key_block)

    def forward_block(carry_in, block_index):
        first_row = block_index * block_rows
        scores, query_block, key_block = block_scores(first_row)
        value_block = lax.dynamic_slice_in_dim(value_padded, first_row, key_rows)
        row_max = jnp.max(scores, axis=-1, keepdims=True)
        weights = jnp.exp(scores - row_max)
        row_total = jnp.sum(weights, axis=-1, keepdims=True)
        probs = (weights / row_total).astype(jnp.bfloat16)
        attended = jnp.einsum(
            "hqk,khd->qhd", probs, value_block, preferred_element_type=jnp.float32
        )
        return (carry_in, (attended.astype(jnp.bfloat16), (row_max + jnp.log(row_total))[..., 0]))

    _, (attended_blocks, lse_blocks) = lax.scan(forward_block, 0, block_numbers)
    attended_heads = attended_blocks.reshape(seq_rows, head_local, HEAD_DIM)

    def back(attended_grad_heads):
        def backward_block(carry_in, block_index):
            key_total, value_total = carry_in
            first_row = block_index * block_rows
            scores, query_block, key_block = block_scores(first_row)
            value_block = lax.dynamic_slice_in_dim(value_padded, first_row, key_rows)
            grad_block = lax.dynamic_slice_in_dim(attended_grad_heads, first_row, block_rows)
            probs = jnp.exp(scores - lse_blocks[block_index][..., None])
            prob_grad = jnp.einsum(
                "qhd,khd->hqk", grad_block, value_block, preferred_element_type=jnp.float32
            )
            row_delta = jnp.sum(probs * prob_grad, axis=-1, keepdims=True)
            score_grad = (probs * (prob_grad - row_delta)).astype(jnp.bfloat16)
            query_part = (
                jnp.einsum("hqk,khd->qhd", score_grad, key_block, preferred_element_type=jnp.float32)
                * score_scale
            )
            key_part = (
                jnp.einsum("hqk,qhd->khd", score_grad, query_block, preferred_element_type=jnp.float32)
                * score_scale
            )
            value_part = jnp.einsum(
                "hqk,qhd->khd",
                probs.astype(jnp.bfloat16),
                grad_block,
                preferred_element_type=jnp.float32,
            )
            key_total = lax.dynamic_update_slice_in_dim(
                key_total,
                lax.dynamic_slice_in_dim(key_total, first_row, key_rows) + key_part,
                first_row,
                0,
            )
            value_total = lax.dynamic_update_slice_in_dim(
                value_total,
                lax.dynamic_slice_in_dim(value_total, first_row, key_rows) + value_part,
                first_row,
                0,
            )
            return ((key_total, value_total), query_part.astype(jnp.bfloat16))

        zero_keys = jnp.zeros((pad_rows + seq_rows, head_local, HEAD_DIM), jnp.float32)
        (key_total, value_total), query_blocks = lax.scan(
            backward_block, (zero_keys, zero_keys), block_numbers
        )
        query_grad_heads = query_blocks.reshape(seq_rows, head_local, HEAD_DIM)
        key_grad_heads = key_total[pad_rows:].astype(jnp.bfloat16)
        value_grad_heads = value_total[pad_rows:].astype(jnp.bfloat16)
        return query_grad_heads, key_grad_heads, value_grad_heads

    return attended_heads, back


def scatter_over_all(partial, rows, sp_count, fs_count, ident, name):
    counts = mesh_counts(sp_count, fs_count)
    width = partial.shape[1]
    parts = 4 if rows % 64 == 0 else 2
    if 1.4 * partial.size * 2 > 52 * 2**20 or rows % (parts * 16):
        part = lax.psum_scatter(partial, "fsdp", scatter_dimension=0, tiled=True)
        return lax.psum_scatter(part, "sp", scatter_dimension=0, tiled=True).astype(jnp.float32)
    n_hi, n_lo, n_x, n_core = counts
    shaped = partial.reshape(n_x, n_core, n_hi, n_lo, rows, width)
    return scatter_sum(shaped, counts, True, parts, jnp.float32, ident, name)


def scatter_over_sp(partial, rows, sp_count, ident, name):
    n_hi, n_lo, _, _ = mesh_counts(sp_count, 1)
    parts = 4 if rows % 64 == 0 else 2
    shaped = partial.reshape(1, 1, n_hi, n_lo, rows, partial.shape[1])
    return scatter_sum(shaped, (n_hi, n_lo, 1, 1), False, parts, jnp.float32, ident, name)


def gather_over_all(own, sp_count, fs_count, ident, name):
    parts = 4 if own.shape[0] % 64 == 0 else 2
    return gather_rows(own, mesh_counts(sp_count, fs_count), True, parts, ident, name)


def gather_over_sp(own, sp_count, ident, name):
    n_hi, n_lo, _, _ = mesh_counts(sp_count, 1)
    parts = 4 if own.shape[0] % 64 == 0 else 2
    return gather_rows(own, (n_hi, n_lo, 1, 1), False, parts, ident, name)


def local(
    tokens,
    doc_lengths,
    expert_ids,
    norm_attn,
    norm_query,
    norm_key,
    norm_ffn,
    w_query,
    w_key,
    w_value,
    w_out,
    w_router,
    w_gate,
    w_up,
    w_down,
    cotangent,
):
    sp_count = lax.axis_size("sp")
    fs_count = lax.axis_size("fsdp")
    my_sp = lax.axis_index("sp")
    my_fs = lax.axis_index("fsdp")
    hidden_in = tokens[0].astype(jnp.float32)
    tok_rows, width = hidden_in.shape
    head_local = HEADS // sp_count
    seq_rows = tok_rows * sp_count
    span = head_local * HEAD_DIM
    expert_local = EXPERTS // sp_count
    first_expert = my_sp * expert_local
    gains = lax.all_gather(
        jnp.stack([norm_attn, norm_query, norm_key, norm_ffn]), "fsdp", axis=1, tiled=True
    ).astype(jnp.float32)
    gain_attn, gain_ffn = gains[0], gains[3]
    own_cols = lax.dynamic_slice_in_dim(gains, my_sp * span, span, axis=1)
    gain_query, gain_key = own_cols[1], own_cols[2]
    qkv_own = jnp.concatenate(
        [
            lax.dynamic_slice_in_dim(w, my_sp * span, span, axis=1)
            for w in (w_query, w_key, w_value)
        ],
        axis=1,
    )
    qkv_mat = lax.all_gather(qkv_own, "fsdp", axis=0, tiled=True)
    out_mat = lax.all_gather(w_out, "fsdp", axis=0, tiled=True)
    router_mat = lax.all_gather(w_router, "fsdp", axis=0, tiled=True)
    cot_all = lax.all_gather(cotangent[0], ("fsdp", "sp"), axis=0, tiled=True)
    routing = route_plan(expert_ids[0], sp_count, fs_count)
    cot_rows, _ = dispatch_rows(cot_all, routing, None)

    attn_normed, attn_pull = jax.vjp(rms_scale, hidden_in, gain_attn)
    attn_in = gather_over_sp(attn_normed.astype(jnp.bfloat16), sp_count, 1, "gather_attn_in")
    qkv_raw = jnp.dot(attn_in, qkv_mat, preferred_element_type=jnp.float32)
    raw = (qkv_raw[:, :span], qkv_raw[:, span : 2 * span])
    value_heads = qkv_raw[:, 2 * span :].astype(jnp.bfloat16).reshape(
        seq_rows, head_local, HEAD_DIM
    )
    squares = lax.psum(jnp.stack([jnp.sum(r * r, axis=-1) for r in raw]), "sp")
    scales = lax.rsqrt(squares / width + eps)[:, :, None]
    cosine, sine = rope_tables(jnp.arange(seq_rows, dtype=jnp.int32), HEAD_DIM)

    def turned(normed):
        return rotate_pairs(normed.reshape(seq_rows, head_local, HEAD_DIM), cosine, sine)

    query_heads = turned(raw[0] * scales[0] * gain_query).astype(jnp.bfloat16)
    key_heads = turned(raw[1] * scales[1] * gain_key).astype(jnp.bfloat16)
    attended_heads, attend_back = attend(query_heads, key_heads, value_heads, doc_lengths[0])
    attended_tok = lax.all_to_all(
        attended_heads.reshape(seq_rows, span), "sp", split_axis=0, concat_axis=1, tiled=True
    )
    after_attn = hidden_in + jnp.dot(attended_tok, out_mat, preferred_element_type=jnp.float32)
    ffn_normed, ffn_pull = jax.vjp(rms_scale, after_attn, gain_ffn)
    ffn_in = ffn_normed.astype(jnp.bfloat16)
    logits = jnp.dot(ffn_in, router_mat, preferred_element_type=jnp.float32)
    router = jax.nn.softmax(logits, axis=-1)
    ffn_all = gather_over_all(ffn_in, sp_count, fs_count, 2, "gather_ffn_in")
    router_all = jax.nn.softmax(
        jnp.dot(ffn_all, router_mat, preferred_element_type=jnp.float32), axis=-1
    )
    gate_rows = (
        lax.dynamic_slice_in_dim(router_all, first_expert, expert_local, axis=1)
        .reshape(-1, BLOCK, expert_local)
        .transpose(0, 2, 1)
    )
    ffn_rows, gate_slots = dispatch_rows(ffn_all, routing, gate_rows)
    out_rows, in_grad_rows, grad_gate, grad_up, grad_down = run_experts(
        ffn_rows, cot_rows, gate_slots, w_gate, w_up, w_down, routing[3], first_expert[None]
    )
    in_grad_sum = scatter_over_all(
        combine_rows(in_grad_rows, routing, "combine_grads"),
        tok_rows, sp_count, fs_count, 3, "scatter_grads",
    )
    moe_sum = scatter_over_all(
        combine_rows(out_rows, routing, "combine_outputs"),
        tok_rows, sp_count, fs_count, 4, "scatter_outputs",
    )
    mixed = (after_attn + moe_sum).astype(jnp.bfloat16)
    upstream = cotangent[0].astype(jnp.float32)
    ffn_in_grad = in_grad_sum[:, :width]
    router_grad = in_grad_sum[:, width : width + EXPERTS]
    logit_grad = (
        router * (router_grad - jnp.sum(router * router_grad, axis=-1, keepdims=True))
    ).astype(jnp.bfloat16)
    ffn_in_grad = ffn_in_grad + jnp.dot(
        logit_grad, router_mat.T, preferred_element_type=jnp.float32
    )
    router_term = jnp.dot(ffn_in.T, logit_grad, preferred_element_type=jnp.float32)
    ffn_hidden_grad, ffn_gain_term = ffn_pull(ffn_in_grad)
    after_grad = upstream + ffn_hidden_grad
    attn_out_grad = after_grad.astype(jnp.bfloat16)
    attended_grad = jnp.dot(attn_out_grad, out_mat.T, preferred_element_type=jnp.float32).astype(
        jnp.bfloat16
    )
    attended_grad_heads = lax.all_to_all(
        attended_grad, "sp", split_axis=1, concat_axis=0, tiled=True
    ).reshape(seq_rows, head_local, HEAD_DIM)
    out_term = jnp.dot(attended_tok.T, attn_out_grad, preferred_element_type=jnp.float32)
    row_terms = jnp.concatenate(
        [
            out_term.astype(jnp.bfloat16),
            router_term.astype(jnp.bfloat16),
            jnp.zeros((width, 128 - EXPERTS), jnp.bfloat16),
        ],
        axis=1,
    )
    row_sums = scatter_over_all(
        row_terms, width // (sp_count * fs_count), sp_count, fs_count, 5, "scatter_out_rows"
    )
    query_grad_heads, key_grad_heads, value_low = attend_back(attended_grad_heads)

    def unturned(grad):
        return rotate_pairs(grad.astype(jnp.float32), cosine, -sine).reshape(seq_rows, span)

    normed_grads = (unturned(query_grad_heads), unturned(key_grad_heads))
    scaled_grads = (normed_grads[0] * gain_query, normed_grads[1] * gain_key)
    products = lax.psum(
        jnp.stack([jnp.sum(g * r, axis=-1) for g, r in zip(scaled_grads, raw)]), "sp"
    )[:, :, None]
    gain_terms = [
        jnp.sum(g * r * s, axis=0) for g, r, s in zip(normed_grads, raw, scales)
    ]
    raw_grads = [
        (g * s - r * (s * s * s) * (p / width)).astype(jnp.bfloat16)
        for g, r, s, p in zip(scaled_grads, raw, scales, products)
    ]
    qkv_low = jnp.concatenate(raw_grads + [value_low.reshape(seq_rows, span)], axis=1)
    attn_partial = lax.dot_general(
        qkv_low, qkv_mat, (((1,), (1,)), ((), ())), preferred_element_type=jnp.float32
    ).astype(jnp.bfloat16)
    attn_in_grad = scatter_over_sp(attn_partial, tok_rows, sp_count, 6, "scatter_attn_in")
    qkv_term = jnp.dot(attn_in.T, qkv_low, preferred_element_type=jnp.float32)
    attn_hidden_grad, attn_gain_term = attn_pull(attn_in_grad)
    grad_tokens = after_grad + attn_hidden_grad
    qkv_sums = lax.psum_scatter(
        qkv_term.astype(jnp.bfloat16), "fsdp", scatter_dimension=0, tiled=True
    )
    qkv_every = lax.all_gather(qkv_sums, "sp", axis=0)
    rows_every = lax.all_gather(row_sums.astype(jnp.bfloat16), "sp", axis=0, tiled=True)
    dense = [
        qkv_every[:, :, k * span : (k + 1) * span]
        .transpose(1, 0, 2)
        .reshape(-1, width)
        .astype(jnp.float32)
        for k in range(3)
    ]
    placed = [
        lax.dynamic_update_slice_in_dim(jnp.zeros((width,), jnp.float32), g, my_sp * span, 0)
        for g in gain_terms
    ]
    gain_sums = lax.psum(
        jnp.stack([attn_gain_term, placed[0], placed[1], ffn_gain_term]), ("sp", "fsdp")
    )
    gain_sums = lax.dynamic_slice_in_dim(
        gain_sums, my_fs * (width // fs_count), width // fs_count, axis=1
    )
    return (
        mixed[None],
        grad_tokens[None],
        gain_sums[0],
        gain_sums[1],
        gain_sums[2],
        gain_sums[3],
        dense[0],
        dense[1],
        dense[2],
        rows_every[:, :width].astype(jnp.float32),
        rows_every[:, width : width + EXPERTS].astype(jnp.float32),
        grad_gate,
        grad_up,
        grad_down,
    )


def solution(mesh):
    in_specs = (
        P("fsdp", "sp", None),
        P("fsdp", None),
        P("fsdp", "sp", None),
        P("fsdp"),
        P("fsdp"),
        P("fsdp"),
        P("fsdp"),
        P("fsdp", None),
        P("fsdp", None),
        P("fsdp", None),
        P("fsdp", None),
        P("fsdp", None),
        P("sp", None, "fsdp"),
        P("sp", None, "fsdp"),
        P("sp", None, "fsdp"),
        P("fsdp", "sp", None),
    )
    out_specs = (
        P("fsdp", "sp", None),
        P("fsdp", "sp", None),
        P("fsdp"),
        P("fsdp"),
        P("fsdp"),
        P("fsdp"),
        P("fsdp", None),
        P("fsdp", None),
        P("fsdp", None),
        P("fsdp", None),
        P("fsdp", None),
        P("sp", None, "fsdp"),
        P("sp", None, "fsdp"),
        P("sp", None, "fsdp"),
    )
    return jax.shard_map(local, mesh=mesh, in_specs=in_specs, out_specs=out_specs, check_vma=False)
```

```python
import functools

import jax
import jax.numpy as jnp
from jax import lax
from jax.experimental import pallas as pl
from jax.experimental.pallas import tpu as pltpu
from jax.sharding import PartitionSpec as P

HEADS = 16
HEAD_DIM = 128
EXPERTS = 64
TOPK = 8
WINDOW = 1024


eps = 1e-05
rope_base = 10000.0
masked_score = -1e30


def rms_scale(values, gain_vec):
    return values * lax.rsqrt(jnp.mean(values * values, axis=-1, keepdims=True) + eps) * gain_vec


def rotate_pairs(values, cosine, sine):
    half_dim = values.shape[-1] // 2
    turned = jnp.concatenate([-values[..., half_dim:], values[..., :half_dim]], axis=-1)
    return values * cosine + turned * sine


def rope_tables(positions, head_size):
    inv_freq = rope_base ** (-jnp.arange(0, head_size, 2, dtype=jnp.float32) / head_size)
    phase_half = positions.astype(jnp.float32)[:, None] * inv_freq[None, :]
    phase_all = jnp.concatenate([phase_half, phase_half], axis=-1)
    return (jnp.cos(phase_all)[:, None, :], jnp.sin(phase_all)[:, None, :])


BLOCK = 256
SLOTS = 64
STEP = 16
TILE = 256


def exclusive_sum(values):
    count = values.shape[0]
    lower = (jnp.arange(count)[:, None] > jnp.arange(count)[None, :]).astype(jnp.float32)
    total = jnp.dot(lower, values.astype(jnp.float32), precision=lax.Precision.HIGHEST)
    return total.astype(jnp.int32)


def route_plan(own_ids, sp_count, fs_count):
    local_experts = EXPERTS // sp_count
    per_device = own_ids.size
    packed = jnp.zeros((32, 128), jnp.bfloat16)
    packed = packed.at[: per_device // 128].set(own_ids.astype(jnp.bfloat16).reshape(-1, 128))
    packed = gather_over_all(packed, sp_count, fs_count, 10, "gather_ids")
    ids = packed.reshape(-1, 32 * 128)[:, :per_device].reshape(-1, TOPK).astype(jnp.int32)
    tokens = ids.shape[0]
    blocks = tokens // BLOCK
    capacity = 5 * tokens * TOPK // (4 * EXPERTS)
    first = lax.axis_index("sp") * local_experts
    mine = first + jnp.arange(local_experts, dtype=jnp.int32)
    named = jnp.any(ids[:, None, :] == mine[None, :, None], axis=-1)
    named = named.reshape(blocks, BLOCK, local_experts)
    upto = (jnp.arange(BLOCK)[:, None] >= jnp.arange(BLOCK)[None, :]).astype(jnp.bfloat16)
    running = jnp.einsum(
        "ts,bse->bte", upto, named.astype(jnp.bfloat16), preferred_element_type=jnp.float32
    ).astype(jnp.int32)
    earlier = exclusive_sum(running[:, -1])
    keep = named & (earlier[:, None, :] + running - 1 < capacity)
    rank = jnp.where(keep, running - 1, -1).transpose(0, 2, 1)
    steps = (jnp.sum(keep.astype(jnp.int32), axis=1) + STEP - 1) // STEP
    starts = exclusive_sum(steps)
    used = starts[-1] + steps[-1]
    slots_all = min(blocks * SLOTS, capacity + blocks * (STEP - 1))
    slots_all = (slots_all + TILE - 1) // TILE * TILE
    return rank, starts.reshape(-1), steps.reshape(-1), used, slots_all


def steps_copy(count, make, act):
    for size in range(1, SLOTS // STEP + 1):

        @pl.when(count == size)
        def _(size=size):
            act(make(size * STEP))


def start_copy(copy):
    copy.start()


def wait_copy(copy):
    copy.wait()


def pick_matrix(rank):
    experts = rank.shape[0]
    slot = lax.broadcasted_iota(jnp.int32, (SLOTS, BLOCK), 0)
    parts = [slot == rank[e : e + 1, :] for e in range(experts)]
    return parts


def dispatch_kernel(
    starts, steps, used, rank_ref, weight_ref, x_ref, out_ref, wout_ref, buf, wbuf, zeros,
    sems, wsems, zsems,
):
    experts = rank_ref.shape[1]
    width = x_ref.shape[1]
    b = pl.program_id(0)
    blocks = pl.num_programs(0)
    slot = lax.rem(b, 2)

    def make(which, e, place):
        first = starts[which * experts + e] * STEP

        def rows(size):
            return pltpu.make_async_copy(
                buf.at[place, pl.ds(e * SLOTS, size)],
                out_ref.at[e, pl.ds(pl.multiple_of(first, STEP), size)],
                sems.at[place, e],
            )

        def weights(size):
            return pltpu.make_async_copy(
                wbuf.at[place, pl.ds(e * SLOTS, size)],
                wout_ref.at[e, pl.ds(pl.multiple_of(first, STEP), size)],
                wsems.at[place, e],
            )

        return rows, weights

    def each(which, place, act):
        for e in range(experts):
            rows, weights = make(which, e, place)
            steps_copy(steps[which * experts + e], rows, act)
            if weight_ref is not None:
                steps_copy(steps[which * experts + e], weights, act)

    def fill(act):
        for e in range(experts):
            rest = lax.rem(TILE // STEP - lax.rem(used[e], TILE // STEP), TILE // STEP)
            done = used[e]
            for k, size in enumerate((8, 4, 2, 1)):
                take = lax.rem(rest // size, 2)

                @pl.when(take == 1)
                def _(e=e, k=k, size=size, done=done):
                    act(
                        pltpu.make_async_copy(
                            zeros.at[pl.ds(0, size * STEP)],
                            out_ref.at[e, pl.ds(pl.multiple_of(done * STEP, STEP), size * STEP)],
                            zsems.at[e, k],
                        )
                    )

                done = done + take * size

    @pl.when(b == 0)
    def _():
        zeros[...] = jnp.zeros_like(zeros)
        fill(start_copy)

    @pl.when(b >= 2)
    def _():
        each(b - 2, slot, wait_copy)

    parts = pick_matrix(rank_ref[0])
    if weight_ref is not None:
        for e in range(experts):
            column = jnp.sum(
                jnp.where(parts[e], weight_ref[0, e : e + 1, :], 0.0), axis=1, keepdims=True
            )
            wbuf[slot, pl.ds(e * SLOTS, SLOTS), :] = jnp.broadcast_to(column, (SLOTS, 128))
    pick = jnp.concatenate([p.astype(jnp.bfloat16) for p in parts], axis=0)
    span = 512
    for n in range(width // span):
        cols = pl.ds(n * span, span)
        buf[slot, :, cols] = jnp.dot(
            pick, x_ref[:, cols], preferred_element_type=jnp.float32
        ).astype(jnp.bfloat16)
    each(b, slot, start_copy)

    @pl.when(b == blocks - 1)
    def _():
        each(b - 1, 1 - slot, wait_copy)
        each(b, slot, wait_copy)
        fill(wait_copy)


def dispatch_rows(table, routing, weights):
    rank, starts, steps, used, slots_all = routing
    blocks, experts, _ = rank.shape
    width = table.shape[1]
    wide = pl.BlockSpec((1, experts, BLOCK), lambda b, *_: (b, 0, 0))
    anywhere = pl.BlockSpec(memory_space=pl.ANY)
    rows_shape = jax.ShapeDtypeStruct((experts, slots_all, width), jnp.bfloat16)
    scratch = [
        pltpu.VMEM((2, experts * SLOTS, width), jnp.bfloat16),
        pltpu.VMEM((2, experts * SLOTS, 128), jnp.float32),
        pltpu.VMEM((8 * STEP, width), jnp.bfloat16),
        pltpu.SemaphoreType.DMA((2, experts)),
        pltpu.SemaphoreType.DMA((2, experts)),
        pltpu.SemaphoreType.DMA((experts, 4)),
    ]
    flops = 2 * blocks * experts * SLOTS * BLOCK * width
    params = dict(
        compiler_params=pltpu.CompilerParams(
            dimension_semantics=("arbitrary",), vmem_limit_bytes=48 * 2**20
        ),
        cost_estimate=pl.CostEstimate(
            flops=flops, bytes_accessed=6 * blocks * BLOCK * width, transcendentals=0
        ),
    )
    x_spec = pl.BlockSpec((BLOCK, width), lambda b, *_: (b, 0))
    if weights is None:

        def plain(starts, steps, used, rank_ref, x_ref, out_ref, *rest):
            dispatch_kernel(
                starts, steps, used, rank_ref, None, x_ref, out_ref, None, *rest
            )

        rows = pl.pallas_call(
            plain,
            grid_spec=pltpu.PrefetchScalarGridSpec(
                num_scalar_prefetch=3,
                grid=(blocks,),
                in_specs=[wide, x_spec],
                out_specs=anywhere,
                scratch_shapes=scratch,
            ),
            out_shape=rows_shape,
            name="dispatch_cotangent",
            **params,
        )(starts, steps, used, rank, table)
        return rows, None
    return pl.pallas_call(
        dispatch_kernel,
        grid_spec=pltpu.PrefetchScalarGridSpec(
            num_scalar_prefetch=3,
            grid=(blocks,),
            in_specs=[wide, wide, x_spec],
            out_specs=[anywhere, anywhere],
            scratch_shapes=scratch,
        ),
        out_shape=[
            rows_shape,
            jax.ShapeDtypeStruct((experts, slots_all, 128), jnp.float32),
        ],
        name="dispatch_tokens",
        **params,
    )(starts, steps, used, rank, weights, table)


def contract(left, right, left_dim, right_dim):
    return lax.dot_general(
        left, right, (((left_dim,), (right_dim,)), ((), ())), preferred_element_type=jnp.float32
    )


def expert_kernel(
    used, first, x_ref, c_ref, w_ref, gate_ref, up_ref, down_ref, y_ref, dx_ref, gg_ref, gu_ref,
    gd_ref, acc_g, acc_u, acc_d,
):
    e = pl.program_id(0)
    t = pl.program_id(1)
    rows_used = used[e] * STEP
    width = x_ref.shape[2]

    @pl.when(t == 0)
    def _():
        acc_g[...] = jnp.zeros_like(acc_g)
        acc_u[...] = jnp.zeros_like(acc_u)
        acc_d[...] = jnp.zeros_like(acc_d)

    @pl.when(t * TILE < rows_used)
    def _():
        x = x_ref[0]
        c = c_ref[0]
        gate_mat = gate_ref[0]
        up_mat = up_ref[0]
        down_mat = down_ref[0]
        row = t * TILE + lax.broadcasted_iota(jnp.int32, (TILE, 1), 0)
        weight = jnp.where(row < rows_used, w_ref[0][:, 0:1], 0.0)
        gate_pre = jnp.dot(x, gate_mat, preferred_element_type=jnp.float32)
        up_pre = jnp.dot(x, up_mat, preferred_element_type=jnp.float32)
        up_act = jnp.dot(c, down_mat, preferred_element_type=jnp.float32)
        sig = 1.0 / (1.0 + jnp.exp(-gate_pre))
        silu = gate_pre * sig
        act = silu * up_pre
        gate_grad = jnp.sum(up_act * act, axis=1, keepdims=True)
        act_low = (act * weight).astype(jnp.bfloat16)
        act_grad = up_act * weight
        dgate = (act_grad * up_pre * sig * (1.0 + gate_pre * (1.0 - sig))).astype(jnp.bfloat16)
        dup = (act_grad * silu).astype(jnp.bfloat16)
        y_ref[0] = contract(act_low, down_mat, 1, 1).astype(jnp.bfloat16)
        dx_ref[0, :, 0:width] = (
            contract(dgate, gate_mat, 1, 1) + contract(dup, up_mat, 1, 1)
        ).astype(jnp.bfloat16)
        column = lax.broadcasted_iota(jnp.int32, (TILE, 128), 1)
        dx_ref[0, :, width : width + 128] = jnp.where(
            column == first[0] + e, gate_grad, 0.0
        ).astype(jnp.bfloat16)
        acc_g[...] += contract(dgate, x, 0, 0)
        acc_u[...] += contract(dup, x, 0, 0)
        acc_d[...] += contract(act_low, c, 0, 0)

    @pl.when(t == pl.num_programs(1) - 1)
    def _():
        gg_ref[0] = acc_g[...].T
        gu_ref[0] = acc_u[...].T
        gd_ref[0] = acc_d[...].T


def run_experts(x_rows, c_rows, w_rows, w_gate, w_up, w_down, used, first):
    experts, slots_all, width = x_rows.shape
    hidden = w_gate.shape[2]

    def tile_map(e, t, used, first):
        last = jnp.maximum((used[e] * STEP + TILE - 1) // TILE - 1, 0)
        return (e, jnp.minimum(t, last), 0)

    def mat_map(e, t, used, first):
        return (e, 0, 0)

    mat = pl.BlockSpec((1, width, hidden), mat_map)
    return pl.pallas_call(
        expert_kernel,
        grid_spec=pltpu.PrefetchScalarGridSpec(
            num_scalar_prefetch=2,
            grid=(experts, slots_all // TILE),
            in_specs=[
                pl.BlockSpec((1, TILE, width), tile_map),
                pl.BlockSpec((1, TILE, width), tile_map),
                pl.BlockSpec((1, TILE, 128), tile_map),
                mat,
                mat,
                mat,
            ],
            out_specs=[
                pl.BlockSpec((1, TILE, width), tile_map),
                pl.BlockSpec((1, TILE, width + 128), tile_map),
                mat,
                mat,
                mat,
            ],
            scratch_shapes=[pltpu.VMEM((hidden, width), jnp.float32)] * 3,
        ),
        out_shape=[
            jax.ShapeDtypeStruct((experts, slots_all, width), jnp.bfloat16),
            jax.ShapeDtypeStruct((experts, slots_all, width + 128), jnp.bfloat16),
        ]
        + [jax.ShapeDtypeStruct((experts, width, hidden), jnp.float32)] * 3,
        input_output_aliases={2: 0},
        compiler_params=pltpu.CompilerParams(
            dimension_semantics=("arbitrary", "arbitrary"), vmem_limit_bytes=60 * 2**20
        ),
        cost_estimate=pl.CostEstimate(
            flops=18 * experts * slots_all * width * hidden,
            bytes_accessed=8 * experts * slots_all * width,
            transcendentals=experts * slots_all * hidden,
        ),
        name="experts",
    )(used, first, x_rows, c_rows, w_rows, w_gate, w_up, w_down)


def combine_kernel(starts, steps, rank_ref, y_ref, out_ref, buf, sems):
    experts = rank_ref.shape[1]
    width = out_ref.shape[1]
    b = pl.program_id(0)
    blocks = pl.num_programs(0)
    slot = lax.rem(b, 2)

    def each(which, place, act):
        for e in range(experts):
            first = starts[which * experts + e] * STEP

            def rows(size, e=e, first=first):
                return pltpu.make_async_copy(
                    y_ref.at[e, pl.ds(pl.multiple_of(first, STEP), size)],
                    buf.at[place, pl.ds(e * SLOTS, size)],
                    sems.at[place, e],
                )

            steps_copy(steps[which * experts + e], rows, act)

    @pl.when(b == 0)
    def _():
        buf[...] = jnp.zeros_like(buf)
        each(0, 0, start_copy)

    @pl.when(b + 1 < blocks)
    def _():
        each(b + 1, 1 - slot, start_copy)

    pick = jnp.concatenate([p.astype(jnp.bfloat16) for p in pick_matrix(rank_ref[0])], axis=0)
    each(b, slot, wait_copy)
    done = 0
    while done < width:
        span = min(512, width - done)
        cols = pl.ds(done, span)
        out_ref[:, cols] = contract(pick, buf[slot, :, cols], 0, 0).astype(jnp.bfloat16)
        done += span


def combine_rows(rows, routing, name):
    rank, starts, steps, used, slots_all = routing
    blocks, experts, _ = rank.shape
    width = rows.shape[2]
    return pl.pallas_call(
        combine_kernel,
        grid_spec=pltpu.PrefetchScalarGridSpec(
            num_scalar_prefetch=2,
            grid=(blocks,),
            in_specs=[
                pl.BlockSpec((1, experts, BLOCK), lambda b, *_: (b, 0, 0)),
                pl.BlockSpec(memory_space=pl.ANY),
            ],
            out_specs=pl.BlockSpec((BLOCK, width), lambda b, *_: (b, 0)),
            scratch_shapes=[
                pltpu.VMEM((2, experts * SLOTS, width), jnp.bfloat16),
                pltpu.SemaphoreType.DMA((2, experts)),
            ],
        ),
        out_shape=jax.ShapeDtypeStruct((blocks * BLOCK, width), jnp.bfloat16),
        compiler_params=pltpu.CompilerParams(
            dimension_semantics=("arbitrary",), vmem_limit_bytes=48 * 2**20
        ),
        cost_estimate=pl.CostEstimate(
            flops=2 * blocks * experts * SLOTS * BLOCK * width,
            bytes_accessed=6 * blocks * BLOCK * width,
            transcendentals=0,
        ),
        name=name,
    )(starts, steps, rank, rows)


MESH = pl.DeviceIdType.MESH


class Place:
    def __init__(self, counts, fsdp_too):
        self.n_hi, self.n_lo, self.n_x, self.n_core = counts
        sp = lax.axis_index("sp")
        self.hi, self.lo = sp // self.n_lo, sp % self.n_lo
        if fsdp_too:
            fs = lax.axis_index("fsdp")
            self.x, self.core = fs // self.n_core, fs % self.n_core
        else:
            self.x, self.core = 0, 0

    def peer(self, dim, ahead):
        if dim == "core":
            return {"fsdp": self.x * self.n_core + (self.core + ahead) % self.n_core}
        if dim == "x":
            return {"fsdp": (self.x + ahead) % self.n_x * self.n_core + self.core}
        if dim == "lo":
            return {"sp": self.hi * self.n_lo + (self.lo + ahead) % self.n_lo}
        return {"sp": (self.hi + ahead) % self.n_hi * self.n_lo + self.lo}

    def sizes(self):
        return {"core": self.n_core, "x": self.n_x, "lo": self.n_lo, "hi": self.n_hi}

    def meet(self):
        barrier = pltpu.get_barrier_semaphore()
        met = 0
        for dim, size in self.sizes().items():
            for ahead in range(1, size):
                pl.semaphore_signal(
                    barrier, inc=1, device_id=self.peer(dim, ahead), device_id_type=MESH
                )
                met += 1
        pl.semaphore_wait(barrier, met)


def mesh_counts(sp_count, fs_count):
    low = 2
    while low * low < sp_count // 2:
        low *= 2
    low = min(low, sp_count)
    core = 2 if fs_count % 2 == 0 else 1
    return sp_count // low, low, fs_count // core, core


def scatter_kernel(
    counts, parts, fsdp_too, part_ref, out_ref, own, buf, first, second, third, own_sem, s0, r0,
    s1, r1, s2, r2, s3, r3,
):
    at = Place(counts, fsdp_too)
    n_hi, n_lo, n_x, n_core = counts
    rows = out_ref.shape[0] // parts
    pairs = parts // 2
    steps = n_hi * pairs
    lag = 1
    orders = [[d for d in o if at.sizes()[d] > 1] for o in (("x", "lo"), ("lo", "x"))]

    def remote(src, dst, send, recv, dim, ahead):
        return pltpu.make_async_remote_copy(
            src_ref=src, dst_ref=dst, send_sem=send, recv_sem=recv,
            device_id=at.peer(dim, ahead), device_id_type=MESH,
        )

    def where(t, v):
        return (at.hi + 1 + t // pairs) % n_hi, t % pairs * 2 + v

    def mine(t, v, core):
        hi, q = where(t, v)
        return part_ref.at[:, core, hi, :, pl.ds(pl.multiple_of(q * rows, 16), rows), :]

    def load_own(t, v):
        place = own.at[t % 2, v] if n_core > 1 else buf.at[2 * t + v]
        return pltpu.make_async_copy(mine(t, v, at.core), place, own_sem.at[t % 2, v])

    def core_copy(t, v):
        return remote(
            mine(t, v, (at.core + 1) % 2), buf.at[2 * t + v], s0.at[2 * t + v], r0.at[2 * t + v],
            "core", 1,
        )

    def mid_copy(t, v, stage, ahead):
        u = 2 * t + v
        dim = orders[v][stage]
        size = at.sizes()[dim]
        to = ((at.x if dim == "x" else at.lo) + ahead) % size
        if stage == 0:
            src = buf.at[u, to] if dim == "x" else buf.at[u, :, to]
            dst = first.at[u, size - ahead - 1, pl.ds(0, n_lo if dim == "x" else n_x)]
            return remote(
                src, dst, s1.at[u, ahead - 1], r1.at[u, size - ahead - 1], dim, ahead
            )
        return remote(
            first.at[u, 0, to], second.at[u, size - ahead - 1],
            s2.at[u, ahead - 1], r2.at[u, size - ahead - 1], dim, ahead,
        )

    def wait_in(t, v, stage):
        size = at.sizes()[orders[v][stage]]
        for ahead in range(1, size):
            mid_copy(t, v, stage, ahead).wait_recv()

    def start_out(t, v, stage):
        size = at.sizes()[orders[v][stage]]
        for ahead in range(1, size):
            mid_copy(t, v, stage, ahead).start()

    def wide(ref):
        return ref[...].astype(jnp.float32)

    def result(t, v):
        u = 2 * t + v
        if len(orders[v]) == 2:
            return second.at[u, 0]
        if len(orders[v]) == 1:
            return first.at[u, 0, 0]
        return buf.at[u, 0, 0]

    def last_copy(t, v, ahead):
        _, q = where(t, v)
        return remote(
            result(t, v), third.at[n_hi - ahead - 1, q],
            s3.at[2 * t + v], r3.at[n_hi - ahead - 1, q], "hi", ahead,
        )

    def send_last(t, v):
        for k in range(n_hi - 1):

            @pl.when(t // pairs == k)
            def _(k=k):
                last_copy(t, v, k + 1).start()

    def stage_core(t, v):
        u = 2 * t + v
        load_own(t, v).wait()
        if n_core > 1:
            core_copy(t, v).wait_recv()

            @pl.loop(0, n_x * n_lo)
            def _(j):
                x, lo = j // n_lo, j % n_lo
                place = buf.at[u, x, lo]
                place[...] = (wide(place) + wide(own.at[t % 2, v, x, lo])).astype(jnp.bfloat16)

        if orders[v]:
            start_out(t, v, 0)
        else:
            send_last(t, v)

    def stage_mid(t, v, stage):
        u = 2 * t + v
        wait_in(t, v, stage)
        dim = orders[v][stage]
        size = at.sizes()[dim]
        if stage == 0:
            keep = n_lo if dim == "x" else n_x

            @pl.loop(0, keep)
            def _(j):
                base = buf.at[u, at.x, j] if dim == "x" else buf.at[u, j, at.lo]
                total = wide(base)
                for s in range(size - 1):
                    total = total + wide(first.at[u, s, j])
                first.at[u, 0, j][...] = total.astype(jnp.bfloat16)

        else:
            base = first.at[u, 0, at.x if dim == "x" else at.lo]
            total = wide(base)
            for s in range(size - 1):
                total = total + wide(second.at[u, s])
            second.at[u, 0][...] = total.astype(jnp.bfloat16)
        if stage + 1 < len(orders[v]):
            start_out(t, v, stage + 1)
        else:
            send_last(t, v)

    at.meet()
    if n_core > 1:

        @pl.loop(0, steps)
        def _(t):
            for v in range(2):
                core_copy(t, v).start()

    for v in range(2):
        load_own(0, v).start()

    depth = len(orders[0])

    @pl.loop(0, steps + depth * lag)
    def _(t):
        @pl.when(t + 1 < steps)
        def _():
            for v in range(2):
                load_own(t + 1, v).start()

        @pl.when(t < steps)
        def _():
            for v in range(2):
                stage_core(t, v)

        for stage in range(depth):
            back = (stage + 1) * lag

            @pl.when((t >= back) & (t < steps + back))
            def _(stage=stage, back=back):
                for v in range(2):
                    stage_mid(t - back, v, stage)

    for g in range(pairs):
        t = (n_hi - 1) * pairs + g
        for v in range(2):
            q = g * 2 + v
            total = wide(result(t, v))
            for s in range(n_hi - 1):
                last_copy(g, v, n_hi - 1 - s).wait_recv()
                total = total + wide(third.at[s, q])
            out_ref[pl.ds(q * rows, rows), :] = total.astype(out_ref.dtype)

    @pl.loop(0, steps)
    def _(t):
        for v in range(2):
            if n_core > 1:
                core_copy(t, v).wait_send()
            for stage in range(depth):
                for ahead in range(1, at.sizes()[orders[v][stage]]):
                    mid_copy(t, v, stage, ahead).wait_send()

            @pl.when(t // pairs < n_hi - 1)
            def _(v=v):
                last_copy(t, v, 1).wait_send()


def scatter_sum(partial, counts, fsdp_too, parts, out_dtype, ident, name):
    n_hi, n_lo, n_x, n_core = counts
    rows, width = partial.shape[4:]
    r = rows // parts
    units = n_hi * parts
    keep = max(n_x, n_lo)
    peers = max(n_x, n_lo, 2) - 1
    b16 = jnp.bfloat16
    own_shape = (2, 2, n_x, n_lo, r, width) if n_core > 1 else (1, 1, 1, 1, 16, 128)
    scratch = [
        pltpu.VMEM(own_shape, b16),
        pltpu.VMEM((units, n_x, n_lo, r, width), b16),
        pltpu.VMEM((units, peers, keep, r, width), b16),
        pltpu.VMEM((units, peers, r, width), b16),
        pltpu.VMEM((max(n_hi - 1, 1), parts, r, width), b16),
        pltpu.SemaphoreType.DMA((2, 2)),
        pltpu.SemaphoreType.DMA((units,)),
        pltpu.SemaphoreType.DMA((units,)),
        pltpu.SemaphoreType.DMA((units, peers)),
        pltpu.SemaphoreType.DMA((units, peers)),
        pltpu.SemaphoreType.DMA((units, peers)),
        pltpu.SemaphoreType.DMA((units, peers)),
        pltpu.SemaphoreType.DMA((units,)),
        pltpu.SemaphoreType.DMA((max(n_hi - 1, 1), parts)),
    ]
    return pl.pallas_call(
        functools.partial(scatter_kernel, counts, parts, fsdp_too),
        in_specs=[pl.BlockSpec(memory_space=pl.ANY)],
        out_specs=pl.BlockSpec(memory_space=pltpu.VMEM),
        out_shape=jax.ShapeDtypeStruct((rows, width), out_dtype),
        scratch_shapes=scratch,
        compiler_params=pltpu.CompilerParams(
            collective_id=ident, has_side_effects=True, vmem_limit_bytes=60 * 2**20
        ),
        cost_estimate=pl.CostEstimate(
            flops=partial.size, bytes_accessed=2 * partial.size, transcendentals=0
        ),
        name=name,
    )(partial)


def gather_kernel(
    counts, parts, fsdp_too, in_ref, out_ref, own_sem, s0, r0, s1, r1, s2, r2, s3, r3
):
    at = Place(counts, fsdp_too)
    n_hi, n_lo, n_x, n_core = counts
    rows = in_ref.shape[0] // parts
    pairs = parts // 2
    steps = n_hi * pairs
    orders = [[d for d in o if at.sizes()[d] > 1] for o in (("lo", "x"), ("x", "lo"))]
    depth = len(orders[0])

    def remote(src, dst, send, recv, dim, ahead):
        return pltpu.make_async_remote_copy(
            src_ref=src, dst_ref=dst, send_sem=send, recv_sem=recv,
            device_id=at.peer(dim, ahead), device_id_type=MESH,
        )

    def span(q):
        return pl.ds(pl.multiple_of(q * rows, 16), rows)

    def hi_copy(q, ahead):
        return remote(
            in_ref.at[span(q)], out_ref.at[at.x, at.core, at.hi, at.lo, span(q)],
            s0.at[ahead - 1, q], r0.at[n_hi - ahead - 1, q], "hi", ahead,
        )

    def where(t, v):
        return (at.hi + n_hi - t // pairs) % n_hi, t % pairs * 2 + v

    def mid_copy(t, v, stage, ahead):
        u = 2 * t + v
        hi, q = where(t, v)
        dim = orders[v][stage]
        size = at.sizes()[dim]
        if stage == 0:
            ref = out_ref.at[at.x, at.core, hi, at.lo, span(q)]
            if_own = in_ref.at[span(q)]
            del if_own
            return remote(
                ref, ref, s1.at[u, ahead - 1], r1.at[u, size - ahead - 1], dim, ahead
            )
        if dim == "x":
            ref = out_ref.at[at.x, at.core, hi, :, span(q)]
        else:
            ref = out_ref.at[:, at.core, hi, at.lo, span(q)]
        return remote(ref, ref, s2.at[u, ahead - 1], r2.at[u, size - ahead - 1], dim, ahead)

    def core_copy(t, v):
        u = 2 * t + v
        hi, q = where(t, v)
        ref = out_ref.at[:, at.core, hi, :, span(q)]
        return remote(ref, ref, s3.at[u], r3.at[u], "core", 1)

    def each_mid(t, v, stage, act):
        size = at.sizes()[orders[v][stage]]
        for ahead in range(1, size):
            act(mid_copy(t, v, stage, ahead))

    keep = pltpu.make_async_copy(
        in_ref, out_ref.at[at.x, at.core, at.hi, at.lo], own_sem
    )
    keep.start()
    at.meet()
    for ahead in range(1, n_hi):
        for q in range(parts):
            hi_copy(q, ahead).start()
    keep.wait()

    @pl.loop(0, steps + depth)
    def _(t):
        @pl.when(t < steps)
        def _():
            for v in range(2):
                _, q = where(t, v)
                for k in range(1, n_hi):

                    @pl.when(t // pairs == k)
                    def _(k=k, q=q):
                        hi_copy(q, k).wait_recv()

                if depth > 0:
                    each_mid(t, v, 0, lambda c: c.start())
                elif n_core > 1:
                    core_copy(t, v).start()

        for stage in range(depth):
            back = stage + 1

            @pl.when((t >= back) & (t < steps + back))
            def _(stage=stage, back=back):
                for v in range(2):
                    each_mid(t - back, v, stage, lambda c: c.wait_recv())
                    if stage + 1 < depth:
                        each_mid(t - back, v, stage + 1, lambda c: c.start())
                    elif n_core > 1:
                        core_copy(t - back, v).start()

    @pl.loop(0, steps)
    def _(t):
        for v in range(2):
            if n_core > 1:
                core_copy(t, v).wait_recv()
                core_copy(t, v).wait_send()
            for stage in range(depth):
                each_mid(t, v, stage, lambda c: c.wait_send())

    for q in range(parts):
        for ahead in range(1, n_hi):
            hi_copy(q, ahead).wait_send()


def gather_rows(own, counts, fsdp_too, parts, ident, name):
    n_hi, n_lo, n_x, n_core = counts
    rows, width = own.shape
    units = n_hi * parts
    peers = max(n_x, n_lo, 2) - 1
    ahead = max(n_hi - 1, 1)
    scratch = [
        pltpu.SemaphoreType.DMA,
        pltpu.SemaphoreType.DMA((ahead, parts)),
        pltpu.SemaphoreType.DMA((ahead, parts)),
        pltpu.SemaphoreType.DMA((units, peers)),
        pltpu.SemaphoreType.DMA((units, peers)),
        pltpu.SemaphoreType.DMA((units, peers)),
        pltpu.SemaphoreType.DMA((units, peers)),
        pltpu.SemaphoreType.DMA((units,)),
        pltpu.SemaphoreType.DMA((units,)),
    ]
    total = rows * n_hi * n_lo * n_x * n_core
    out = pl.pallas_call(
        functools.partial(gather_kernel, counts, parts, fsdp_too),
        in_specs=[pl.BlockSpec(memory_space=pl.ANY)],
        out_specs=pl.BlockSpec(memory_space=pl.ANY),
        out_shape=jax.ShapeDtypeStruct((n_x, n_core, n_hi, n_lo, rows, width), own.dtype),
        scratch_shapes=scratch,
        compiler_params=pltpu.CompilerParams(collective_id=ident, has_side_effects=True),
        cost_estimate=pl.CostEstimate(
            flops=0, bytes_accessed=4 * total * width, transcendentals=0
        ),
        name=name,
    )(own)
    return out.reshape(total, width)


def small_sum_kernel(counts, part_ref, out_ref, first, second, s0, r0, s1, r1):
    sp_count, fs_count = counts
    at = {"sp": lax.axis_index("sp"), "fsdp": lax.axis_index("fsdp")}

    def peer(dim, ahead, size):
        return {dim: (at[dim] + ahead) % size}

    barrier = pltpu.get_barrier_semaphore()
    for dim, size in (("sp", sp_count), ("fsdp", fs_count)):
        for ahead in range(1, size):
            pl.semaphore_signal(
                barrier, inc=1, device_id=peer(dim, ahead, size), device_id_type=MESH
            )
    pl.semaphore_wait(barrier, sp_count + fs_count - 2)

    def exchange(src, held, send, recv, dim, size):
        copies = [
            pltpu.make_async_remote_copy(
                src_ref=src, dst_ref=held.at[size - ahead - 1],
                send_sem=send.at[ahead - 1], recv_sem=recv.at[size - ahead - 1],
                device_id=peer(dim, ahead, size), device_id_type=MESH,
            )
            for ahead in range(1, size)
        ]
        for copy in copies:
            copy.start()
        total = src[...]
        for ahead, copy in enumerate(copies, 1):
            pltpu.make_async_remote_copy(
                src_ref=src, dst_ref=held.at[ahead - 1],
                send_sem=send.at[size - ahead - 1], recv_sem=recv.at[ahead - 1],
                device_id=peer(dim, size - ahead, size), device_id_type=MESH,
            ).wait_recv()
            total = total + held[ahead - 1]
        for copy in copies:
            copy.wait_send()
        return total

    total = exchange(part_ref, first, s0, r0, "sp", sp_count)
    out_ref[...] = total
    if fs_count > 1:
        total = exchange(out_ref, second, s1, r1, "fsdp", fs_count)
        out_ref[...] = total


def small_sum(part, sp_count, fs_count, ident, name):
    sems = [pltpu.SemaphoreType.DMA((max(n - 1, 1),)) for n in (sp_count, sp_count, fs_count, fs_count)]
    return pl.pallas_call(
        functools.partial(small_sum_kernel, (sp_count, fs_count)),
        in_specs=[pl.BlockSpec(memory_space=pltpu.VMEM)],
        out_specs=pl.BlockSpec(memory_space=pltpu.VMEM),
        out_shape=jax.ShapeDtypeStruct(part.shape, jnp.float32),
        scratch_shapes=[
            pltpu.VMEM((max(sp_count - 1, 1),) + part.shape, jnp.float32),
            pltpu.VMEM((max(fs_count - 1, 1),) + part.shape, jnp.float32),
        ]
        + sems,
        compiler_params=pltpu.CompilerParams(collective_id=ident, has_side_effects=True),
        name=name,
    )(part)


ROWS = 256


def window_scores(ends, count, q, k, first, top):
    scores = contract(q, k, 1, 1) * HEAD_DIM ** (-0.5)
    place = top + lax.broadcasted_iota(jnp.int32, (ROWS, 1), 0)
    oldest = jnp.maximum(place - (WINDOW - 1), 0)
    for n in range(count):
        oldest = jnp.maximum(oldest, jnp.where(place >= ends[n], ends[n], 0))
    other = first + lax.broadcasted_iota(jnp.int32, scores.shape, 1)
    return jnp.where((other >= oldest) & (other <= place), scores, masked_score)


def window_first(i, reach, total):
    return pl.multiple_of(jnp.clip(i * ROWS + ROWS - reach, 0, total - reach), ROWS)


def softmax_rows(scores):
    weights = jnp.exp(scores - jnp.max(scores, axis=-1, keepdims=True))
    return weights / jnp.sum(weights, axis=-1, keepdims=True)


def attend_kernel(count, reach, ends, q_ref, k_ref, v_ref, o_ref):
    i = pl.program_id(1)
    first = window_first(i, reach, k_ref.shape[0])
    keys = pl.ds(first, reach)
    scores = window_scores(ends, count, q_ref[...], k_ref[keys, :], first, i * ROWS)
    probs = softmax_rows(scores).astype(jnp.bfloat16)
    o_ref[...] = jnp.dot(probs, v_ref[keys, :], preferred_element_type=jnp.float32).astype(
        jnp.bfloat16
    )


def attend_back_kernel(
    count, reach, ends, q_ref, k_ref, v_ref, g_ref, dq_ref, dk_ref, dv_ref, dk_acc, dv_acc
):
    i = pl.program_id(1)
    first = window_first(i, reach, k_ref.shape[0])
    keys = pl.ds(first, reach)
    scale = HEAD_DIM ** (-0.5)

    @pl.when(i == 0)
    def _():
        dk_acc[...] = jnp.zeros_like(dk_acc)
        dv_acc[...] = jnp.zeros_like(dv_acc)

    q = q_ref[...]
    k = k_ref[keys, :]
    grad = g_ref[...]
    probs = softmax_rows(window_scores(ends, count, q, k, first, i * ROWS))
    prob_grad = contract(grad, v_ref[keys, :], 1, 1)
    delta = jnp.sum(probs * prob_grad, axis=-1, keepdims=True)
    score_grad = (probs * (prob_grad - delta)).astype(jnp.bfloat16)
    dq_ref[...] = (
        jnp.dot(score_grad, k, preferred_element_type=jnp.float32) * scale
    ).astype(jnp.bfloat16)
    dk_acc[keys, :] += contract(score_grad, q, 0, 0) * scale
    dv_acc[keys, :] += contract(probs.astype(jnp.bfloat16), grad, 0, 0)

    @pl.when(i == pl.num_programs(1) - 1)
    def _():
        dk_ref[...] = dk_acc[...].astype(jnp.bfloat16)
        dv_ref[...] = dv_acc[...].astype(jnp.bfloat16)


def attend(query, key, value, lengths):
    seq_rows, span = query.shape
    heads = span // HEAD_DIM
    reach = min(WINDOW + ROWS, seq_rows)
    count = lengths.shape[0]
    ends = jnp.cumsum(lengths)
    tile = pl.BlockSpec((ROWS, HEAD_DIM), lambda h, i, ends: (i, h))
    whole = pl.BlockSpec((seq_rows, HEAD_DIM), lambda h, i, ends: (0, h))
    shape = jax.ShapeDtypeStruct((seq_rows, span), jnp.bfloat16)
    pairs = seq_rows * heads * reach

    def call(kernel, ins, outs, scratch, name):
        return pl.pallas_call(
            kernel,
            grid_spec=pltpu.PrefetchScalarGridSpec(
                num_scalar_prefetch=1,
                grid=(heads, seq_rows // ROWS),
                in_specs=ins,
                out_specs=outs,
                scratch_shapes=scratch,
            ),
            out_shape=[shape] * len(outs),
            compiler_params=pltpu.CompilerParams(
                dimension_semantics=("arbitrary", "arbitrary"), vmem_limit_bytes=48 * 2**20
            ),
            cost_estimate=pl.CostEstimate(
                flops=4 * len(outs) * pairs * HEAD_DIM,
                bytes_accessed=8 * seq_rows * span,
                transcendentals=pairs,
            ),
            name=name,
        )

    attended = call(
        functools.partial(attend_kernel, count, reach), [tile, whole, whole], [tile], [], "attend"
    )(ends, query, key, value)[0]

    def back(grad):
        return call(
            functools.partial(attend_back_kernel, count, reach),
            [tile, whole, whole, tile],
            [tile, whole, whole],
            [pltpu.VMEM((seq_rows, HEAD_DIM), jnp.float32)] * 2,
            "attend_back",
        )(ends, query, key, value, grad)

    return attended, back


def scatter_over_all(partial, rows, sp_count, fs_count, ident, name):
    counts = mesh_counts(sp_count, fs_count)
    width = partial.shape[1]
    parts = 4 if rows % 64 == 0 else 2
    if 1.4 * partial.size * 2 > 52 * 2**20 or rows % (parts * 16):
        part = lax.psum_scatter(partial, "fsdp", scatter_dimension=0, tiled=True)
        return lax.psum_scatter(part, "sp", scatter_dimension=0, tiled=True).astype(jnp.float32)
    n_hi, n_lo, n_x, n_core = counts
    shaped = partial.reshape(n_x, n_core, n_hi, n_lo, rows, width)
    return scatter_sum(shaped, counts, True, parts, jnp.float32, ident, name)


def scatter_over_sp(partial, rows, sp_count, ident, name):
    n_hi, n_lo, _, _ = mesh_counts(sp_count, 1)
    parts = 4 if rows % 64 == 0 else 2
    shaped = partial.reshape(1, 1, n_hi, n_lo, rows, partial.shape[1])
    return scatter_sum(shaped, (n_hi, n_lo, 1, 1), False, parts, jnp.float32, ident, name)


def gather_over_all(own, sp_count, fs_count, ident, name):
    parts = 4 if own.shape[0] % 64 == 0 else 2
    return gather_rows(own, mesh_counts(sp_count, fs_count), True, parts, ident, name)


def gather_over_sp(own, sp_count, ident, name):
    n_hi, n_lo, _, _ = mesh_counts(sp_count, 1)
    parts = 4 if own.shape[0] % 64 == 0 else 2
    return gather_rows(own, (n_hi, n_lo, 1, 1), False, parts, ident, name)


def sum_over_sp(rows, sp_count, ident, name):
    part = jnp.stack(rows)
    return small_sum(part.reshape(-1, 128), sp_count, 1, ident, name).reshape(part.shape)


def local(
    tokens,
    doc_lengths,
    expert_ids,
    norm_attn,
    norm_query,
    norm_key,
    norm_ffn,
    w_query,
    w_key,
    w_value,
    w_out,
    w_router,
    w_gate,
    w_up,
    w_down,
    cotangent,
):
    sp_count = lax.axis_size("sp")
    fs_count = lax.axis_size("fsdp")
    my_sp = lax.axis_index("sp")
    my_fs = lax.axis_index("fsdp")
    hidden_in = tokens[0].astype(jnp.float32)
    tok_rows, width = hidden_in.shape
    head_local = HEADS // sp_count
    seq_rows = tok_rows * sp_count
    span = head_local * HEAD_DIM
    expert_local = EXPERTS // sp_count
    first_expert = my_sp * expert_local
    gains = lax.all_gather(
        jnp.stack([norm_attn, norm_query, norm_key, norm_ffn]), "fsdp", axis=1, tiled=True
    ).astype(jnp.float32)
    gain_attn, gain_ffn = gains[0], gains[3]
    own_cols = lax.dynamic_slice_in_dim(gains, my_sp * span, span, axis=1)
    gain_query, gain_key = own_cols[1], own_cols[2]
    qkv_own = jnp.concatenate(
        [
            lax.dynamic_slice_in_dim(w, my_sp * span, span, axis=1)
            for w in (w_query, w_key, w_value)
        ],
        axis=1,
    )
    qkv_mat = lax.all_gather(qkv_own, "fsdp", axis=0, tiled=True)
    out_mat = lax.all_gather(w_out, "fsdp", axis=0, tiled=True)
    router_mat = lax.all_gather(w_router, "fsdp", axis=0, tiled=True)
    cot_all = lax.all_gather(cotangent[0], ("fsdp", "sp"), axis=0, tiled=True)
    routing = route_plan(expert_ids[0], sp_count, fs_count)
    cot_rows, _ = dispatch_rows(cot_all, routing, None)

    attn_normed, attn_pull = jax.vjp(rms_scale, hidden_in, gain_attn)
    attn_in = gather_over_sp(attn_normed.astype(jnp.bfloat16), sp_count, 1, "gather_attn_in")
    qkv_raw = jnp.dot(attn_in, qkv_mat, preferred_element_type=jnp.float32)
    raw = (qkv_raw[:, :span], qkv_raw[:, span : 2 * span])
    value_heads = qkv_raw[:, 2 * span :].astype(jnp.bfloat16)
    squares = sum_over_sp([jnp.sum(r * r, axis=-1) for r in raw], sp_count, 7, "sum_squares")
    scales = lax.rsqrt(squares / width + eps)[:, :, None]
    cosine, sine = rope_tables(jnp.arange(seq_rows, dtype=jnp.int32), HEAD_DIM)

    def turned(normed):
        return rotate_pairs(
            normed.reshape(seq_rows, head_local, HEAD_DIM), cosine, sine
        ).reshape(seq_rows, span)

    query_heads = turned(raw[0] * scales[0] * gain_query).astype(jnp.bfloat16)
    key_heads = turned(raw[1] * scales[1] * gain_key).astype(jnp.bfloat16)
    attended_heads, attend_back = attend(query_heads, key_heads, value_heads, doc_lengths[0])
    attended_tok = lax.all_to_all(
        attended_heads, "sp", split_axis=0, concat_axis=1, tiled=True
    )
    after_attn = hidden_in + jnp.dot(attended_tok, out_mat, preferred_element_type=jnp.float32)
    ffn_normed, ffn_pull = jax.vjp(rms_scale, after_attn, gain_ffn)
    ffn_in = ffn_normed.astype(jnp.bfloat16)
    logits = jnp.dot(ffn_in, router_mat, preferred_element_type=jnp.float32)
    router = jax.nn.softmax(logits, axis=-1)
    ffn_all = gather_over_all(ffn_in, sp_count, fs_count, 2, "gather_ffn_in")
    router_all = jax.nn.softmax(
        jnp.dot(ffn_all, router_mat, preferred_element_type=jnp.float32), axis=-1
    )
    gate_rows = (
        lax.dynamic_slice_in_dim(router_all, first_expert, expert_local, axis=1)
        .reshape(-1, BLOCK, expert_local)
        .transpose(0, 2, 1)
    )
    ffn_rows, gate_slots = dispatch_rows(ffn_all, routing, gate_rows)
    out_rows, in_grad_rows, grad_gate, grad_up, grad_down = run_experts(
        ffn_rows, cot_rows, gate_slots, w_gate, w_up, w_down, routing[3], first_expert[None]
    )
    in_grad_sum = scatter_over_all(
        combine_rows(in_grad_rows, routing, "combine_grads"),
        tok_rows, sp_count, fs_count, 3, "scatter_grads",
    )
    moe_sum = scatter_over_all(
        combine_rows(out_rows, routing, "combine_outputs"),
        tok_rows, sp_count, fs_count, 4, "scatter_outputs",
    )
    mixed = (after_attn + moe_sum).astype(jnp.bfloat16)
    upstream = cotangent[0].astype(jnp.float32)
    ffn_in_grad = in_grad_sum[:, :width]
    router_grad = in_grad_sum[:, width : width + EXPERTS]
    logit_grad = (
        router * (router_grad - jnp.sum(router * router_grad, axis=-1, keepdims=True))
    ).astype(jnp.bfloat16)
    ffn_in_grad = ffn_in_grad + jnp.dot(
        logit_grad, router_mat.T, preferred_element_type=jnp.float32
    )
    router_term = jnp.dot(ffn_in.T, logit_grad, preferred_element_type=jnp.float32)
    ffn_hidden_grad, ffn_gain_term = ffn_pull(ffn_in_grad)
    after_grad = upstream + ffn_hidden_grad
    attn_out_grad = after_grad.astype(jnp.bfloat16)
    attended_grad = jnp.dot(attn_out_grad, out_mat.T, preferred_element_type=jnp.float32).astype(
        jnp.bfloat16
    )
    attended_grad_heads = lax.all_to_all(
        attended_grad, "sp", split_axis=1, concat_axis=0, tiled=True
    )
    out_term = jnp.dot(attended_tok.T, attn_out_grad, preferred_element_type=jnp.float32)
    row_terms = jnp.concatenate(
        [
            out_term.astype(jnp.bfloat16),
            router_term.astype(jnp.bfloat16),
            jnp.zeros((width, 128 - EXPERTS), jnp.bfloat16),
        ],
        axis=1,
    )
    row_sums = scatter_over_all(
        row_terms, width // (sp_count * fs_count), sp_count, fs_count, 5, "scatter_out_rows"
    )
    query_grad_heads, key_grad_heads, value_low = attend_back(attended_grad_heads)

    def unturned(grad):
        shaped = grad.astype(jnp.float32).reshape(seq_rows, head_local, HEAD_DIM)
        return rotate_pairs(shaped, cosine, -sine).reshape(seq_rows, span)

    normed_grads = (unturned(query_grad_heads), unturned(key_grad_heads))
    scaled_grads = (normed_grads[0] * gain_query, normed_grads[1] * gain_key)
    products = sum_over_sp(
        [jnp.sum(g * r, axis=-1) for g, r in zip(scaled_grads, raw)], sp_count, 8, "sum_products"
    )[:, :, None]
    gain_terms = [
        jnp.sum(g * r * s, axis=0) for g, r, s in zip(normed_grads, raw, scales)
    ]
    raw_grads = [
        (g * s - r * (s * s * s) * (p / width)).astype(jnp.bfloat16)
        for g, r, s, p in zip(scaled_grads, raw, scales, products)
    ]
    qkv_low = jnp.concatenate(raw_grads + [value_low], axis=1)
    attn_partial = lax.dot_general(
        qkv_low, qkv_mat, (((1,), (1,)), ((), ())), preferred_element_type=jnp.float32
    ).astype(jnp.bfloat16)
    attn_in_grad = scatter_over_sp(attn_partial, tok_rows, sp_count, 6, "scatter_attn_in")
    qkv_term = jnp.dot(attn_in.T, qkv_low, preferred_element_type=jnp.float32)
    attn_hidden_grad, attn_gain_term = attn_pull(attn_in_grad)
    grad_tokens = after_grad + attn_hidden_grad
    qkv_sums = lax.psum_scatter(
        qkv_term.astype(jnp.bfloat16), "fsdp", scatter_dimension=0, tiled=True
    )
    qkv_every = lax.all_gather(qkv_sums, "sp", axis=0)
    rows_every = lax.all_gather(row_sums.astype(jnp.bfloat16), "sp", axis=0, tiled=True)
    dense = [
        qkv_every[:, :, k * span : (k + 1) * span]
        .transpose(1, 0, 2)
        .reshape(-1, width)
        .astype(jnp.float32)
        for k in range(3)
    ]
    placed = [
        lax.dynamic_update_slice_in_dim(jnp.zeros((width,), jnp.float32), g, my_sp * span, 0)
        for g in gain_terms
    ]
    gain_sums = small_sum(
        jnp.stack([attn_gain_term, placed[0], placed[1], ffn_gain_term]).reshape(-1, 128),
        sp_count, fs_count, 9, "sum_gains",
    ).reshape(4, width)
    gain_sums = lax.dynamic_slice_in_dim(
        gain_sums, my_fs * (width // fs_count), width // fs_count, axis=1
    )
    return (
        mixed[None],
        grad_tokens[None],
        gain_sums[0],
        gain_sums[1],
        gain_sums[2],
        gain_sums[3],
        dense[0],
        dense[1],
        dense[2],
        rows_every[:, :width].astype(jnp.float32),
        rows_every[:, width : width + EXPERTS].astype(jnp.float32),
        grad_gate,
        grad_up,
        grad_down,
    )


def solution(mesh):
    in_specs = (
        P("fsdp", "sp", None),
        P("fsdp", None),
        P("fsdp", "sp", None),
        P("fsdp"),
        P("fsdp"),
        P("fsdp"),
        P("fsdp"),
        P("fsdp", None),
        P("fsdp", None),
        P("fsdp", None),
        P("fsdp", None),
        P("fsdp", None),
        P("sp", None, "fsdp"),
        P("sp", None, "fsdp"),
        P("sp", None, "fsdp"),
        P("fsdp", "sp", None),
    )
    out_specs = (
        P("fsdp", "sp", None),
        P("fsdp", "sp", None),
        P("fsdp"),
        P("fsdp"),
        P("fsdp"),
        P("fsdp"),
        P("fsdp", None),
        P("fsdp", None),
        P("fsdp", None),
        P("fsdp", None),
        P("fsdp", None),
        P("sp", None, "fsdp"),
        P("sp", None, "fsdp"),
        P("sp", None, "fsdp"),
    )
    return jax.shard_map(local, mesh=mesh, in_specs=in_specs, out_specs=out_specs, check_vma=False)
```

```python
import functools

import jax
import jax.numpy as jnp
from jax import lax
from jax.experimental import pallas as pl
from jax.experimental.pallas import tpu as pltpu
from jax.sharding import PartitionSpec as P

HEADS = 16
HEAD_DIM = 128
EXPERTS = 64
TOPK = 8
WINDOW = 1024


eps = 1e-05
rope_base = 10000.0
masked_score = -1e30


def rms_scale(values, gain_vec):
    return values * lax.rsqrt(jnp.mean(values * values, axis=-1, keepdims=True) + eps) * gain_vec


def rotate_pairs(values, cosine, sine):
    half_dim = values.shape[-1] // 2
    turned = jnp.concatenate([-values[..., half_dim:], values[..., :half_dim]], axis=-1)
    return values * cosine + turned * sine


def rope_tables(positions, head_size):
    inv_freq = rope_base ** (-jnp.arange(0, head_size, 2, dtype=jnp.float32) / head_size)
    phase_half = positions.astype(jnp.float32)[:, None] * inv_freq[None, :]
    phase_all = jnp.concatenate([phase_half, phase_half], axis=-1)
    return (jnp.cos(phase_all)[:, None, :], jnp.sin(phase_all)[:, None, :])


TILE = 256
LANES = 128


def route_plan(own_ids, sp_count, fs_count):
    local_experts = EXPERTS // sp_count
    block = own_ids.shape[0]
    per_device = own_ids.size
    packed = jnp.zeros((32, LANES), jnp.bfloat16)
    packed = packed.at[: per_device // LANES].set(own_ids.astype(jnp.bfloat16).reshape(-1, LANES))
    packed = gather_over_all(packed, sp_count, fs_count, 10, "gather_ids")
    ids = packed.reshape(-1, 32 * LANES)[:, :per_device].reshape(-1, TOPK).astype(jnp.int32)
    blocks = ids.shape[0] // block
    capacity = 5 * ids.shape[0] * TOPK // (4 * EXPERTS)
    first = lax.axis_index("sp") * local_experts
    mine = first + jnp.arange(local_experts, dtype=jnp.int32)
    named = jnp.any(ids[:, None, :] == mine[None, :, None], axis=-1)
    named = named.reshape(blocks, block, local_experts)
    upto = (jnp.arange(block)[:, None] >= jnp.arange(block)[None, :]).astype(jnp.bfloat16)
    running = jnp.einsum(
        "ts,bse->bte", upto, named.astype(jnp.bfloat16), preferred_element_type=jnp.float32
    ).astype(jnp.int32)
    before = (jnp.arange(blocks)[:, None] > jnp.arange(blocks)[None, :]).astype(jnp.float32)
    earlier = jnp.dot(
        before, running[:, -1].astype(jnp.float32), precision=lax.Precision.HIGHEST
    ).astype(jnp.int32)
    keep = named & (earlier[:, None, :] + running - 1 < capacity)
    rank = jnp.where(keep, running - 1, -1).transpose(0, 2, 1)
    slots = 2 * block * TOPK // EXPERTS
    some = jnp.any(keep, axis=1).reshape(-1, TILE // slots, local_experts)
    live = jnp.any(some, axis=1).astype(jnp.int32).T.reshape(-1)
    return rank, live


def pick_matrix(rank, slots):
    experts, block = rank.shape
    slot = lax.broadcasted_iota(jnp.int32, (slots, block), 0)
    return jnp.concatenate(
        [(slot == rank[e : e + 1, :]).astype(jnp.bfloat16) for e in range(experts)], axis=0
    )


def column_spans(width):
    return [(done, min(512, width - done)) for done in range(0, width, 512)]


def contract(left, right, left_dim, right_dim):
    return lax.dot_general(
        left, right, (((left_dim,), (right_dim,)), ((), ())), preferred_element_type=jnp.float32
    )


def expert_kernel(
    live, first, x_ref, c_ref, gate_ref, up_ref, down_ref, dx_ref, y_ref, gg_ref, gu_ref,
    gd_ref, acc_g, acc_u, acc_d,
):
    e = pl.program_id(0)
    t = pl.program_id(1)
    width = c_ref.shape[2]

    @pl.when(t == 0)
    def _():
        acc_g[...] = jnp.zeros_like(acc_g)
        acc_u[...] = jnp.zeros_like(acc_u)
        acc_d[...] = jnp.zeros_like(acc_d)

    @pl.when(live[e * pl.num_programs(1) + t] == 0)
    def _():
        dx_ref[...] = jnp.zeros_like(dx_ref)
        y_ref[...] = jnp.zeros_like(y_ref)

    @pl.when(live[e * pl.num_programs(1) + t] > 0)
    def _():
        x = x_ref[0, :, 0:width]
        c = c_ref[0]
        gate_mat = gate_ref[0]
        up_mat = up_ref[0]
        down_mat = down_ref[0]
        column = lax.broadcasted_iota(jnp.int32, (TILE, LANES), 1)
        mine = lax.rem(column, EXPERTS) == first[0] + e
        gates = jnp.where(mine, x_ref[0, :, width : width + LANES].astype(jnp.float32), 0.0)
        weight = jnp.sum(gates, axis=1, keepdims=True)
        gate_pre = jnp.dot(x, gate_mat, preferred_element_type=jnp.float32)
        up_pre = jnp.dot(x, up_mat, preferred_element_type=jnp.float32)
        up_act = jnp.dot(c, down_mat, preferred_element_type=jnp.float32)
        sig = 1.0 / (1.0 + jnp.exp(-gate_pre))
        silu = gate_pre * sig
        act = silu * up_pre
        gate_grad = jnp.sum(up_act * act, axis=1, keepdims=True)
        act_low = (act * weight).astype(jnp.bfloat16)
        act_grad = up_act * weight
        dgate = (act_grad * up_pre * sig * (1.0 + gate_pre * (1.0 - sig))).astype(jnp.bfloat16)
        dup = (act_grad * silu).astype(jnp.bfloat16)
        y_ref[0] = contract(act_low, down_mat, 1, 1).astype(jnp.bfloat16)
        dx_ref[0, :, 0:width] = (
            contract(dgate, gate_mat, 1, 1) + contract(dup, up_mat, 1, 1)
        ).astype(jnp.bfloat16)
        dx_ref[0, :, width : width + LANES] = jnp.where(
            column == first[0] + e, gate_grad, 0.0
        ).astype(jnp.bfloat16)
        acc_g[...] += contract(dgate, x, 0, 0)
        acc_u[...] += contract(dup, x, 0, 0)
        acc_d[...] += contract(act_low, c, 0, 0)

    @pl.when(t == pl.num_programs(1) - 1)
    def _():
        gg_ref[0] = acc_g[...].T
        gu_ref[0] = acc_u[...].T
        gd_ref[0] = acc_d[...].T


def run_experts(x_rows, c_rows, w_gate, w_up, w_down, live, first):
    experts, rows, width = c_rows.shape
    hidden = w_gate.shape[2]

    def tile_map(e, t, live, first):
        return (e, t, 0)

    mat = pl.BlockSpec((1, width, hidden), lambda e, t, live, first: (e, 0, 0))
    wide = pl.BlockSpec((1, TILE, width + LANES), tile_map)
    plain = pl.BlockSpec((1, TILE, width), tile_map)
    return pl.pallas_call(
        expert_kernel,
        grid_spec=pltpu.PrefetchScalarGridSpec(
            num_scalar_prefetch=2,
            grid=(experts, rows // TILE),
            in_specs=[wide, plain, mat, mat, mat],
            out_specs=[wide, plain, mat, mat, mat],
            scratch_shapes=[pltpu.VMEM((hidden, width), jnp.float32)] * 3,
        ),
        out_shape=[
            jax.ShapeDtypeStruct(x_rows.shape, jnp.bfloat16),
            jax.ShapeDtypeStruct(c_rows.shape, jnp.bfloat16),
        ]
        + [jax.ShapeDtypeStruct((experts, width, hidden), jnp.float32)] * 3,
        input_output_aliases={2: 0, 3: 1},
        compiler_params=pltpu.CompilerParams(
            dimension_semantics=("arbitrary", "arbitrary"), vmem_limit_bytes=60 * 2**20
        ),
        cost_estimate=pl.CostEstimate(
            flops=18 * experts * rows * width * hidden,
            bytes_accessed=8 * experts * rows * width,
            transcendentals=experts * rows * hidden,
        ),
        name="experts",
    )(live, first, x_rows, c_rows, w_gate, w_up, w_down)


MESH = pl.DeviceIdType.MESH


class Place:
    def __init__(self, counts, fsdp_too):
        self.n_hi, self.n_lo, self.n_x, self.n_core = counts
        sp = lax.axis_index("sp")
        self.hi, self.lo = sp // self.n_lo, sp % self.n_lo
        if fsdp_too:
            fs = lax.axis_index("fsdp")
            self.x, self.core = fs // self.n_core, fs % self.n_core
        else:
            self.x, self.core = 0, 0

    def peer(self, dim, ahead):
        if dim == "core":
            return {"fsdp": self.x * self.n_core + (self.core + ahead) % self.n_core}
        if dim == "x":
            return {"fsdp": (self.x + ahead) % self.n_x * self.n_core + self.core}
        if dim == "lo":
            return {"sp": self.hi * self.n_lo + (self.lo + ahead) % self.n_lo}
        return {"sp": (self.hi + ahead) % self.n_hi * self.n_lo + self.lo}

    def sizes(self):
        return {"core": self.n_core, "x": self.n_x, "lo": self.n_lo, "hi": self.n_hi}

    def meet(self):
        barrier = pltpu.get_barrier_semaphore()
        met = 0
        for dim, size in self.sizes().items():
            for ahead in range(1, size):
                pl.semaphore_signal(
                    barrier, inc=1, device_id=self.peer(dim, ahead), device_id_type=MESH
                )
                met += 1
        pl.semaphore_wait(barrier, met)


def mesh_counts(sp_count, fs_count):
    low = 2
    while low * low < sp_count // 2:
        low *= 2
    low = min(low, sp_count)
    core = 2 if fs_count % 2 == 0 else 1
    return sp_count // low, low, fs_count // core, core


def scatter_kernel(
    counts, parts, fsdp_too, part_ref, out_ref, own, buf, first, second, third, own_sem, s0, r0,
    s1, r1, s2, r2, s3, r3, host=None,
):
    at = Place(counts, fsdp_too)
    n_hi, n_lo, n_x, n_core = counts
    rows = out_ref.shape[0] // parts
    pairs = parts // 2
    steps = n_hi * pairs
    lag = 1
    orders = [[d for d in o if at.sizes()[d] > 1] for o in (("x", "lo"), ("lo", "x"))]

    def remote(src, dst, send, recv, dim, ahead):
        return pltpu.make_async_remote_copy(
            src_ref=src, dst_ref=dst, send_sem=send, recv_sem=recv,
            device_id=at.peer(dim, ahead), device_id_type=MESH,
        )

    def where(t, v):
        return (at.hi + 1 + t // pairs) % n_hi, t % pairs * 2 + v

    def mine(t, v, core):
        hi, q = where(t, v)
        cut = pl.ds(pl.multiple_of(q * rows, 16), rows)
        if host is not None:
            return host.part.at[t // pairs % 2, :, core, :, cut, :]
        return part_ref.at[:, core, hi, :, cut, :]

    def load_own(t, v):
        place = own.at[t % 2, v] if n_core > 1 else buf.at[2 * t + v]
        return pltpu.make_async_copy(mine(t, v, at.core), place, own_sem.at[t % 2, v])

    def core_copy(t, v):
        return remote(
            mine(t, v, (at.core + 1) % 2), buf.at[2 * t + v], s0.at[2 * t + v], r0.at[2 * t + v],
            "core", 1,
        )

    def mid_copy(t, v, stage, ahead):
        u = 2 * t + v
        dim = orders[v][stage]
        size = at.sizes()[dim]
        to = ((at.x if dim == "x" else at.lo) + ahead) % size
        if stage == 0:
            src = buf.at[u, to] if dim == "x" else buf.at[u, :, to]
            dst = first.at[u, size - ahead - 1, pl.ds(0, n_lo if dim == "x" else n_x)]
            return remote(
                src, dst, s1.at[u, ahead - 1], r1.at[u, size - ahead - 1], dim, ahead
            )
        return remote(
            first.at[u, 0, to], second.at[u, size - ahead - 1],
            s2.at[u, ahead - 1], r2.at[u, size - ahead - 1], dim, ahead,
        )

    def wait_in(t, v, stage):
        size = at.sizes()[orders[v][stage]]
        for ahead in range(1, size):
            mid_copy(t, v, stage, ahead).wait_recv()

    def start_out(t, v, stage):
        size = at.sizes()[orders[v][stage]]
        for ahead in range(1, size):
            mid_copy(t, v, stage, ahead).start()

    def wide(ref):
        return ref[...].astype(jnp.float32)

    def result(t, v):
        u = 2 * t + v
        if len(orders[v]) == 2:
            return second.at[u, 0]
        if len(orders[v]) == 1:
            return first.at[u, 0, 0]
        return buf.at[u, 0, 0]

    def last_copy(t, v, ahead):
        _, q = where(t, v)
        return remote(
            result(t, v), third.at[n_hi - ahead - 1, q],
            s3.at[2 * t + v], r3.at[n_hi - ahead - 1, q], "hi", ahead,
        )

    def send_last(t, v):
        for k in range(n_hi - 1):

            @pl.when(t // pairs == k)
            def _(k=k):
                last_copy(t, v, k + 1).start()

    def stage_core(t, v):
        u = 2 * t + v
        if host is None:
            load_own(t, v).wait()
            own_part = own.at[t % 2, v]
        else:
            own_part = mine(t, v, at.core)
        if n_core > 1:
            core_copy(t, v).wait_recv()

            @pl.loop(0, n_x * n_lo)
            def _(j):
                x, lo = j // n_lo, j % n_lo
                place = buf.at[u, x, lo]
                place[...] = (wide(place) + wide(own_part.at[x, lo])).astype(jnp.bfloat16)

        if orders[v]:
            start_out(t, v, 0)
        else:
            send_last(t, v)

    def stage_mid(t, v, stage):
        u = 2 * t + v
        wait_in(t, v, stage)
        dim = orders[v][stage]
        size = at.sizes()[dim]
        if stage == 0:
            keep = n_lo if dim == "x" else n_x

            @pl.loop(0, keep)
            def _(j):
                base = buf.at[u, at.x, j] if dim == "x" else buf.at[u, j, at.lo]
                total = wide(base)
                for s in range(size - 1):
                    total = total + wide(first.at[u, s, j])
                first.at[u, 0, j][...] = total.astype(jnp.bfloat16)

        else:
            base = first.at[u, 0, at.x if dim == "x" else at.lo]
            total = wide(base)
            for s in range(size - 1):
                total = total + wide(second.at[u, s])
            second.at[u, 0][...] = total.astype(jnp.bfloat16)
        if stage + 1 < len(orders[v]):
            start_out(t, v, stage + 1)
        else:
            send_last(t, v)

    def each_core_copy(group, act):
        @pl.loop(0, pairs)
        def _(g):
            for v in range(2):
                act(core_copy(group * pairs + g, v))

    def make_group(group, piece, pieces):
        host.run(at, (at.hi + 1 + group) % n_hi, group % 2, piece, pieces)

    at.meet()
    if host is not None:
        make_group(0, 0, 1)
        each_core_copy(0, lambda c: c.start())
    else:
        if n_core > 1:

            @pl.loop(0, n_hi)
            def _(group):
                each_core_copy(group, lambda c: c.start())

        for v in range(2):
            load_own(0, v).start()

    depth = len(orders[0])

    @pl.loop(0, steps + depth * lag)
    def _(t):
        if host is None:

            @pl.when(t + 1 < steps)
            def _():
                for v in range(2):
                    load_own(t + 1, v).start()

        @pl.when(t < steps)
        def _():
            for v in range(2):
                stage_core(t, v)

        for stage in range(depth):
            back = (stage + 1) * lag

            @pl.when((t >= back) & (t < steps + back))
            def _(stage=stage, back=back):
                for v in range(2):
                    stage_mid(t - back, v, stage)

        if host is not None:

            @pl.when(t + pairs < steps)
            def _():
                group = t // pairs + 1

                @pl.when((t % pairs == 0) & (group >= 2))
                def _():
                    each_core_copy(group - 2, lambda c: c.wait_send())

                make_group(group, t % pairs, pairs)

                @pl.when(t % pairs == pairs - 1)
                def _():
                    each_core_copy(group, lambda c: c.start())

    for g in range(pairs):
        t = (n_hi - 1) * pairs + g
        for v in range(2):
            q = g * 2 + v
            total = wide(result(t, v))
            for s in range(n_hi - 1):
                last_copy(g, v, n_hi - 1 - s).wait_recv()
                total = total + wide(third.at[s, q])
            out_ref[pl.ds(q * rows, rows), :] = total.astype(out_ref.dtype)

    @pl.loop(0, steps)
    def _(t):
        for v in range(2):
            if host is None and n_core > 1:
                core_copy(t, v).wait_send()
            for stage in range(depth):
                for ahead in range(1, at.sizes()[orders[v][stage]]):
                    mid_copy(t, v, stage, ahead).wait_send()

            @pl.when(t // pairs < n_hi - 1)
            def _(v=v):
                last_copy(t, v, 1).wait_send()

    if host is not None:
        for group in range(max(n_hi - 2, 0), n_hi):
            each_core_copy(group, lambda c: c.wait_send())


class Combine:
    def __init__(self, rows_ref, rank_ref, part, held, sems, counts):
        self.rows_ref, self.rank_ref, self.part, self.held, self.sems = (
            rows_ref, rank_ref, part, held, sems,
        )
        self.n_hi, self.n_lo, self.n_x, self.n_core = counts

    def run(self, at, hi, slot, piece, pieces):
        total = self.n_x * self.n_core * self.n_lo
        count = total // pieces
        _, experts, slots, width = self.held.shape

        def spot(j):
            j = piece * count + j
            return j // (self.n_core * self.n_lo), j // self.n_lo % self.n_core, j % self.n_lo

        def block(j):
            x, core, lo = spot(j)
            return ((x * self.n_core + core) * self.n_hi + hi) * self.n_lo + lo

        def load(j, place):
            return pltpu.make_async_copy(
                self.rows_ref.at[:, block(j)], self.held.at[place], self.sems.at[place]
            )

        load(0, 0).start()

        @pl.loop(0, count)
        def _(j):
            place = j % 2

            @pl.when(j + 1 < count)
            def _():
                load(j + 1, 1 - place).start()

            load(j, place).wait()
            pick = pick_matrix(self.rank_ref[block(j)], slots)
            x, core, lo = spot(j)
            for start, size in column_spans(width):
                cols = pl.ds(start, size)
                found = self.held[place, :, :, cols].reshape(experts * slots, size)
                self.part[slot, x, core, lo, :, cols] = contract(pick, found, 0, 0).astype(
                    jnp.bfloat16
                )


def combine_scatter_kernel(
    counts, parts, rows_ref, rank_ref, out_ref, part, held, held_sem, *scratch
):
    host = Combine(rows_ref, rank_ref, part, held, held_sem, counts)
    scatter_kernel(counts, parts, True, None, out_ref, None, *scratch, host=host)


def scatter_scratch(counts, parts, r, width):
    n_hi, n_lo, n_x, _ = counts
    units = n_hi * parts
    keep = max(n_x, n_lo)
    peers = max(n_x, n_lo, 2) - 1
    b16 = jnp.bfloat16
    return [
        pltpu.VMEM((units, n_x, n_lo, r, width), b16),
        pltpu.VMEM((units, peers, keep, r, width), b16),
        pltpu.VMEM((units, peers, r, width), b16),
        pltpu.VMEM((max(n_hi - 1, 1), parts, r, width), b16),
        pltpu.SemaphoreType.DMA((2, 2)),
        pltpu.SemaphoreType.DMA((units,)),
        pltpu.SemaphoreType.DMA((units,)),
        pltpu.SemaphoreType.DMA((units, peers)),
        pltpu.SemaphoreType.DMA((units, peers)),
        pltpu.SemaphoreType.DMA((units, peers)),
        pltpu.SemaphoreType.DMA((units, peers)),
        pltpu.SemaphoreType.DMA((units,)),
        pltpu.SemaphoreType.DMA((max(n_hi - 1, 1), parts)),
    ]


def scatter_bytes(counts, parts, rows, width):
    n_hi, n_lo, n_x, _ = counts
    keep = max(n_x, n_lo)
    peers = max(n_x, n_lo, 2) - 1
    held = n_hi * (n_x * n_lo + peers * keep + peers) + max(n_hi - 1, 1)
    return (2 * held + 4) * rows * width


VMEM_ROOM = 58 * 2**20


def combine_sum(rows, rank, counts, parts, slots, ident, name):
    blocks, experts, block = rank.shape
    width = rows.shape[-1]
    _, n_lo, n_x, n_core = counts
    b16 = jnp.bfloat16
    return pl.pallas_call(
        functools.partial(combine_scatter_kernel, counts, parts),
        in_specs=[pl.BlockSpec(memory_space=pl.ANY), pl.BlockSpec(memory_space=pltpu.VMEM)],
        out_specs=pl.BlockSpec(memory_space=pltpu.VMEM),
        out_shape=jax.ShapeDtypeStruct((block, width), jnp.float32),
        scratch_shapes=[
            pltpu.VMEM((2, n_x, n_core, n_lo, block, width), b16),
            pltpu.VMEM((2, experts, slots, width), b16),
            pltpu.SemaphoreType.DMA((2,)),
        ]
        + scatter_scratch(counts, parts, block // parts, width),
        compiler_params=pltpu.CompilerParams(
            collective_id=ident, has_side_effects=True, vmem_limit_bytes=62 * 2**20
        ),
        cost_estimate=pl.CostEstimate(
            flops=2 * blocks * experts * slots * block * width,
            bytes_accessed=4 * blocks * block * width,
            transcendentals=0,
        ),
        name=name,
    )(rows.reshape(experts, blocks, slots, width), rank)


def scatter_sum(partial, counts, fsdp_too, parts, out_dtype, ident, name):
    _, n_lo, n_x, n_core = counts
    rows, width = partial.shape[4:]
    r = rows // parts
    own_shape = (2, 2, n_x, n_lo, r, width) if n_core > 1 else (1, 1, 1, 1, 16, 128)
    scratch = [pltpu.VMEM(own_shape, jnp.bfloat16)] + scatter_scratch(counts, parts, r, width)
    return pl.pallas_call(
        functools.partial(scatter_kernel, counts, parts, fsdp_too),
        in_specs=[pl.BlockSpec(memory_space=pl.ANY)],
        out_specs=pl.BlockSpec(memory_space=pltpu.VMEM),
        out_shape=jax.ShapeDtypeStruct((rows, width), out_dtype),
        scratch_shapes=scratch,
        compiler_params=pltpu.CompilerParams(
            collective_id=ident, has_side_effects=True, vmem_limit_bytes=60 * 2**20
        ),
        cost_estimate=pl.CostEstimate(
            flops=partial.size, bytes_accessed=2 * partial.size, transcendentals=0
        ),
        name=name,
    )(partial)


def gather_kernel(
    counts, parts, fsdp_too, in_ref, out_ref, own_sem, s0, r0, s1, r1, s2, r2, s3, r3, host=None
):
    at = Place(counts, fsdp_too)
    n_hi, n_lo, n_x, n_core = counts
    rows = in_ref.shape[0] // parts
    pairs = parts // 2
    steps = n_hi * pairs
    orders = [[d for d in o if at.sizes()[d] > 1] for o in (("lo", "x"), ("x", "lo"))]
    depth = len(orders[0])

    def remote(src, dst, send, recv, dim, ahead):
        return pltpu.make_async_remote_copy(
            src_ref=src, dst_ref=dst, send_sem=send, recv_sem=recv,
            device_id=at.peer(dim, ahead), device_id_type=MESH,
        )

    def span(q):
        return pl.ds(pl.multiple_of(q * rows, 16), rows)

    def hi_copy(q, ahead):
        return remote(
            in_ref.at[span(q)], out_ref.at[at.x, at.core, at.hi, at.lo, span(q)],
            s0.at[ahead - 1, q], r0.at[n_hi - ahead - 1, q], "hi", ahead,
        )

    def where(t, v):
        return (at.hi + n_hi - t // pairs) % n_hi, t % pairs * 2 + v

    def mid_copy(t, v, stage, ahead):
        u = 2 * t + v
        hi, q = where(t, v)
        dim = orders[v][stage]
        size = at.sizes()[dim]
        if stage == 0:
            ref = out_ref.at[at.x, at.core, hi, at.lo, span(q)]
            if_own = in_ref.at[span(q)]
            del if_own
            return remote(
                ref, ref, s1.at[u, ahead - 1], r1.at[u, size - ahead - 1], dim, ahead
            )
        if dim == "x":
            ref = out_ref.at[at.x, at.core, hi, :, span(q)]
        else:
            ref = out_ref.at[:, at.core, hi, at.lo, span(q)]
        return remote(ref, ref, s2.at[u, ahead - 1], r2.at[u, size - ahead - 1], dim, ahead)

    def core_copy(t, v):
        u = 2 * t + v
        hi, q = where(t, v)
        ref = out_ref.at[:, at.core, hi, :, span(q)]
        return remote(ref, ref, s3.at[u], r3.at[u], "core", 1)

    def each_mid(t, v, stage, act):
        size = at.sizes()[orders[v][stage]]
        for ahead in range(1, size):
            act(mid_copy(t, v, stage, ahead))

    keep = pltpu.make_async_copy(
        in_ref, out_ref.at[at.x, at.core, at.hi, at.lo], own_sem
    )
    keep.start()
    at.meet()
    for ahead in range(1, n_hi):
        for q in range(parts):
            hi_copy(q, ahead).start()
    keep.wait()

    @pl.loop(0, steps + depth + (1 if host is not None and n_core > 1 else 0))
    def _(t):
        @pl.when(t < steps)
        def _():
            for v in range(2):
                _, q = where(t, v)
                for k in range(1, n_hi):

                    @pl.when(t // pairs == k)
                    def _(k=k, q=q):
                        hi_copy(q, k).wait_recv()

                if depth > 0:
                    each_mid(t, v, 0, lambda c: c.start())
                elif n_core > 1:
                    core_copy(t, v).start()

        for stage in range(depth):
            back = stage + 1

            @pl.when((t >= back) & (t < steps + back))
            def _(stage=stage, back=back):
                for v in range(2):
                    each_mid(t - back, v, stage, lambda c: c.wait_recv())
                    if stage + 1 < depth:
                        each_mid(t - back, v, stage + 1, lambda c: c.start())
                    elif n_core > 1:
                        core_copy(t - back, v).start()

        if host is not None:
            for origin_step in range(n_hi):
                done = (origin_step + 1) * pairs - 1 + depth
                hi = (at.hi + n_hi - origin_step) % n_hi

                @pl.when(t == done)
                def _(hi=hi):
                    host.blocks(at, at.core, hi)

                if n_core > 1:

                    @pl.when(t == done + 1)
                    def _(hi=hi, origin_step=origin_step):
                        for g in range(pairs):
                            for v in range(2):
                                core_copy(origin_step * pairs + g, v).wait_recv()
                        host.blocks(at, 1 - at.core, hi)

            host.others(t, steps + depth)

    @pl.loop(0, steps)
    def _(t):
        for v in range(2):
            if n_core > 1:
                if host is None:
                    core_copy(t, v).wait_recv()
                core_copy(t, v).wait_send()
            for stage in range(depth):
                each_mid(t, v, stage, lambda c: c.wait_send())

    for q in range(parts):
        for ahead in range(1, n_hi):
            hi_copy(q, ahead).wait_send()


class Dispatch:
    def __init__(self, tables, rows, bufs, ins, outs, rank_ref, geometry):
        self.tables, self.rows, self.bufs, self.ins, self.outs = tables, rows, bufs, ins, outs
        self.rank_ref = rank_ref
        self.n_hi, self.n_lo, self.n_x, self.n_core = geometry

    def load(self, which, place, index, slot):
        held, _ = self.bufs[which]
        return pltpu.make_async_copy(
            self.tables[which].at[index], held.at[slot], self.ins[which].at[slot]
        )

    def store(self, which, block, slot):
        _, found = self.bufs[which]
        return pltpu.make_async_copy(
            found.at[slot], self.rows[which].at[:, block], self.outs[which].at[slot]
        )

    def run(self, which, block_of, index_of, count):
        held, found = self.bufs[which]
        experts, slots, width = found.shape[1:]
        self.load(which, None, index_of(0), 0).start()

        @pl.loop(0, count)
        def _(j):
            slot = j % 2

            @pl.when(j + 1 < count)
            def _():
                self.load(which, None, index_of(j + 1), 1 - slot).start()

            @pl.when(j >= 2)
            def _():
                self.store(which, block_of(j - 2), slot).wait()

            self.load(which, None, index_of(j), slot).wait()
            pick = pick_matrix(self.rank_ref[block_of(j)], slots)
            for start, size in column_spans(width):
                cols = pl.ds(start, size)
                picked = jnp.dot(
                    pick, held[slot, :, cols], preferred_element_type=jnp.float32
                ).astype(jnp.bfloat16)
                found[slot, :, :, cols] = picked.reshape(experts, slots, size)
            self.store(which, block_of(j), slot).start()

        for j in range(max(count - 2, 0), count):
            self.store(which, block_of(j), j % 2).wait()

    def blocks(self, at, core, hi):
        def spot(j):
            return j // self.n_lo, core, hi, j % self.n_lo

        def block_of(j):
            x, c, h, lo = spot(j)
            return ((x * self.n_core + c) * self.n_hi + h) * self.n_lo + lo

        self.run(0, block_of, spot, self.n_x * self.n_lo)

    def others(self, t, steps):
        total = self.n_x * self.n_core * self.n_hi * self.n_lo
        each = -(-total // steps)
        for step in range(steps):
            first = min(step * each, total)
            count = min(each, total - first)
            if count > 0:

                @pl.when(t == step)
                def _(first=first, count=count):
                    self.run(1, lambda j: first + j, lambda j: first + j, count)


def dispatch_kernel(
    counts, parts, in_ref, other_ref, rank_ref, out_ref, rows_ref, other_rows_ref, held, found,
    other_held, other_found, in_sem, put_sem, other_in_sem, other_put_sem, *sems,
):
    host = Dispatch(
        (out_ref, other_ref), (rows_ref, other_rows_ref),
        ((held, found), (other_held, other_found)), (in_sem, other_in_sem),
        (put_sem, other_put_sem), rank_ref, counts,
    )
    gather_kernel(counts, parts, True, in_ref, out_ref, *sems, host=host)


def gather_sems(counts, parts):
    n_hi, n_lo, n_x, n_core = counts
    units = n_hi * parts
    peers = max(n_x, n_lo, 2) - 1
    ahead = max(n_hi - 1, 1)
    sizes = [(ahead, parts)] * 2 + [(units, peers)] * 4 + [(units,)] * 2
    return [pltpu.SemaphoreType.DMA] + [pltpu.SemaphoreType.DMA(size) for size in sizes]


def gather_and_dispatch(own, other_all, rank, slots, sp_count, fs_count, ident, name):
    counts = mesh_counts(sp_count, fs_count)
    n_hi, n_lo, n_x, n_core = counts
    rows, width = own.shape
    other_width = other_all.shape[1]
    blocks, experts, _ = rank.shape
    parts = 4 if rows % 64 == 0 else 2
    b16 = jnp.bfloat16
    anywhere = pl.BlockSpec(memory_space=pl.ANY)
    scratch = [
        pltpu.VMEM((2, rows, width), b16),
        pltpu.VMEM((2, experts, slots, width), b16),
        pltpu.VMEM((2, rows, other_width), b16),
        pltpu.VMEM((2, experts, slots, other_width), b16),
    ] + [pltpu.SemaphoreType.DMA((2,))] * 4
    flops = 2 * blocks * experts * slots * rows * (width + other_width)
    _, picked, other_picked = pl.pallas_call(
        functools.partial(dispatch_kernel, counts, parts),
        in_specs=[anywhere, anywhere, pl.BlockSpec(memory_space=pltpu.VMEM)],
        out_specs=[anywhere] * 3,
        out_shape=[
            jax.ShapeDtypeStruct((n_x, n_core, n_hi, n_lo, rows, width), b16),
            jax.ShapeDtypeStruct((experts, blocks, slots, width), b16),
            jax.ShapeDtypeStruct((experts, blocks, slots, other_width), b16),
        ],
        scratch_shapes=scratch + gather_sems(counts, parts),
        compiler_params=pltpu.CompilerParams(
            collective_id=ident, has_side_effects=True, vmem_limit_bytes=48 * 2**20
        ),
        cost_estimate=pl.CostEstimate(
            flops=flops, bytes_accessed=8 * blocks * rows * width, transcendentals=0
        ),
        name=name,
    )(own, other_all.reshape(blocks, rows, other_width), rank)
    return picked.reshape(experts, -1, width), other_picked.reshape(experts, -1, other_width)


def gather_rows(own, counts, fsdp_too, parts, ident, name):
    n_hi, n_lo, n_x, n_core = counts
    rows, width = own.shape
    total = rows * n_hi * n_lo * n_x * n_core
    out = pl.pallas_call(
        functools.partial(gather_kernel, counts, parts, fsdp_too),
        in_specs=[pl.BlockSpec(memory_space=pl.ANY)],
        out_specs=pl.BlockSpec(memory_space=pl.ANY),
        out_shape=jax.ShapeDtypeStruct((n_x, n_core, n_hi, n_lo, rows, width), own.dtype),
        scratch_shapes=gather_sems(counts, parts),
        compiler_params=pltpu.CompilerParams(collective_id=ident, has_side_effects=True),
        cost_estimate=pl.CostEstimate(
            flops=0, bytes_accessed=4 * total * width, transcendentals=0
        ),
        name=name,
    )(own)
    return out.reshape(total, width)


def small_sum_kernel(counts, part_ref, out_ref, first, second, s0, r0, s1, r1):
    sp_count, fs_count = counts
    at = {"sp": lax.axis_index("sp"), "fsdp": lax.axis_index("fsdp")}

    def peer(dim, ahead, size):
        return {dim: (at[dim] + ahead) % size}

    barrier = pltpu.get_barrier_semaphore()
    for dim, size in (("sp", sp_count), ("fsdp", fs_count)):
        for ahead in range(1, size):
            pl.semaphore_signal(
                barrier, inc=1, device_id=peer(dim, ahead, size), device_id_type=MESH
            )
    pl.semaphore_wait(barrier, sp_count + fs_count - 2)

    def exchange(src, held, send, recv, dim, size):
        copies = [
            pltpu.make_async_remote_copy(
                src_ref=src, dst_ref=held.at[size - ahead - 1],
                send_sem=send.at[ahead - 1], recv_sem=recv.at[size - ahead - 1],
                device_id=peer(dim, ahead, size), device_id_type=MESH,
            )
            for ahead in range(1, size)
        ]
        for copy in copies:
            copy.start()
        total = src[...]
        for ahead, copy in enumerate(copies, 1):
            pltpu.make_async_remote_copy(
                src_ref=src, dst_ref=held.at[ahead - 1],
                send_sem=send.at[size - ahead - 1], recv_sem=recv.at[ahead - 1],
                device_id=peer(dim, size - ahead, size), device_id_type=MESH,
            ).wait_recv()
            total = total + held[ahead - 1]
        for copy in copies:
            copy.wait_send()
        return total

    total = exchange(part_ref, first, s0, r0, "sp", sp_count)
    out_ref[...] = total
    if fs_count > 1:
        total = exchange(out_ref, second, s1, r1, "fsdp", fs_count)
        out_ref[...] = total


def small_sum(part, sp_count, fs_count, ident, name):
    sems = [pltpu.SemaphoreType.DMA((max(n - 1, 1),)) for n in (sp_count, sp_count, fs_count, fs_count)]
    return pl.pallas_call(
        functools.partial(small_sum_kernel, (sp_count, fs_count)),
        in_specs=[pl.BlockSpec(memory_space=pltpu.VMEM)],
        out_specs=pl.BlockSpec(memory_space=pltpu.VMEM),
        out_shape=jax.ShapeDtypeStruct(part.shape, jnp.float32),
        scratch_shapes=[
            pltpu.VMEM((max(sp_count - 1, 1),) + part.shape, jnp.float32),
            pltpu.VMEM((max(fs_count - 1, 1),) + part.shape, jnp.float32),
        ]
        + sems,
        compiler_params=pltpu.CompilerParams(collective_id=ident, has_side_effects=True),
        name=name,
    )(part)


ROWS = 256


def window_scores(ends, count, q, k, first, top):
    scores = contract(q, k, 1, 1) * HEAD_DIM ** (-0.5)
    place = top + lax.broadcasted_iota(jnp.int32, (ROWS, 1), 0)
    oldest = jnp.maximum(place - (WINDOW - 1), 0)
    for n in range(count):
        oldest = jnp.maximum(oldest, jnp.where(place >= ends[n], ends[n], 0))
    other = first + lax.broadcasted_iota(jnp.int32, scores.shape, 1)
    return jnp.where((other >= oldest) & (other <= place), scores, masked_score)


def window_first(i, reach, total):
    return pl.multiple_of(jnp.clip(i * ROWS + ROWS - reach, 0, total - reach), ROWS)


def softmax_rows(scores):
    weights = jnp.exp(scores - jnp.max(scores, axis=-1, keepdims=True))
    return weights / jnp.sum(weights, axis=-1, keepdims=True)


def attend_kernel(count, reach, ends, q_ref, k_ref, v_ref, o_ref):
    i = pl.program_id(1)
    first = window_first(i, reach, k_ref.shape[0])
    keys = pl.ds(first, reach)
    scores = window_scores(ends, count, q_ref[...], k_ref[keys, :], first, i * ROWS)
    probs = softmax_rows(scores).astype(jnp.bfloat16)
    o_ref[...] = jnp.dot(probs, v_ref[keys, :], preferred_element_type=jnp.float32).astype(
        jnp.bfloat16
    )


def attend_back_kernel(
    count, reach, ends, q_ref, k_ref, v_ref, g_ref, dq_ref, dk_ref, dv_ref, dk_acc, dv_acc
):
    i = pl.program_id(1)
    first = window_first(i, reach, k_ref.shape[0])
    keys = pl.ds(first, reach)
    scale = HEAD_DIM ** (-0.5)

    @pl.when(i == 0)
    def _():
        dk_acc[...] = jnp.zeros_like(dk_acc)
        dv_acc[...] = jnp.zeros_like(dv_acc)

    q = q_ref[...]
    k = k_ref[keys, :]
    grad = g_ref[...]
    probs = softmax_rows(window_scores(ends, count, q, k, first, i * ROWS))
    prob_grad = contract(grad, v_ref[keys, :], 1, 1)
    delta = jnp.sum(probs * prob_grad, axis=-1, keepdims=True)
    score_grad = (probs * (prob_grad - delta)).astype(jnp.bfloat16)
    dq_ref[...] = (
        jnp.dot(score_grad, k, preferred_element_type=jnp.float32) * scale
    ).astype(jnp.bfloat16)
    dk_acc[keys, :] += contract(score_grad, q, 0, 0) * scale
    dv_acc[keys, :] += contract(probs.astype(jnp.bfloat16), grad, 0, 0)

    @pl.when(i == pl.num_programs(1) - 1)
    def _():
        dk_ref[...] = dk_acc[...].astype(jnp.bfloat16)
        dv_ref[...] = dv_acc[...].astype(jnp.bfloat16)


def attend(query, key, value, lengths):
    seq_rows, span = query.shape
    heads = span // HEAD_DIM
    reach = min(WINDOW + ROWS, seq_rows)
    count = lengths.shape[0]
    ends = jnp.cumsum(lengths)
    tile = pl.BlockSpec((ROWS, HEAD_DIM), lambda h, i, ends: (i, h))
    whole = pl.BlockSpec((seq_rows, HEAD_DIM), lambda h, i, ends: (0, h))
    shape = jax.ShapeDtypeStruct((seq_rows, span), jnp.bfloat16)
    pairs = seq_rows * heads * reach

    def call(kernel, ins, outs, scratch, name):
        return pl.pallas_call(
            kernel,
            grid_spec=pltpu.PrefetchScalarGridSpec(
                num_scalar_prefetch=1,
                grid=(heads, seq_rows // ROWS),
                in_specs=ins,
                out_specs=outs,
                scratch_shapes=scratch,
            ),
            out_shape=[shape] * len(outs),
            compiler_params=pltpu.CompilerParams(
                dimension_semantics=("arbitrary", "arbitrary"), vmem_limit_bytes=48 * 2**20
            ),
            cost_estimate=pl.CostEstimate(
                flops=4 * len(outs) * pairs * HEAD_DIM,
                bytes_accessed=8 * seq_rows * span,
                transcendentals=pairs,
            ),
            name=name,
        )

    attended = call(
        functools.partial(attend_kernel, count, reach), [tile, whole, whole], [tile], [], "attend"
    )(ends, query, key, value)[0]

    def back(grad):
        return call(
            functools.partial(attend_back_kernel, count, reach),
            [tile, whole, whole, tile],
            [tile, whole, whole],
            [pltpu.VMEM((seq_rows, HEAD_DIM), jnp.float32)] * 2,
            "attend_back",
        )(ends, query, key, value, grad)

    return attended, back


def scatter_over_all(partial, rows, sp_count, fs_count, ident, name):
    counts = mesh_counts(sp_count, fs_count)
    width = partial.shape[1]
    parts = 4 if rows % 64 == 0 else 2
    room = scatter_bytes(counts, parts, rows, width)
    room += 8 * counts[1] * counts[2] * rows // parts * width
    if room > VMEM_ROOM or rows % (parts * 16):
        part = lax.psum_scatter(partial, "fsdp", scatter_dimension=0, tiled=True)
        return lax.psum_scatter(part, "sp", scatter_dimension=0, tiled=True).astype(jnp.float32)
    n_hi, n_lo, n_x, n_core = counts
    shaped = partial.reshape(n_x, n_core, n_hi, n_lo, rows, width)
    return scatter_sum(shaped, counts, True, parts, jnp.float32, ident, name)


def combine_and_scatter(rows, rank, slots, sp_count, fs_count, ident, name):
    blocks, experts, block = rank.shape
    counts = mesh_counts(sp_count, fs_count)
    n_hi, n_lo, n_x, n_core = counts
    width = rows.shape[-1]
    parts = 4 if block % 64 == 0 else 2
    room = scatter_bytes(counts, parts, block, width)
    room += 4 * (n_x * n_core * n_lo * block + experts * slots) * width
    if n_core == 2 and room <= VMEM_ROOM and block % (parts * 16) == 0:
        return combine_sum(rows, rank, counts, parts, slots, ident, name)
    shaped = rows.reshape(experts, blocks, slots, -1)
    pick = (rank[:, :, None, :] == jnp.arange(slots)[None, None, :, None]).astype(jnp.bfloat16)
    partial = jnp.einsum("best,ebsw->btw", pick, shaped, preferred_element_type=jnp.float32)
    partial = partial.astype(jnp.bfloat16).reshape(blocks * block, -1)
    return scatter_over_all(partial, block, sp_count, fs_count, ident, name)


def scatter_over_sp(partial, rows, sp_count, ident, name):
    n_hi, n_lo, _, _ = mesh_counts(sp_count, 1)
    parts = 4 if rows % 64 == 0 else 2
    shaped = partial.reshape(1, 1, n_hi, n_lo, rows, partial.shape[1])
    return scatter_sum(shaped, (n_hi, n_lo, 1, 1), False, parts, jnp.float32, ident, name)


def gather_over_all(own, sp_count, fs_count, ident, name):
    parts = 4 if own.shape[0] % 64 == 0 else 2
    return gather_rows(own, mesh_counts(sp_count, fs_count), True, parts, ident, name)


def gather_over_sp(own, sp_count, ident, name):
    n_hi, n_lo, _, _ = mesh_counts(sp_count, 1)
    parts = 4 if own.shape[0] % 64 == 0 else 2
    return gather_rows(own, (n_hi, n_lo, 1, 1), False, parts, ident, name)


def sum_over_sp(rows, sp_count, ident, name):
    part = jnp.stack(rows)
    return small_sum(part.reshape(-1, 128), sp_count, 1, ident, name).reshape(part.shape)


def local(
    tokens,
    doc_lengths,
    expert_ids,
    norm_attn,
    norm_query,
    norm_key,
    norm_ffn,
    w_query,
    w_key,
    w_value,
    w_out,
    w_router,
    w_gate,
    w_up,
    w_down,
    cotangent,
):
    sp_count = lax.axis_size("sp")
    fs_count = lax.axis_size("fsdp")
    my_sp = lax.axis_index("sp")
    my_fs = lax.axis_index("fsdp")
    hidden_in = tokens[0].astype(jnp.float32)
    tok_rows, width = hidden_in.shape
    head_local = HEADS // sp_count
    seq_rows = tok_rows * sp_count
    span = head_local * HEAD_DIM
    expert_local = EXPERTS // sp_count
    first_expert = my_sp * expert_local
    gains = lax.all_gather(
        jnp.stack([norm_attn, norm_query, norm_key, norm_ffn]), "fsdp", axis=1, tiled=True
    ).astype(jnp.float32)
    gain_attn, gain_ffn = gains[0], gains[3]
    own_cols = lax.dynamic_slice_in_dim(gains, my_sp * span, span, axis=1)
    gain_query, gain_key = own_cols[1], own_cols[2]
    qkv_own = jnp.concatenate(
        [
            lax.dynamic_slice_in_dim(w, my_sp * span, span, axis=1)
            for w in (w_query, w_key, w_value)
        ],
        axis=1,
    )
    qkv_mat = lax.all_gather(qkv_own, "fsdp", axis=0, tiled=True)
    out_mat = lax.all_gather(w_out, "fsdp", axis=0, tiled=True)
    router_mat = lax.all_gather(w_router, "fsdp", axis=0, tiled=True)
    cot_all = lax.all_gather(cotangent[0], ("fsdp", "sp"), axis=0, tiled=True)
    rank, live = route_plan(expert_ids[0], sp_count, fs_count)
    slots = 2 * tok_rows * TOPK // EXPERTS

    attn_normed, attn_pull = jax.vjp(rms_scale, hidden_in, gain_attn)
    attn_in = gather_over_sp(attn_normed.astype(jnp.bfloat16), sp_count, 1, "gather_attn_in")
    qkv_raw = jnp.dot(attn_in, qkv_mat, preferred_element_type=jnp.float32)
    raw = (qkv_raw[:, :span], qkv_raw[:, span : 2 * span])
    value_heads = qkv_raw[:, 2 * span :].astype(jnp.bfloat16)
    squares = sum_over_sp([jnp.sum(r * r, axis=-1) for r in raw], sp_count, 7, "sum_squares")
    scales = lax.rsqrt(squares / width + eps)[:, :, None]
    cosine, sine = rope_tables(jnp.arange(seq_rows, dtype=jnp.int32), HEAD_DIM)

    def turned(normed):
        return rotate_pairs(
            normed.reshape(seq_rows, head_local, HEAD_DIM), cosine, sine
        ).reshape(seq_rows, span)

    query_heads = turned(raw[0] * scales[0] * gain_query).astype(jnp.bfloat16)
    key_heads = turned(raw[1] * scales[1] * gain_key).astype(jnp.bfloat16)
    attended_heads, attend_back = attend(query_heads, key_heads, value_heads, doc_lengths[0])
    attended_tok = lax.all_to_all(
        attended_heads, "sp", split_axis=0, concat_axis=1, tiled=True
    )
    after_attn = hidden_in + jnp.dot(attended_tok, out_mat, preferred_element_type=jnp.float32)
    ffn_normed, ffn_pull = jax.vjp(rms_scale, after_attn, gain_ffn)
    ffn_in = ffn_normed.astype(jnp.bfloat16)
    logits = jnp.dot(ffn_in, router_mat, preferred_element_type=jnp.float32)
    router = jax.nn.softmax(logits, axis=-1)
    router_high = router.astype(jnp.bfloat16)
    router_low = (router - router_high.astype(jnp.float32)).astype(jnp.bfloat16)
    ffn_rows, cot_rows = gather_and_dispatch(
        jnp.concatenate([ffn_in, router_high, router_low], axis=1),
        cot_all, rank, slots, sp_count, fs_count, 2, "gather_ffn_in",
    )
    in_grad_rows, out_rows, grad_gate, grad_up, grad_down = run_experts(
        ffn_rows, cot_rows, w_gate, w_up, w_down, live, first_expert[None]
    )
    in_grad_sum = combine_and_scatter(
        in_grad_rows, rank, slots, sp_count, fs_count, 3, "scatter_grads"
    )
    moe_sum = combine_and_scatter(out_rows, rank, slots, sp_count, fs_count, 4, "scatter_outputs")
    mixed = (after_attn + moe_sum).astype(jnp.bfloat16)
    upstream = cotangent[0].astype(jnp.float32)
    ffn_in_grad = in_grad_sum[:, :width]
    router_grad = in_grad_sum[:, width : width + EXPERTS]
    logit_grad = (
        router * (router_grad - jnp.sum(router * router_grad, axis=-1, keepdims=True))
    ).astype(jnp.bfloat16)
    ffn_in_grad = ffn_in_grad + jnp.dot(
        logit_grad, router_mat.T, preferred_element_type=jnp.float32
    )
    router_term = jnp.dot(ffn_in.T, logit_grad, preferred_element_type=jnp.float32)
    ffn_hidden_grad, ffn_gain_term = ffn_pull(ffn_in_grad)
    after_grad = upstream + ffn_hidden_grad
    attn_out_grad = after_grad.astype(jnp.bfloat16)
    attended_grad = jnp.dot(attn_out_grad, out_mat.T, preferred_element_type=jnp.float32).astype(
        jnp.bfloat16
    )
    attended_grad_heads = lax.all_to_all(
        attended_grad, "sp", split_axis=1, concat_axis=0, tiled=True
    )
    out_term = jnp.dot(attended_tok.T, attn_out_grad, preferred_element_type=jnp.float32)
    row_terms = jnp.concatenate(
        [
            out_term.astype(jnp.bfloat16),
            router_term.astype(jnp.bfloat16),
            jnp.zeros((width, 128 - EXPERTS), jnp.bfloat16),
        ],
        axis=1,
    )
    row_sums = scatter_over_all(
        row_terms, width // (sp_count * fs_count), sp_count, fs_count, 5, "scatter_out_rows"
    )
    query_grad_heads, key_grad_heads, value_low = attend_back(attended_grad_heads)

    def unturned(grad):
        shaped = grad.astype(jnp.float32).reshape(seq_rows, head_local, HEAD_DIM)
        return rotate_pairs(shaped, cosine, -sine).reshape(seq_rows, span)

    normed_grads = (unturned(query_grad_heads), unturned(key_grad_heads))
    scaled_grads = (normed_grads[0] * gain_query, normed_grads[1] * gain_key)
    products = sum_over_sp(
        [jnp.sum(g * r, axis=-1) for g, r in zip(scaled_grads, raw)], sp_count, 8, "sum_products"
    )[:, :, None]
    gain_terms = [
        jnp.sum(g * r * s, axis=0) for g, r, s in zip(normed_grads, raw, scales)
    ]
    raw_grads = [
        (g * s - r * (s * s * s) * (p / width)).astype(jnp.bfloat16)
        for g, r, s, p in zip(scaled_grads, raw, scales, products)
    ]
    qkv_low = jnp.concatenate(raw_grads + [value_low], axis=1)
    attn_partial = lax.dot_general(
        qkv_low, qkv_mat, (((1,), (1,)), ((), ())), preferred_element_type=jnp.float32
    ).astype(jnp.bfloat16)
    attn_in_grad = scatter_over_sp(attn_partial, tok_rows, sp_count, 6, "scatter_attn_in")
    qkv_term = jnp.dot(attn_in.T, qkv_low, preferred_element_type=jnp.float32)
    attn_hidden_grad, attn_gain_term = attn_pull(attn_in_grad)
    grad_tokens = after_grad + attn_hidden_grad
    qkv_sums = lax.psum_scatter(
        qkv_term.astype(jnp.bfloat16), "fsdp", scatter_dimension=0, tiled=True
    )
    qkv_every = lax.all_gather(qkv_sums, "sp", axis=0)
    rows_every = lax.all_gather(row_sums.astype(jnp.bfloat16), "sp", axis=0, tiled=True)
    dense = [
        qkv_every[:, :, k * span : (k + 1) * span]
        .transpose(1, 0, 2)
        .reshape(-1, width)
        .astype(jnp.float32)
        for k in range(3)
    ]
    placed = [
        lax.dynamic_update_slice_in_dim(jnp.zeros((width,), jnp.float32), g, my_sp * span, 0)
        for g in gain_terms
    ]
    gain_sums = small_sum(
        jnp.stack([attn_gain_term, placed[0], placed[1], ffn_gain_term]).reshape(-1, 128),
        sp_count, fs_count, 9, "sum_gains",
    ).reshape(4, width)
    gain_sums = lax.dynamic_slice_in_dim(
        gain_sums, my_fs * (width // fs_count), width // fs_count, axis=1
    )
    return (
        mixed[None],
        grad_tokens[None],
        gain_sums[0],
        gain_sums[1],
        gain_sums[2],
        gain_sums[3],
        dense[0],
        dense[1],
        dense[2],
        rows_every[:, :width].astype(jnp.float32),
        rows_every[:, width : width + EXPERTS].astype(jnp.float32),
        grad_gate,
        grad_up,
        grad_down,
    )


def solution(mesh):
    in_specs = (
        P("fsdp", "sp", None),
        P("fsdp", None),
        P("fsdp", "sp", None),
        P("fsdp"),
        P("fsdp"),
        P("fsdp"),
        P("fsdp"),
        P("fsdp", None),
        P("fsdp", None),
        P("fsdp", None),
        P("fsdp", None),
        P("fsdp", None),
        P("sp", None, "fsdp"),
        P("sp", None, "fsdp"),
        P("sp", None, "fsdp"),
        P("fsdp", "sp", None),
    )
    out_specs = (
        P("fsdp", "sp", None),
        P("fsdp", "sp", None),
        P("fsdp"),
        P("fsdp"),
        P("fsdp"),
        P("fsdp"),
        P("fsdp", None),
        P("fsdp", None),
        P("fsdp", None),
        P("fsdp", None),
        P("fsdp", None),
        P("sp", None, "fsdp"),
        P("sp", None, "fsdp"),
        P("sp", None, "fsdp"),
    )
    return jax.shard_map(local, mesh=mesh, in_specs=in_specs, out_specs=out_specs, check_vma=False)
```

```python
import functools

import jax
import jax.numpy as jnp
from jax import lax
from jax.experimental import pallas as pl
from jax.experimental.pallas import tpu as pltpu
from jax.sharding import PartitionSpec as P

HEADS = 16
HEAD_DIM = 128
EXPERTS = 64
TOPK = 8
WINDOW = 1024


eps = 1e-05
rope_base = 10000.0
masked_score = -1e30


def rms_scale(values, gain_vec):
    return values * lax.rsqrt(jnp.mean(values * values, axis=-1, keepdims=True) + eps) * gain_vec


def rotate_pairs(values, cosine, sine):
    half_dim = values.shape[-1] // 2
    turned = jnp.concatenate([-values[..., half_dim:], values[..., :half_dim]], axis=-1)
    return values * cosine + turned * sine


def rope_tables(positions, head_size):
    inv_freq = rope_base ** (-jnp.arange(0, head_size, 2, dtype=jnp.float32) / head_size)
    phase_half = positions.astype(jnp.float32)[:, None] * inv_freq[None, :]
    phase_all = jnp.concatenate([phase_half, phase_half], axis=-1)
    return (jnp.cos(phase_all)[:, None, :], jnp.sin(phase_all)[:, None, :])


TILE = 1024
LANES = 128


def route_plan(ids, block, sp_count):
    local_experts = EXPERTS // sp_count
    blocks = ids.shape[0] // block
    capacity = 5 * ids.shape[0] * TOPK // (4 * EXPERTS)
    first = lax.axis_index("sp") * local_experts
    mine = first + jnp.arange(local_experts, dtype=jnp.int32)
    named = jnp.any(ids[:, None, :] == mine[None, :, None], axis=-1)
    named = named.reshape(blocks, block, local_experts)
    upto = (jnp.arange(block)[:, None] >= jnp.arange(block)[None, :]).astype(jnp.bfloat16)
    running = jnp.einsum(
        "ts,bse->bte", upto, named.astype(jnp.bfloat16), preferred_element_type=jnp.float32
    ).astype(jnp.int32)
    before = (jnp.arange(blocks)[:, None] > jnp.arange(blocks)[None, :]).astype(jnp.float32)
    earlier = jnp.dot(
        before, running[:, -1].astype(jnp.float32), precision=lax.Precision.HIGHEST
    ).astype(jnp.int32)
    keep = named & (earlier[:, None, :] + running - 1 < capacity)
    rank = jnp.where(keep, running - 1, -1).transpose(0, 2, 1)
    slots = 2 * block * TOPK // EXPERTS
    some = jnp.any(keep, axis=1).reshape(-1, TILE // slots, local_experts)
    live = jnp.any(some, axis=1).astype(jnp.int32).T.reshape(-1)
    return rank, live


def pick_matrix(rank, slots):
    experts, block = rank.shape
    slot = lax.broadcasted_iota(jnp.int32, (slots, block), 0)
    return jnp.concatenate(
        [(slot == rank[e : e + 1, :]).astype(jnp.bfloat16) for e in range(experts)], axis=0
    )


def column_spans(width):
    return [(done, min(512, width - done)) for done in range(0, width, 512)]


def contract(left, right, left_dim, right_dim):
    return lax.dot_general(
        left, right, (((left_dim,), (right_dim,)), ((), ())), preferred_element_type=jnp.float32
    )


def expert_kernel(
    live, first, x_ref, c_ref, gate_ref, up_ref, down_ref, dx_ref, y_ref, dgate_ref, dup_ref,
    act_ref,
):
    e = pl.program_id(0)
    t = pl.program_id(1)
    width = c_ref.shape[2]

    @pl.when(live[e * pl.num_programs(1) + t] == 0)
    def _():
        for ref in (dx_ref, y_ref, dgate_ref, dup_ref, act_ref):
            ref[...] = jnp.zeros_like(ref)

    @pl.when(live[e * pl.num_programs(1) + t] > 0)
    def _():
        x = x_ref[0, :, 0:width]
        gate_mat = gate_ref[0]
        up_mat = up_ref[0]
        down_mat = down_ref[0]
        column = lax.broadcasted_iota(jnp.int32, (TILE, LANES), 1)
        mine = lax.rem(column, EXPERTS) == first[0] + e
        gates = jnp.where(mine, x_ref[0, :, width : width + LANES].astype(jnp.float32), 0.0)
        weight = jnp.sum(gates, axis=1, keepdims=True)
        gate_pre = jnp.dot(x, gate_mat, preferred_element_type=jnp.float32)
        up_pre = jnp.dot(x, up_mat, preferred_element_type=jnp.float32)
        up_act = jnp.dot(c_ref[0], down_mat, preferred_element_type=jnp.float32)
        sig = 1.0 / (1.0 + jnp.exp(-gate_pre))
        silu = gate_pre * sig
        act = silu * up_pre
        gate_grad = jnp.sum(up_act * act, axis=1, keepdims=True)
        act_low = (act * weight).astype(jnp.bfloat16)
        act_grad = up_act * weight
        dgate = (act_grad * up_pre * sig * (1.0 + gate_pre * (1.0 - sig))).astype(jnp.bfloat16)
        dup = (act_grad * silu).astype(jnp.bfloat16)
        act_ref[0] = act_low
        dgate_ref[0] = dgate
        dup_ref[0] = dup
        y_ref[0] = contract(act_low, down_mat, 1, 1).astype(jnp.bfloat16)
        dx_ref[0, :, 0:width] = (
            contract(dgate, gate_mat, 1, 1) + contract(dup, up_mat, 1, 1)
        ).astype(jnp.bfloat16)
        dx_ref[0, :, width : width + LANES] = jnp.where(
            column == first[0] + e, gate_grad, 0.0
        ).astype(jnp.bfloat16)


def run_experts(x_rows, c_rows, w_gate, w_up, w_down, live, first):
    experts, rows, width = c_rows.shape
    hidden = w_gate.shape[2]

    def tile_map(e, t, live, first):
        return (e, t, 0)

    mat = pl.BlockSpec((1, width, hidden), lambda e, t, live, first: (e, 0, 0))
    wide = pl.BlockSpec((1, TILE, width + LANES), tile_map)
    plain = pl.BlockSpec((1, TILE, width), tile_map)
    inner = pl.BlockSpec((1, TILE, hidden), tile_map)
    b16 = jnp.bfloat16
    return pl.pallas_call(
        expert_kernel,
        grid_spec=pltpu.PrefetchScalarGridSpec(
            num_scalar_prefetch=2,
            grid=(experts, rows // TILE),
            in_specs=[wide, plain, mat, mat, mat],
            out_specs=[wide, plain, inner, inner, inner],
        ),
        out_shape=[
            jax.ShapeDtypeStruct(x_rows.shape, b16),
            jax.ShapeDtypeStruct(c_rows.shape, b16),
        ]
        + [jax.ShapeDtypeStruct((experts, rows, hidden), b16)] * 3,
        compiler_params=pltpu.CompilerParams(
            dimension_semantics=("arbitrary", "arbitrary"), vmem_limit_bytes=60 * 2**20
        ),
        cost_estimate=pl.CostEstimate(
            flops=12 * experts * rows * width * hidden,
            bytes_accessed=8 * experts * rows * width,
            transcendentals=experts * rows * hidden,
        ),
        name="experts",
    )(live, first, x_rows, c_rows, w_gate, w_up, w_down)


MESH = pl.DeviceIdType.MESH


class Place:
    def __init__(self, counts, fsdp_too):
        self.n_hi, self.n_lo, self.n_x, self.n_core = counts
        sp = lax.axis_index("sp")
        self.hi, self.lo = sp // self.n_lo, sp % self.n_lo
        if fsdp_too:
            fs = lax.axis_index("fsdp")
            self.x, self.core = fs // self.n_core, fs % self.n_core
        else:
            self.x, self.core = 0, 0

    def peer(self, dim, ahead):
        if dim == "core":
            return {"fsdp": self.x * self.n_core + (self.core + ahead) % self.n_core}
        if dim == "x":
            return {"fsdp": (self.x + ahead) % self.n_x * self.n_core + self.core}
        if dim == "lo":
            return {"sp": self.hi * self.n_lo + (self.lo + ahead) % self.n_lo}
        return {"sp": (self.hi + ahead) % self.n_hi * self.n_lo + self.lo}

    def sizes(self):
        return {"core": self.n_core, "x": self.n_x, "lo": self.n_lo, "hi": self.n_hi}

    def meet(self, other=None):
        barrier = pltpu.get_barrier_semaphore()
        met = 0
        for dim, size in self.sizes().items():
            for ahead in range(1, size):
                pl.semaphore_signal(
                    barrier, inc=1, device_id=self.peer(dim, ahead), device_id_type=MESH
                )
                met += 1
        for dim in ("x", "core") if other is not None else ():
            for ahead in range(1, other.sizes()[dim]):
                pl.semaphore_signal(
                    barrier, inc=1, device_id=other.peer(dim, ahead), device_id_type=MESH
                )
                met += 1
        pl.semaphore_wait(barrier, met)


def mesh_counts(sp_count, fs_count):
    low = 2
    while low * low < sp_count // 2:
        low *= 2
    low = min(low, sp_count)
    core = 2 if fs_count % 2 == 0 else 1
    return sp_count // low, low, fs_count // core, core


def scatter_kernel(
    counts, parts, fsdp_too, part_ref, out_ref, own, buf, first, second, third, own_sem, s0, r0,
    s1, r1, s2, r2, s3, r3, host=None, side=None,
):
    at = Place(counts, fsdp_too)
    n_hi, n_lo, n_x, n_core = counts
    rows = out_ref.shape[0] // parts
    pairs = parts // 2
    steps = n_hi * pairs
    lag = 1
    orders = [[d for d in o if at.sizes()[d] > 1] for o in (("x", "lo"), ("lo", "x"))]

    def remote(src, dst, send, recv, dim, ahead):
        return pltpu.make_async_remote_copy(
            src_ref=src, dst_ref=dst, send_sem=send, recv_sem=recv,
            device_id=at.peer(dim, ahead), device_id_type=MESH,
        )

    def where(t, v):
        return (at.hi + 1 + t // pairs) % n_hi, t % pairs * 2 + v

    def mine(t, v, core):
        hi, q = where(t, v)
        cut = pl.ds(pl.multiple_of(q * rows, 16), rows)
        if host is not None:
            return host.part.at[t // pairs % 2, :, core, :, cut, :]
        return part_ref.at[:, core, hi, :, cut, :]

    def load_own(t, v):
        place = own.at[t % 2, v] if n_core > 1 else buf.at[2 * t + v]
        return pltpu.make_async_copy(mine(t, v, at.core), place, own_sem.at[t % 2, v])

    def core_copy(t, v):
        return remote(
            mine(t, v, (at.core + 1) % 2), buf.at[2 * t + v], s0.at[2 * t + v], r0.at[2 * t + v],
            "core", 1,
        )

    def mid_copy(t, v, stage, ahead):
        u = 2 * t + v
        dim = orders[v][stage]
        size = at.sizes()[dim]
        to = ((at.x if dim == "x" else at.lo) + ahead) % size
        if stage == 0:
            src = buf.at[u, to] if dim == "x" else buf.at[u, :, to]
            dst = first.at[u, size - ahead - 1, pl.ds(0, n_lo if dim == "x" else n_x)]
            return remote(
                src, dst, s1.at[u, ahead - 1], r1.at[u, size - ahead - 1], dim, ahead
            )
        return remote(
            first.at[u, 0, to], second.at[u, size - ahead - 1],
            s2.at[u, ahead - 1], r2.at[u, size - ahead - 1], dim, ahead,
        )

    def wait_in(t, v, stage):
        size = at.sizes()[orders[v][stage]]
        for ahead in range(1, size):
            mid_copy(t, v, stage, ahead).wait_recv()

    def start_out(t, v, stage):
        size = at.sizes()[orders[v][stage]]
        for ahead in range(1, size):
            mid_copy(t, v, stage, ahead).start()

    def wide(ref):
        return ref[...].astype(jnp.float32)

    def result(t, v):
        u = 2 * t + v
        if len(orders[v]) == 2:
            return second.at[u, 0]
        if len(orders[v]) == 1:
            return first.at[u, 0, 0]
        return buf.at[u, 0, 0]

    def last_copy(t, v, ahead):
        _, q = where(t, v)
        return remote(
            result(t, v), third.at[n_hi - ahead - 1, q],
            s3.at[2 * t + v], r3.at[n_hi - ahead - 1, q], "hi", ahead,
        )

    def send_last(t, v):
        for k in range(n_hi - 1):

            @pl.when(t // pairs == k)
            def _(k=k):
                last_copy(t, v, k + 1).start()

    def stage_core(t, v):
        u = 2 * t + v
        if host is None:
            load_own(t, v).wait()
            own_part = own.at[t % 2, v]
        else:
            own_part = mine(t, v, at.core)
        if n_core > 1:
            core_copy(t, v).wait_recv()

            @pl.loop(0, n_x * n_lo)
            def _(j):
                x, lo = j // n_lo, j % n_lo
                place = buf.at[u, x, lo]
                place[...] = (wide(place) + wide(own_part.at[x, lo])).astype(jnp.bfloat16)

        if orders[v]:
            start_out(t, v, 0)
        else:
            send_last(t, v)

    def stage_mid(t, v, stage):
        u = 2 * t + v
        wait_in(t, v, stage)
        dim = orders[v][stage]
        size = at.sizes()[dim]
        if stage == 0:
            keep = n_lo if dim == "x" else n_x

            @pl.loop(0, keep)
            def _(j):
                base = buf.at[u, at.x, j] if dim == "x" else buf.at[u, j, at.lo]
                total = wide(base)
                for s in range(size - 1):
                    total = total + wide(first.at[u, s, j])
                first.at[u, 0, j][...] = total.astype(jnp.bfloat16)

        else:
            base = first.at[u, 0, at.x if dim == "x" else at.lo]
            total = wide(base)
            for s in range(size - 1):
                total = total + wide(second.at[u, s])
            second.at[u, 0][...] = total.astype(jnp.bfloat16)
        if stage + 1 < len(orders[v]):
            start_out(t, v, stage + 1)
        else:
            send_last(t, v)

    def each_core_copy(group, act):
        @pl.loop(0, pairs)
        def _(g):
            for v in range(2):
                act(core_copy(group * pairs + g, v))

    def make_group(group, piece, pieces):
        host.run(at, (at.hi + 1 + group) % n_hi, group % 2, piece, pieces)

    at.meet()
    if host is not None:
        make_group(0, 0, 1)
        each_core_copy(0, lambda c: c.start())
    else:
        if n_core > 1:

            @pl.loop(0, n_hi)
            def _(group):
                each_core_copy(group, lambda c: c.start())

        for v in range(2):
            load_own(0, v).start()

    depth = len(orders[0])

    @pl.loop(0, steps + depth * lag)
    def _(t):
        if host is None:

            @pl.when(t + 1 < steps)
            def _():
                for v in range(2):
                    load_own(t + 1, v).start()

        @pl.when(t < steps)
        def _():
            for v in range(2):
                stage_core(t, v)

        for stage in range(depth):
            back = (stage + 1) * lag

            @pl.when((t >= back) & (t < steps + back))
            def _(stage=stage, back=back):
                for v in range(2):
                    stage_mid(t - back, v, stage)

        if host is not None:

            @pl.when(t + pairs < steps)
            def _():
                group = t // pairs + 1

                @pl.when((t % pairs == 0) & (group >= 2))
                def _():
                    each_core_copy(group - 2, lambda c: c.wait_send())

                make_group(group, t % pairs, pairs)

                @pl.when(t % pairs == pairs - 1)
                def _():
                    each_core_copy(group, lambda c: c.start())

        if side is not None:
            side.share(t, steps + depth * lag)

    for g in range(pairs):
        t = (n_hi - 1) * pairs + g
        for v in range(2):
            q = g * 2 + v
            total = wide(result(t, v))
            for s in range(n_hi - 1):
                last_copy(g, v, n_hi - 1 - s).wait_recv()
                total = total + wide(third.at[s, q])
            out_ref[pl.ds(q * rows, rows), :] = total.astype(out_ref.dtype)

    @pl.loop(0, steps)
    def _(t):
        for v in range(2):
            if host is None and n_core > 1:
                core_copy(t, v).wait_send()
            for stage in range(depth):
                for ahead in range(1, at.sizes()[orders[v][stage]]):
                    mid_copy(t, v, stage, ahead).wait_send()

            @pl.when(t // pairs < n_hi - 1)
            def _(v=v):
                last_copy(t, v, 1).wait_send()

    if host is not None:
        for group in range(max(n_hi - 2, 0), n_hi):
            each_core_copy(group, lambda c: c.wait_send())


class WeightGrads:
    def __init__(self, rows, grads, outs, row_bufs, grad_buf, acc, stage, in_sems, out_sems):
        self.rows, self.grads, self.outs = rows, grads, outs
        self.row_bufs, self.grad_buf, self.acc, self.stage = row_bufs, grad_buf, acc, stage
        self.in_sems, self.out_sems = in_sems, out_sems
        experts, total, _ = grads[0].shape
        self.depth = grad_buf.shape[2]
        self.each = total // self.depth
        self.jobs = experts * self.each

    def loads(self, j, slot):
        e = j // self.each
        rows = pl.ds(pl.multiple_of(j % self.each * self.depth, self.depth), self.depth)
        copies = []
        for k in range(2):
            width = self.row_bufs[k].shape[2]
            copies.append(
                pltpu.make_async_copy(
                    self.rows[k].at[e, rows, pl.ds(0, width)], self.row_bufs[k].at[slot],
                    self.in_sems.at[slot, k],
                )
            )
        for k in range(3):
            copies.append(
                pltpu.make_async_copy(
                    self.grads[k].at[e, rows], self.grad_buf.at[slot, k],
                    self.in_sems.at[slot, 2 + k],
                )
            )
        return copies

    def stores(self, e):
        return [
            pltpu.make_async_copy(self.stage.at[k], self.outs[k].at[e], self.out_sems.at[k])
            for k in range(3)
        ]

    def begin(self):
        for copy in self.loads(0, 0):
            copy.start()

    def share(self, t, turns):
        count = -(-self.jobs // turns)

        @pl.loop(0, count)
        def _(i):
            j = t * count + i

            @pl.when(j < self.jobs)
            def _():
                self.job(j)

    def job(self, j):
        slot = j % 2

        @pl.when(j + 1 < self.jobs)
        def _():
            for copy in self.loads(j + 1, 1 - slot):
                copy.start()

        for copy in self.loads(j, slot):
            copy.wait()

        @pl.when(j % self.each == 0)
        def _():
            self.acc[...] = jnp.zeros_like(self.acc)

        for k in range(3):
            rows = self.row_bufs[0 if k < 2 else 1]
            for start, size in column_spans(rows.shape[2]):
                cols = pl.ds(start, size)
                self.acc[k, :, cols] += contract(
                    self.grad_buf[slot, k], rows[slot, :, cols], 0, 0
                )

        @pl.when(j % self.each == self.each - 1)
        def _():
            e = j // self.each

            @pl.when(e > 0)
            def _():
                for copy in self.stores(e - 1):
                    copy.wait()

            for k in range(3):
                self.stage[k] = self.acc[k].T
            for copy in self.stores(e):
                copy.start()

    def finish(self):
        for copy in self.stores(self.jobs // self.each - 1):
            copy.wait()


def scatter_grads_kernel(
    counts, parts, part_ref, x_ref, c_ref, dgate_ref, dup_ref, act_ref, out_ref, gg_ref, gu_ref,
    gd_ref, x_buf, c_buf, grad_buf, acc, stage, in_sems, out_sems, own, *scratch,
):
    side = WeightGrads(
        (x_ref, c_ref), (dgate_ref, dup_ref, act_ref), (gg_ref, gu_ref, gd_ref), (x_buf, c_buf),
        grad_buf, acc, stage, in_sems, out_sems,
    )
    side.begin()
    scatter_kernel(counts, parts, False, part_ref, out_ref, own, *scratch, side=side)
    side.finish()


def scatter_and_grads(partial, counts, parts, x_rows, c_rows, grads, ident, name):
    n_hi, n_lo, n_x, n_core = counts
    rows, width = partial.shape[4:]
    experts, slots, hidden = grads[0].shape
    depth = 512
    b16 = jnp.bfloat16
    anywhere = pl.BlockSpec(memory_space=pl.ANY)
    weight = jax.ShapeDtypeStruct((experts, width, hidden), jnp.float32)
    return pl.pallas_call(
        functools.partial(scatter_grads_kernel, counts, parts),
        in_specs=[anywhere] * 6,
        out_specs=[pl.BlockSpec(memory_space=pltpu.VMEM)] + [anywhere] * 3,
        out_shape=[jax.ShapeDtypeStruct((rows, width), jnp.float32)] + [weight] * 3,
        scratch_shapes=[
            pltpu.VMEM((2, depth, width), b16),
            pltpu.VMEM((2, depth, width), b16),
            pltpu.VMEM((2, 3, depth, hidden), b16),
            pltpu.VMEM((3, hidden, width), jnp.float32),
            pltpu.VMEM((3, width, hidden), jnp.float32),
            pltpu.SemaphoreType.DMA((2, 5)),
            pltpu.SemaphoreType.DMA((3,)),
            pltpu.VMEM((1, 1, 1, 1, 16, 128), b16),
        ]
        + scatter_scratch(counts, parts, rows // parts, width),
        compiler_params=pltpu.CompilerParams(
            collective_id=ident, has_side_effects=True, vmem_limit_bytes=60 * 2**20
        ),
        cost_estimate=pl.CostEstimate(
            flops=6 * experts * slots * width * hidden,
            bytes_accessed=4 * experts * slots * width,
            transcendentals=0,
        ),
        name=name,
    )(partial, x_rows, c_rows, *grads)


class Combine:
    def __init__(self, rows_ref, rank_ref, part, held, sems, counts):
        self.rows_ref, self.rank_ref, self.part, self.held, self.sems = (
            rows_ref, rank_ref, part, held, sems,
        )
        self.n_hi, self.n_lo, self.n_x, self.n_core = counts

    def run(self, at, hi, slot, piece, pieces):
        total = self.n_x * self.n_core * self.n_lo
        count = total // pieces
        _, experts, slots, width = self.held.shape

        def spot(j):
            j = piece * count + j
            return j // (self.n_core * self.n_lo), j // self.n_lo % self.n_core, j % self.n_lo

        def block(j):
            x, core, lo = spot(j)
            return ((x * self.n_core + core) * self.n_hi + hi) * self.n_lo + lo

        def load(j, place):
            return pltpu.make_async_copy(
                self.rows_ref.at[:, block(j)], self.held.at[place], self.sems.at[place]
            )

        load(0, 0).start()

        @pl.loop(0, count)
        def _(j):
            place = j % 2

            @pl.when(j + 1 < count)
            def _():
                load(j + 1, 1 - place).start()

            load(j, place).wait()
            pick = pick_matrix(self.rank_ref[block(j)], slots)
            x, core, lo = spot(j)
            for start, size in column_spans(width):
                cols = pl.ds(start, size)
                found = self.held[place, :, :, cols].reshape(experts * slots, size)
                self.part[slot, x, core, lo, :, cols] = contract(pick, found, 0, 0).astype(
                    jnp.bfloat16
                )


def combine_scatter_kernel(
    counts, parts, rows_ref, rank_ref, out_ref, part, held, held_sem, *scratch
):
    host = Combine(rows_ref, rank_ref, part, held, held_sem, counts)
    scatter_kernel(counts, parts, True, None, out_ref, None, *scratch, host=host)


def scatter_scratch(counts, parts, r, width):
    n_hi, n_lo, n_x, _ = counts
    units = n_hi * parts
    keep = max(n_x, n_lo)
    peers = max(n_x, n_lo, 2) - 1
    b16 = jnp.bfloat16
    return [
        pltpu.VMEM((units, n_x, n_lo, r, width), b16),
        pltpu.VMEM((units, peers, keep, r, width), b16),
        pltpu.VMEM((units, peers, r, width), b16),
        pltpu.VMEM((max(n_hi - 1, 1), parts, r, width), b16),
        pltpu.SemaphoreType.DMA((2, 2)),
        pltpu.SemaphoreType.DMA((units,)),
        pltpu.SemaphoreType.DMA((units,)),
        pltpu.SemaphoreType.DMA((units, peers)),
        pltpu.SemaphoreType.DMA((units, peers)),
        pltpu.SemaphoreType.DMA((units, peers)),
        pltpu.SemaphoreType.DMA((units, peers)),
        pltpu.SemaphoreType.DMA((units,)),
        pltpu.SemaphoreType.DMA((max(n_hi - 1, 1), parts)),
    ]


def scatter_bytes(counts, parts, rows, width):
    n_hi, n_lo, n_x, _ = counts
    keep = max(n_x, n_lo)
    peers = max(n_x, n_lo, 2) - 1
    held = n_hi * (n_x * n_lo + peers * keep + peers) + max(n_hi - 1, 1)
    return (2 * held + 4) * rows * width


VMEM_ROOM = 58 * 2**20


def combine_sum(rows, rank, counts, parts, slots, ident, name):
    blocks, experts, block = rank.shape
    width = rows.shape[-1]
    _, n_lo, n_x, n_core = counts
    b16 = jnp.bfloat16
    return pl.pallas_call(
        functools.partial(combine_scatter_kernel, counts, parts),
        in_specs=[pl.BlockSpec(memory_space=pl.ANY), pl.BlockSpec(memory_space=pltpu.VMEM)],
        out_specs=pl.BlockSpec(memory_space=pltpu.VMEM),
        out_shape=jax.ShapeDtypeStruct((block, width), jnp.float32),
        scratch_shapes=[
            pltpu.VMEM((2, n_x, n_core, n_lo, block, width), b16),
            pltpu.VMEM((2, experts, slots, width), b16),
            pltpu.SemaphoreType.DMA((2,)),
        ]
        + scatter_scratch(counts, parts, block // parts, width),
        compiler_params=pltpu.CompilerParams(
            collective_id=ident, has_side_effects=True, vmem_limit_bytes=62 * 2**20
        ),
        cost_estimate=pl.CostEstimate(
            flops=2 * blocks * experts * slots * block * width,
            bytes_accessed=4 * blocks * block * width,
            transcendentals=0,
        ),
        name=name,
    )(rows.reshape(experts, blocks, slots, width), rank)


def scatter_sum(partial, counts, fsdp_too, parts, out_dtype, ident, name):
    _, n_lo, n_x, n_core = counts
    rows, width = partial.shape[4:]
    r = rows // parts
    own_shape = (2, 2, n_x, n_lo, r, width) if n_core > 1 else (1, 1, 1, 1, 16, 128)
    scratch = [pltpu.VMEM(own_shape, jnp.bfloat16)] + scatter_scratch(counts, parts, r, width)
    return pl.pallas_call(
        functools.partial(scatter_kernel, counts, parts, fsdp_too),
        in_specs=[pl.BlockSpec(memory_space=pl.ANY)],
        out_specs=pl.BlockSpec(memory_space=pltpu.VMEM),
        out_shape=jax.ShapeDtypeStruct((rows, width), out_dtype),
        scratch_shapes=scratch,
        compiler_params=pltpu.CompilerParams(
            collective_id=ident, has_side_effects=True, vmem_limit_bytes=60 * 2**20
        ),
        cost_estimate=pl.CostEstimate(
            flops=partial.size, bytes_accessed=2 * partial.size, transcendentals=0
        ),
        name=name,
    )(partial)


def gather_kernel(
    counts, parts, fsdp_too, in_ref, out_ref, own_sem, s0, r0, s1, r1, s2, r2, s3, r3, host=None,
    side=None,
):
    at = Place(counts, fsdp_too)
    n_hi, n_lo, n_x, n_core = counts
    rows = in_ref.shape[0] // parts
    pairs = parts // 2
    steps = n_hi * pairs
    orders = [[d for d in o if at.sizes()[d] > 1] for o in (("lo", "x"), ("x", "lo"))]
    depth = len(orders[0])

    def remote(src, dst, send, recv, dim, ahead):
        return pltpu.make_async_remote_copy(
            src_ref=src, dst_ref=dst, send_sem=send, recv_sem=recv,
            device_id=at.peer(dim, ahead), device_id_type=MESH,
        )

    def span(q):
        return pl.ds(pl.multiple_of(q * rows, 16), rows)

    def hi_copy(q, ahead):
        return remote(
            in_ref.at[span(q)], out_ref.at[at.x, at.core, at.hi, at.lo, span(q)],
            s0.at[ahead - 1, q], r0.at[n_hi - ahead - 1, q], "hi", ahead,
        )

    def where(t, v):
        return (at.hi + n_hi - t // pairs) % n_hi, t % pairs * 2 + v

    def mid_copy(t, v, stage, ahead):
        u = 2 * t + v
        hi, q = where(t, v)
        dim = orders[v][stage]
        size = at.sizes()[dim]
        if stage == 0:
            ref = out_ref.at[at.x, at.core, hi, at.lo, span(q)]
            if_own = in_ref.at[span(q)]
            del if_own
            return remote(
                ref, ref, s1.at[u, ahead - 1], r1.at[u, size - ahead - 1], dim, ahead
            )
        if dim == "x":
            ref = out_ref.at[at.x, at.core, hi, :, span(q)]
        else:
            ref = out_ref.at[:, at.core, hi, at.lo, span(q)]
        return remote(ref, ref, s2.at[u, ahead - 1], r2.at[u, size - ahead - 1], dim, ahead)

    def core_copy(t, v):
        u = 2 * t + v
        hi, q = where(t, v)
        ref = out_ref.at[:, at.core, hi, :, span(q)]
        return remote(ref, ref, s3.at[u], r3.at[u], "core", 1)

    def each_mid(t, v, stage, act):
        size = at.sizes()[orders[v][stage]]
        for ahead in range(1, size):
            act(mid_copy(t, v, stage, ahead))

    keep = pltpu.make_async_copy(
        in_ref, out_ref.at[at.x, at.core, at.hi, at.lo], own_sem
    )
    keep.start()
    at.meet(side.at if side is not None else None)
    if side is not None:
        side.begin()
    for ahead in range(1, n_hi):
        for q in range(parts):
            hi_copy(q, ahead).start()
    keep.wait()

    @pl.loop(0, steps + depth + (1 if host is not None and n_core > 1 else 0))
    def _(t):
        @pl.when(t < steps)
        def _():
            for v in range(2):
                _, q = where(t, v)
                for k in range(1, n_hi):

                    @pl.when(t // pairs == k)
                    def _(k=k, q=q):
                        hi_copy(q, k).wait_recv()

                if depth > 0:
                    each_mid(t, v, 0, lambda c: c.start())
                elif n_core > 1:
                    core_copy(t, v).start()

        for stage in range(depth):
            back = stage + 1

            @pl.when((t >= back) & (t < steps + back))
            def _(stage=stage, back=back):
                for v in range(2):
                    each_mid(t - back, v, stage, lambda c: c.wait_recv())
                    if stage + 1 < depth:
                        each_mid(t - back, v, stage + 1, lambda c: c.start())
                    elif n_core > 1:
                        core_copy(t - back, v).start()

        if side is not None:

            @pl.when(t == steps // 2 + 1)
            def _():
                side.middle()

        if host is not None:
            for origin_step in range(n_hi):
                done = (origin_step + 1) * pairs - 1 + depth
                hi = (at.hi + n_hi - origin_step) % n_hi

                @pl.when(t == done)
                def _(hi=hi):
                    host.blocks(at, at.core, hi)

                if n_core > 1:

                    @pl.when(t == done + 1)
                    def _(hi=hi, origin_step=origin_step):
                        for g in range(pairs):
                            for v in range(2):
                                core_copy(origin_step * pairs + g, v).wait_recv()
                        host.blocks(at, 1 - at.core, hi)

            host.others(t, steps + depth)

    @pl.loop(0, steps)
    def _(t):
        for v in range(2):
            if n_core > 1:
                if host is None:
                    core_copy(t, v).wait_recv()
                core_copy(t, v).wait_send()
            for stage in range(depth):
                each_mid(t, v, stage, lambda c: c.wait_send())

    for q in range(parts):
        for ahead in range(1, n_hi):
            hi_copy(q, ahead).wait_send()

    if side is not None:
        side.end()


class SideGather:
    def __init__(self, counts, in_ref, out_ref, own_sem, s_x, r_x, s_core, r_core):
        self.at = Place(counts, True)
        self.in_ref, self.out_ref, self.own_sem = in_ref, out_ref, own_sem
        self.s_x, self.r_x, self.s_core, self.r_core = s_x, r_x, s_core, r_core

    def own(self):
        at = self.at
        return pltpu.make_async_copy(self.in_ref, self.out_ref.at[at.x, at.core], self.own_sem)

    def x_copy(self, ahead):
        at = self.at
        return pltpu.make_async_remote_copy(
            src_ref=self.in_ref, dst_ref=self.out_ref.at[at.x, at.core],
            send_sem=self.s_x.at[ahead - 1], recv_sem=self.r_x.at[at.n_x - ahead - 1],
            device_id=at.peer("x", ahead), device_id_type=MESH,
        )

    def core_copy(self):
        ref = self.out_ref.at[:, self.at.core]
        return pltpu.make_async_remote_copy(
            src_ref=ref, dst_ref=ref, send_sem=self.s_core, recv_sem=self.r_core,
            device_id=self.at.peer("core", 1), device_id_type=MESH,
        )

    def begin(self):
        self.own().start()
        for ahead in range(1, self.at.n_x):
            self.x_copy(ahead).start()

    def middle(self):
        self.own().wait()
        for ahead in range(1, self.at.n_x):
            self.x_copy(ahead).wait_recv()
        if self.at.n_core > 1:
            self.core_copy().start()

    def end(self):
        for ahead in range(1, self.at.n_x):
            self.x_copy(ahead).wait_send()
        if self.at.n_core > 1:
            self.core_copy().wait()


def gather_two_kernel(
    counts, parts, side_counts, in_ref, side_in, out_ref, side_out, own_sem, s_x, r_x, s_core,
    r_core, *sems,
):
    side = SideGather(side_counts, side_in, side_out, own_sem, s_x, r_x, s_core, r_core)
    gather_kernel(counts, parts, False, in_ref, out_ref, *sems, side=side)


def gather_two(own, weight, counts, side_counts, parts, ident, name):
    n_hi, n_lo, _, _ = counts
    _, _, n_x, n_core = side_counts
    rows, width = own.shape
    anywhere = pl.BlockSpec(memory_space=pl.ANY)
    dma = pltpu.SemaphoreType.DMA
    out, side = pl.pallas_call(
        functools.partial(gather_two_kernel, counts, parts, side_counts),
        in_specs=[anywhere] * 2,
        out_specs=[anywhere] * 2,
        out_shape=[
            jax.ShapeDtypeStruct((1, 1, n_hi, n_lo, rows, width), own.dtype),
            jax.ShapeDtypeStruct((n_x, n_core) + weight.shape, weight.dtype),
        ],
        scratch_shapes=[dma, dma((max(n_x - 1, 1),)), dma((max(n_x - 1, 1),)), dma, dma]
        + gather_sems(counts, parts),
        compiler_params=pltpu.CompilerParams(collective_id=ident, has_side_effects=True),
        cost_estimate=pl.CostEstimate(
            flops=0, bytes_accessed=4 * n_hi * n_lo * rows * width, transcendentals=0
        ),
        name=name,
    )(own, weight)
    return out.reshape(-1, width), side.reshape(-1, weight.shape[1])


class Dispatch:
    def __init__(self, tables, rows, bufs, ins, outs, rank_ref, geometry):
        self.tables, self.rows, self.bufs, self.ins, self.outs = tables, rows, bufs, ins, outs
        self.rank_ref = rank_ref
        self.n_hi, self.n_lo, self.n_x, self.n_core = geometry

    def load(self, which, index, slot):
        held, _ = self.bufs[which]
        return pltpu.make_async_copy(
            self.tables[which].at[index + (slice(None), pl.ds(0, held.shape[2]))],
            held.at[slot], self.ins[which].at[slot],
        )

    def store(self, which, block, slot):
        _, found = self.bufs[which]
        return pltpu.make_async_copy(
            found.at[slot], self.rows[which].at[:, block], self.outs[which].at[slot]
        )

    def run(self, which, block_of, index_of, count):
        held, found = self.bufs[which]
        experts, slots, width = found.shape[1:]
        if held is not None:
            self.load(which, index_of(0), 0).start()

        @pl.loop(0, count)
        def _(j):
            slot = j % 2

            if held is not None:

                @pl.when(j + 1 < count)
                def _():
                    self.load(which, index_of(j + 1), 1 - slot).start()

            @pl.when(j >= 2)
            def _():
                self.store(which, block_of(j - 2), slot).wait()

            if held is not None:
                self.load(which, index_of(j), slot).wait()
                table = held.at[slot]
            else:
                table = self.tables[which].at[index_of(j)]
            pick = pick_matrix(self.rank_ref[block_of(j)], slots)
            for start, size in column_spans(width):
                cols = pl.ds(start, size)
                picked = jnp.dot(
                    pick, table[:, cols], preferred_element_type=jnp.float32
                ).astype(jnp.bfloat16)
                found[slot, :, :, cols] = picked.reshape(experts, slots, size)
            self.store(which, block_of(j), slot).start()

        for j in range(max(count - 2, 0), count):
            self.store(which, block_of(j), j % 2).wait()

    def blocks(self, at, core, hi):
        def spot(j):
            return j // self.n_lo, core, hi, j % self.n_lo

        def block_of(j):
            x, c, h, lo = spot(j)
            return ((x * self.n_core + c) * self.n_hi + h) * self.n_lo + lo

        self.run(0, block_of, spot, self.n_x * self.n_lo)

    def others(self, t, steps):
        total = self.n_x * self.n_core * self.n_hi * self.n_lo
        each = -(-total // steps)
        for step in range(steps):
            first = min(step * each, total)
            count = min(each, total - first)
            if count > 0:

                @pl.when(t == step)
                def _(first=first, count=count):
                    self.run(1, lambda j: first + j, lambda j: (first + j,), count)


def dispatch_kernel(
    counts, parts, in_ref, other_ref, rank_ref, rows_ref, other_rows_ref, *rest
):
    out_ref, held, found, other_held, other_found, in_sem, put_sem, other_in_sem, other_put_sem = (
        rest[:9]
    )
    sems = rest[9:]
    if len(out_ref.shape) == 6 and held.shape[0] == 1:
        held = None
    host = Dispatch(
        (out_ref, other_ref), (rows_ref, other_rows_ref),
        ((held, found), (other_held, other_found)), (in_sem, other_in_sem),
        (put_sem, other_put_sem), rank_ref, counts,
    )
    gather_kernel(counts, parts, True, in_ref, out_ref, *sems, host=host)


def gather_sems(counts, parts):
    n_hi, n_lo, n_x, n_core = counts
    units = n_hi * parts
    peers = max(n_x, n_lo, 2) - 1
    ahead = max(n_hi - 1, 1)
    sizes = [(ahead, parts)] * 2 + [(units, peers)] * 4 + [(units,)] * 2
    return [pltpu.SemaphoreType.DMA] + [pltpu.SemaphoreType.DMA(size) for size in sizes]


def gather_and_dispatch(own, other_all, other_width, rank, slots, sp_count, fs_count, ident, name):
    counts = mesh_counts(sp_count, fs_count)
    n_hi, n_lo, n_x, n_core = counts
    rows, width = own.shape
    blocks, experts, _ = rank.shape
    parts = 4 if rows % 64 == 0 else 2
    b16 = jnp.bfloat16
    anywhere = pl.BlockSpec(memory_space=pl.ANY)
    table = (n_x, n_core, n_hi, n_lo, rows, width)
    inside = 2 * blocks * rows * width <= 36 * 2**20
    scratch = [
        pltpu.VMEM((1, 16, LANES) if inside else (2, rows, width), b16),
        pltpu.VMEM((2, experts, slots, width), b16),
        pltpu.VMEM((2, rows, other_width), b16),
        pltpu.VMEM((2, experts, slots, other_width), b16),
    ] + [pltpu.SemaphoreType.DMA((2,))] * 4
    flops = 2 * blocks * experts * slots * rows * (width + other_width)
    results = [
        jax.ShapeDtypeStruct((experts, blocks, slots, width), b16),
        jax.ShapeDtypeStruct((experts, blocks, slots, other_width), b16),
    ]
    if inside:
        scratch = [pltpu.VMEM(table, b16)] + scratch
    else:
        results.append(jax.ShapeDtypeStruct(table, b16))
    picked, other_picked, *_ = pl.pallas_call(
        functools.partial(dispatch_kernel, counts, parts),
        in_specs=[anywhere, anywhere, pl.BlockSpec(memory_space=pltpu.VMEM)],
        out_specs=[anywhere] * len(results),
        out_shape=results,
        scratch_shapes=scratch + gather_sems(counts, parts),
        compiler_params=pltpu.CompilerParams(
            collective_id=ident, has_side_effects=True, vmem_limit_bytes=56 * 2**20
        ),
        cost_estimate=pl.CostEstimate(
            flops=flops, bytes_accessed=8 * blocks * rows * width, transcendentals=0
        ),
        name=name,
    )(own, other_all.reshape(blocks, rows, -1), rank)
    return picked.reshape(experts, -1, width), other_picked.reshape(experts, -1, other_width)


def gather_rows(own, counts, fsdp_too, parts, ident, name):
    n_hi, n_lo, n_x, n_core = counts
    rows, width = own.shape
    total = rows * n_hi * n_lo * n_x * n_core
    out = pl.pallas_call(
        functools.partial(gather_kernel, counts, parts, fsdp_too),
        in_specs=[pl.BlockSpec(memory_space=pl.ANY)],
        out_specs=pl.BlockSpec(memory_space=pl.ANY),
        out_shape=jax.ShapeDtypeStruct((n_x, n_core, n_hi, n_lo, rows, width), own.dtype),
        scratch_shapes=gather_sems(counts, parts),
        compiler_params=pltpu.CompilerParams(collective_id=ident, has_side_effects=True),
        cost_estimate=pl.CostEstimate(
            flops=0, bytes_accessed=4 * total * width, transcendentals=0
        ),
        name=name,
    )(own)
    return out.reshape(total, width)


def small_sum_kernel(counts, part_ref, out_ref, first, second, s0, r0, s1, r1):
    sp_count, fs_count = counts
    at = {"sp": lax.axis_index("sp"), "fsdp": lax.axis_index("fsdp")}

    def peer(dim, ahead, size):
        return {dim: (at[dim] + ahead) % size}

    barrier = pltpu.get_barrier_semaphore()
    for dim, size in (("sp", sp_count), ("fsdp", fs_count)):
        for ahead in range(1, size):
            pl.semaphore_signal(
                barrier, inc=1, device_id=peer(dim, ahead, size), device_id_type=MESH
            )
    pl.semaphore_wait(barrier, sp_count + fs_count - 2)

    def exchange(src, held, send, recv, dim, size):
        copies = [
            pltpu.make_async_remote_copy(
                src_ref=src, dst_ref=held.at[size - ahead - 1],
                send_sem=send.at[ahead - 1], recv_sem=recv.at[size - ahead - 1],
                device_id=peer(dim, ahead, size), device_id_type=MESH,
            )
            for ahead in range(1, size)
        ]
        for copy in copies:
            copy.start()
        total = src[...]
        for ahead, copy in enumerate(copies, 1):
            pltpu.make_async_remote_copy(
                src_ref=src, dst_ref=held.at[ahead - 1],
                send_sem=send.at[size - ahead - 1], recv_sem=recv.at[ahead - 1],
                device_id=peer(dim, size - ahead, size), device_id_type=MESH,
            ).wait_recv()
            total = total + held[ahead - 1]
        for copy in copies:
            copy.wait_send()
        return total

    total = exchange(part_ref, first, s0, r0, "sp", sp_count)
    out_ref[...] = total
    if fs_count > 1:
        total = exchange(out_ref, second, s1, r1, "fsdp", fs_count)
        out_ref[...] = total


def small_sum(part, sp_count, fs_count, ident, name):
    sems = [pltpu.SemaphoreType.DMA((max(n - 1, 1),)) for n in (sp_count, sp_count, fs_count, fs_count)]
    return pl.pallas_call(
        functools.partial(small_sum_kernel, (sp_count, fs_count)),
        in_specs=[pl.BlockSpec(memory_space=pltpu.VMEM)],
        out_specs=pl.BlockSpec(memory_space=pltpu.VMEM),
        out_shape=jax.ShapeDtypeStruct(part.shape, jnp.float32),
        scratch_shapes=[
            pltpu.VMEM((max(sp_count - 1, 1),) + part.shape, jnp.float32),
            pltpu.VMEM((max(fs_count - 1, 1),) + part.shape, jnp.float32),
        ]
        + sems,
        compiler_params=pltpu.CompilerParams(collective_id=ident, has_side_effects=True),
        name=name,
    )(part)


ROWS = 256


def window_scores(ends, count, q, k, first, top):
    scores = contract(q, k, 1, 1) * HEAD_DIM ** (-0.5)
    place = top + lax.broadcasted_iota(jnp.int32, (ROWS, 1), 0)
    oldest = jnp.maximum(place - (WINDOW - 1), 0)
    for n in range(count):
        oldest = jnp.maximum(oldest, jnp.where(place >= ends[n], ends[n], 0))
    other = first + lax.broadcasted_iota(jnp.int32, scores.shape, 1)
    return jnp.where((other >= oldest) & (other <= place), scores, masked_score)


def window_first(i, reach, total):
    return pl.multiple_of(jnp.clip(i * ROWS + ROWS - reach, 0, total - reach), ROWS)


def softmax_rows(scores):
    weights = jnp.exp(scores - jnp.max(scores, axis=-1, keepdims=True))
    return weights / jnp.sum(weights, axis=-1, keepdims=True)


def attend_kernel(count, reach, ends, q_ref, k_ref, v_ref, o_ref):
    i = pl.program_id(1)
    first = window_first(i, reach, k_ref.shape[0])
    keys = pl.ds(first, reach)
    scores = window_scores(ends, count, q_ref[...], k_ref[keys, :], first, i * ROWS)
    probs = softmax_rows(scores).astype(jnp.bfloat16)
    o_ref[...] = jnp.dot(probs, v_ref[keys, :], preferred_element_type=jnp.float32).astype(
        jnp.bfloat16
    )


def attend_back_kernel(
    count, reach, ends, q_ref, k_ref, v_ref, g_ref, dq_ref, dk_ref, dv_ref, dk_acc, dv_acc
):
    i = pl.program_id(1)
    first = window_first(i, reach, k_ref.shape[0])
    keys = pl.ds(first, reach)
    scale = HEAD_DIM ** (-0.5)

    @pl.when(i == 0)
    def _():
        dk_acc[...] = jnp.zeros_like(dk_acc)
        dv_acc[...] = jnp.zeros_like(dv_acc)

    q = q_ref[...]
    k = k_ref[keys, :]
    grad = g_ref[...]
    probs = softmax_rows(window_scores(ends, count, q, k, first, i * ROWS))
    prob_grad = contract(grad, v_ref[keys, :], 1, 1)
    delta = jnp.sum(probs * prob_grad, axis=-1, keepdims=True)
    score_grad = (probs * (prob_grad - delta)).astype(jnp.bfloat16)
    dq_ref[...] = (
        jnp.dot(score_grad, k, preferred_element_type=jnp.float32) * scale
    ).astype(jnp.bfloat16)
    dk_acc[keys, :] += contract(score_grad, q, 0, 0) * scale
    dv_acc[keys, :] += contract(probs.astype(jnp.bfloat16), grad, 0, 0)

    @pl.when(i == pl.num_programs(1) - 1)
    def _():
        dk_ref[...] = dk_acc[...].astype(jnp.bfloat16)
        dv_ref[...] = dv_acc[...].astype(jnp.bfloat16)


def attend(query, key, value, lengths):
    seq_rows, span = query.shape
    heads = span // HEAD_DIM
    reach = min(WINDOW + ROWS, seq_rows)
    count = lengths.shape[0]
    ends = jnp.cumsum(lengths)
    tile = pl.BlockSpec((ROWS, HEAD_DIM), lambda h, i, ends: (i, h))
    whole = pl.BlockSpec((seq_rows, HEAD_DIM), lambda h, i, ends: (0, h))
    shape = jax.ShapeDtypeStruct((seq_rows, span), jnp.bfloat16)
    pairs = seq_rows * heads * reach

    def call(kernel, ins, outs, scratch, name):
        return pl.pallas_call(
            kernel,
            grid_spec=pltpu.PrefetchScalarGridSpec(
                num_scalar_prefetch=1,
                grid=(heads, seq_rows // ROWS),
                in_specs=ins,
                out_specs=outs,
                scratch_shapes=scratch,
            ),
            out_shape=[shape] * len(outs),
            compiler_params=pltpu.CompilerParams(
                dimension_semantics=("arbitrary", "arbitrary"), vmem_limit_bytes=48 * 2**20
            ),
            cost_estimate=pl.CostEstimate(
                flops=4 * len(outs) * pairs * HEAD_DIM,
                bytes_accessed=8 * seq_rows * span,
                transcendentals=pairs,
            ),
            name=name,
        )

    attended = call(
        functools.partial(attend_kernel, count, reach), [tile, whole, whole], [tile], [], "attend"
    )(ends, query, key, value)[0]

    def back(grad):
        return call(
            functools.partial(attend_back_kernel, count, reach),
            [tile, whole, whole, tile],
            [tile, whole, whole],
            [pltpu.VMEM((seq_rows, HEAD_DIM), jnp.float32)] * 2,
            "attend_back",
        )(ends, query, key, value, grad)

    return attended, back


def scatter_over_all(partial, rows, sp_count, fs_count, ident, name):
    counts = mesh_counts(sp_count, fs_count)
    width = partial.shape[1]
    parts = 4 if rows % 64 == 0 else 2
    room = scatter_bytes(counts, parts, rows, width)
    room += 8 * counts[1] * counts[2] * rows // parts * width
    if room > VMEM_ROOM or rows % (parts * 16):
        part = lax.psum_scatter(partial, "fsdp", scatter_dimension=0, tiled=True)
        return lax.psum_scatter(part, "sp", scatter_dimension=0, tiled=True).astype(jnp.float32)
    n_hi, n_lo, n_x, n_core = counts
    shaped = partial.reshape(n_x, n_core, n_hi, n_lo, rows, width)
    return scatter_sum(shaped, counts, True, parts, jnp.float32, ident, name)


def combine_and_scatter(rows, rank, slots, sp_count, fs_count, ident, name):
    blocks, experts, block = rank.shape
    counts = mesh_counts(sp_count, fs_count)
    n_hi, n_lo, n_x, n_core = counts
    width = rows.shape[-1]
    parts = 4 if block % 64 == 0 else 2
    room = scatter_bytes(counts, parts, block, width)
    room += 4 * (n_x * n_core * n_lo * block + experts * slots) * width
    if n_core == 2 and room <= VMEM_ROOM and block % (parts * 16) == 0:
        return combine_sum(rows, rank, counts, parts, slots, ident, name)
    shaped = rows.reshape(experts, blocks, slots, -1)
    pick = (rank[:, :, None, :] == jnp.arange(slots)[None, None, :, None]).astype(jnp.bfloat16)
    partial = jnp.einsum("best,ebsw->btw", pick, shaped, preferred_element_type=jnp.float32)
    partial = partial.astype(jnp.bfloat16).reshape(blocks * block, -1)
    return scatter_over_all(partial, block, sp_count, fs_count, ident, name)


def scatter_over_fsdp(partial, rows, fs_count, ident, name):
    _, _, n_x, n_core = mesh_counts(1, fs_count)
    parts = 4 if rows % 64 == 0 else 2
    shaped = partial.reshape(n_x, n_core, 1, 1, rows, partial.shape[1])
    return scatter_sum(shaped, (1, 1, n_x, n_core), True, parts, jnp.float32, ident, name)


def gather_over_all(own, sp_count, fs_count, ident, name):
    parts = 4 if own.shape[0] % 64 == 0 else 2
    return gather_rows(own, mesh_counts(sp_count, fs_count), True, parts, ident, name)


def gather_over_sp(own, sp_count, ident, name):
    n_hi, n_lo, _, _ = mesh_counts(sp_count, 1)
    parts = 4 if own.shape[0] % 64 == 0 else 2
    return gather_rows(own, (n_hi, n_lo, 1, 1), False, parts, ident, name)


def sum_over_sp(rows, sp_count, ident, name):
    part = jnp.stack(rows)
    return small_sum(part.reshape(-1, 128), sp_count, 1, ident, name).reshape(part.shape)


def local(
    tokens,
    doc_lengths,
    expert_ids,
    norm_attn,
    norm_query,
    norm_key,
    norm_ffn,
    w_query,
    w_key,
    w_value,
    w_out,
    w_router,
    w_gate,
    w_up,
    w_down,
    cotangent,
):
    sp_count = lax.axis_size("sp")
    fs_count = lax.axis_size("fsdp")
    my_sp = lax.axis_index("sp")
    my_fs = lax.axis_index("fsdp")
    hidden_in = tokens[0].astype(jnp.float32)
    tok_rows, width = hidden_in.shape
    head_local = HEADS // sp_count
    seq_rows = tok_rows * sp_count
    span = head_local * HEAD_DIM
    expert_local = EXPERTS // sp_count
    first_expert = my_sp * expert_local
    gains = lax.all_gather(
        jnp.stack([norm_attn, norm_query, norm_key, norm_ffn]), "fsdp", axis=1, tiled=True
    ).astype(jnp.float32)
    gain_attn, gain_ffn = gains[0], gains[3]
    own_cols = lax.dynamic_slice_in_dim(gains, my_sp * span, span, axis=1)
    gain_query, gain_key = own_cols[1], own_cols[2]
    qkv_own = jnp.concatenate(
        [
            lax.dynamic_slice_in_dim(w, my_sp * span, span, axis=1)
            for w in (w_query, w_key, w_value)
        ],
        axis=1,
    )
    qkv_mat = lax.all_gather(qkv_own, "fsdp", axis=0, tiled=True)
    router_mat = lax.all_gather(w_router, "fsdp", axis=0, tiled=True)
    ids_own = jnp.pad(expert_ids[0].astype(jnp.bfloat16), ((0, 0), (0, LANES - TOPK)))
    cot_all = lax.all_gather(
        jnp.concatenate([cotangent[0], ids_own], axis=1), ("fsdp", "sp"), axis=0, tiled=True
    )
    ids_all = cot_all[:, width : width + TOPK].astype(jnp.int32)
    rank, live = route_plan(ids_all, tok_rows, sp_count)
    slots = 2 * tok_rows * TOPK // EXPERTS

    attn_normed, attn_pull = jax.vjp(rms_scale, hidden_in, gain_attn)
    n_hi, n_lo, n_x, n_core = mesh_counts(sp_count, fs_count)
    attn_in, out_mat = gather_two(
        attn_normed.astype(jnp.bfloat16), w_out, (n_hi, n_lo, 1, 1), (1, 1, n_x, n_core),
        4 if tok_rows % 64 == 0 else 2, 1, "gather_attn_in",
    )
    qkv_raw = jnp.dot(attn_in, qkv_mat, preferred_element_type=jnp.float32)
    raw = (qkv_raw[:, :span], qkv_raw[:, span : 2 * span])
    value_heads = qkv_raw[:, 2 * span :].astype(jnp.bfloat16)
    squares = sum_over_sp([jnp.sum(r * r, axis=-1) for r in raw], sp_count, 7, "sum_squares")
    scales = lax.rsqrt(squares / width + eps)[:, :, None]
    cosine, sine = rope_tables(jnp.arange(seq_rows, dtype=jnp.int32), HEAD_DIM)

    def turned(normed):
        return rotate_pairs(
            normed.reshape(seq_rows, head_local, HEAD_DIM), cosine, sine
        ).reshape(seq_rows, span)

    query_heads = turned(raw[0] * scales[0] * gain_query).astype(jnp.bfloat16)
    key_heads = turned(raw[1] * scales[1] * gain_key).astype(jnp.bfloat16)
    attended_heads, attend_back = attend(query_heads, key_heads, value_heads, doc_lengths[0])
    attended_tok = lax.all_to_all(
        attended_heads, "sp", split_axis=0, concat_axis=1, tiled=True
    )
    after_attn = hidden_in + jnp.dot(attended_tok, out_mat, preferred_element_type=jnp.float32)
    ffn_normed, ffn_pull = jax.vjp(rms_scale, after_attn, gain_ffn)
    ffn_in = ffn_normed.astype(jnp.bfloat16)
    logits = jnp.dot(ffn_in, router_mat, preferred_element_type=jnp.float32)
    router = jax.nn.softmax(logits, axis=-1)
    router_high = router.astype(jnp.bfloat16)
    router_low = (router - router_high.astype(jnp.float32)).astype(jnp.bfloat16)
    ffn_rows, cot_rows = gather_and_dispatch(
        jnp.concatenate([ffn_in, router_high, router_low], axis=1),
        cot_all, width, rank, slots, sp_count, fs_count, 2, "gather_ffn_in",
    )
    in_grad_rows, out_rows, *inner_grads = run_experts(
        ffn_rows, cot_rows, w_gate, w_up, w_down, live, first_expert[None]
    )
    in_grad_sum = combine_and_scatter(
        in_grad_rows, rank, slots, sp_count, fs_count, 3, "scatter_grads"
    )
    moe_sum = combine_and_scatter(out_rows, rank, slots, sp_count, fs_count, 4, "scatter_outputs")
    mixed = (after_attn + moe_sum).astype(jnp.bfloat16)
    upstream = cotangent[0].astype(jnp.float32)
    ffn_in_grad = in_grad_sum[:, :width]
    router_grad = in_grad_sum[:, width : width + EXPERTS]
    logit_grad = (
        router * (router_grad - jnp.sum(router * router_grad, axis=-1, keepdims=True))
    ).astype(jnp.bfloat16)
    ffn_in_grad = ffn_in_grad + jnp.dot(
        logit_grad, router_mat.T, preferred_element_type=jnp.float32
    )
    ffn_hidden_grad, ffn_gain_term = ffn_pull(ffn_in_grad)
    after_grad = upstream + ffn_hidden_grad
    attn_out_grad = after_grad.astype(jnp.bfloat16)
    attended_grad = jnp.dot(attn_out_grad, out_mat.T, preferred_element_type=jnp.float32).astype(
        jnp.bfloat16
    )
    attended_grad_heads = lax.all_to_all(
        attended_grad, "sp", split_axis=1, concat_axis=0, tiled=True
    )
    row_terms = lax.dot_general(
        jnp.concatenate([attended_tok, ffn_in], axis=0),
        jnp.concatenate(
            [
                jnp.pad(attn_out_grad, ((0, 0), (0, LANES))),
                jnp.pad(logit_grad, ((0, 0), (width, LANES - EXPERTS))),
            ],
            axis=0,
        ),
        (((0,), (0,)), ((), ())),
        preferred_element_type=jnp.float32,
    ).astype(jnp.bfloat16)
    row_sums = scatter_over_all(
        row_terms, width // (sp_count * fs_count), sp_count, fs_count, 5, "scatter_out_rows"
    )
    attended_grad_heads, row_sums = lax.optimization_barrier((attended_grad_heads, row_sums))
    rows_every = lax.all_gather(row_sums.astype(jnp.bfloat16), "sp", axis=0, tiled=True)
    query_grad_heads, key_grad_heads, value_low = attend_back(attended_grad_heads)

    def unturned(grad):
        shaped = grad.astype(jnp.float32).reshape(seq_rows, head_local, HEAD_DIM)
        return rotate_pairs(shaped, cosine, -sine).reshape(seq_rows, span)

    normed_grads = (unturned(query_grad_heads), unturned(key_grad_heads))
    scaled_grads = (normed_grads[0] * gain_query, normed_grads[1] * gain_key)
    products = sum_over_sp(
        [jnp.sum(g * r, axis=-1) for g, r in zip(scaled_grads, raw)], sp_count, 8, "sum_products"
    )[:, :, None]
    gain_terms = [
        jnp.sum(g * r * s, axis=0) for g, r, s in zip(normed_grads, raw, scales)
    ]
    raw_grads = [
        (g * s - r * (s * s * s) * (p / width)).astype(jnp.bfloat16)
        for g, r, s, p in zip(scaled_grads, raw, scales, products)
    ]
    qkv_low = jnp.concatenate(raw_grads + [value_low], axis=1)
    qkv_term = jnp.dot(attn_in.T, qkv_low, preferred_element_type=jnp.float32)
    qkv_sums = scatter_over_fsdp(
        qkv_term.astype(jnp.bfloat16), width // fs_count, fs_count, 11, "scatter_qkv"
    ).astype(jnp.bfloat16)
    qkv_every = lax.all_gather(qkv_sums, "sp", axis=0)
    attn_partial = lax.dot_general(
        qkv_low, qkv_mat, (((1,), (1,)), ((), ())), preferred_element_type=jnp.float32
    ).astype(jnp.bfloat16)
    attn_in_grad, grad_gate, grad_up, grad_down = scatter_and_grads(
        attn_partial.reshape(1, 1, n_hi, n_lo, tok_rows, width), (n_hi, n_lo, 1, 1),
        4 if tok_rows % 64 == 0 else 2, ffn_rows, cot_rows, inner_grads, 6, "scatter_attn_in",
    )
    attn_hidden_grad, attn_gain_term = attn_pull(attn_in_grad)
    grad_tokens = after_grad + attn_hidden_grad
    dense = [
        qkv_every[:, :, k * span : (k + 1) * span]
        .transpose(1, 0, 2)
        .reshape(-1, width)
        .astype(jnp.float32)
        for k in range(3)
    ]
    placed = [
        lax.dynamic_update_slice_in_dim(jnp.zeros((width,), jnp.float32), g, my_sp * span, 0)
        for g in gain_terms
    ]
    gain_sums = small_sum(
        jnp.stack([attn_gain_term, placed[0], placed[1], ffn_gain_term]).reshape(-1, 128),
        sp_count, fs_count, 9, "sum_gains",
    ).reshape(4, width)
    gain_sums = lax.dynamic_slice_in_dim(
        gain_sums, my_fs * (width // fs_count), width // fs_count, axis=1
    )
    return (
        mixed[None],
        grad_tokens[None],
        gain_sums[0],
        gain_sums[1],
        gain_sums[2],
        gain_sums[3],
        dense[0],
        dense[1],
        dense[2],
        rows_every[:, :width].astype(jnp.float32),
        rows_every[:, width : width + EXPERTS].astype(jnp.float32),
        grad_gate,
        grad_up,
        grad_down,
    )


def solution(mesh):
    in_specs = (
        P("fsdp", "sp", None),
        P("fsdp", None),
        P("fsdp", "sp", None),
        P("fsdp"),
        P("fsdp"),
        P("fsdp"),
        P("fsdp"),
        P("fsdp", None),
        P("fsdp", None),
        P("fsdp", None),
        P("fsdp", None),
        P("fsdp", None),
        P("sp", None, "fsdp"),
        P("sp", None, "fsdp"),
        P("sp", None, "fsdp"),
        P("fsdp", "sp", None),
    )
    out_specs = (
        P("fsdp", "sp", None),
        P("fsdp", "sp", None),
        P("fsdp"),
        P("fsdp"),
        P("fsdp"),
        P("fsdp"),
        P("fsdp", None),
        P("fsdp", None),
        P("fsdp", None),
        P("fsdp", None),
        P("fsdp", None),
        P("sp", None, "fsdp"),
        P("sp", None, "fsdp"),
        P("sp", None, "fsdp"),
    )
    return jax.shard_map(local, mesh=mesh, in_specs=in_specs, out_specs=out_specs, check_vma=False)
```

```python
import functools

import jax
import jax.numpy as jnp
from jax import lax
from jax.experimental import pallas as pl
from jax.experimental.pallas import tpu as pltpu
from jax.sharding import PartitionSpec as P

HEADS = 16
HEAD_DIM = 128
EXPERTS = 64
TOPK = 8
WINDOW = 1024


eps = 1e-05
rope_base = 10000.0
masked_score = -1e30


def rms_scale(values, gain_vec):
    return values * lax.rsqrt(jnp.mean(values * values, axis=-1, keepdims=True) + eps) * gain_vec


def rotate_pairs(values, cosine, sine):
    half_dim = values.shape[-1] // 2
    turned = jnp.concatenate([-values[..., half_dim:], values[..., :half_dim]], axis=-1)
    return values * cosine + turned * sine


def rope_tables(positions, head_size):
    inv_freq = rope_base ** (-jnp.arange(0, head_size, 2, dtype=jnp.float32) / head_size)
    phase_half = positions.astype(jnp.float32)[:, None] * inv_freq[None, :]
    phase_all = jnp.concatenate([phase_half, phase_half], axis=-1)
    return (jnp.cos(phase_all)[:, None, :], jnp.sin(phase_all)[:, None, :])


TILE = 1024
LANES = 128


def route_plan(ids, block, sp_count):
    local_experts = EXPERTS // sp_count
    blocks = ids.shape[0] // block
    capacity = 5 * ids.shape[0] * TOPK // (4 * EXPERTS)
    first = lax.axis_index("sp") * local_experts
    mine = first + jnp.arange(local_experts, dtype=jnp.int32)
    named = jnp.any(ids[:, None, :] == mine[None, :, None], axis=-1)
    named = named.reshape(blocks, block, local_experts)
    upto = (jnp.arange(block)[:, None] >= jnp.arange(block)[None, :]).astype(jnp.bfloat16)
    running = jnp.einsum(
        "ts,bse->bte", upto, named.astype(jnp.bfloat16), preferred_element_type=jnp.float32
    ).astype(jnp.int32)
    before = (jnp.arange(blocks)[:, None] > jnp.arange(blocks)[None, :]).astype(jnp.float32)
    earlier = jnp.dot(
        before, running[:, -1].astype(jnp.float32), precision=lax.Precision.HIGHEST
    ).astype(jnp.int32)
    keep = named & (earlier[:, None, :] + running - 1 < capacity)
    rank = jnp.where(keep, running - 1, -1).transpose(0, 2, 1)
    slots = 2 * block * TOPK // EXPERTS
    some = jnp.any(keep, axis=1).reshape(-1, TILE // slots, local_experts)
    live = jnp.any(some, axis=1).astype(jnp.int32).T.reshape(-1)
    return rank, live


def pick_matrix(rank, slots):
    experts, block = rank.shape
    slot = lax.broadcasted_iota(jnp.int32, (slots, block), 0)
    return jnp.concatenate(
        [(slot == rank[e : e + 1, :]).astype(jnp.bfloat16) for e in range(experts)], axis=0
    )


def column_spans(width):
    return [(done, min(512, width - done)) for done in range(0, width, 512)]


def contract(left, right, left_dim, right_dim):
    return lax.dot_general(
        left, right, (((left_dim,), (right_dim,)), ((), ())), preferred_element_type=jnp.float32
    )


def expert_kernel(
    live, first, x_ref, c_ref, gate_ref, up_ref, down_ref, dx_ref, y_ref, dgate_ref, dup_ref,
    act_ref,
):
    e = pl.program_id(0)
    t = pl.program_id(1)
    width = c_ref.shape[2]

    @pl.when(live[e * pl.num_programs(1) + t] == 0)
    def _():
        for ref in (dx_ref, y_ref, dgate_ref, dup_ref, act_ref):
            ref[...] = jnp.zeros_like(ref)

    @pl.when(live[e * pl.num_programs(1) + t] > 0)
    def _():
        x = x_ref[0, :, 0:width]
        gate_mat = gate_ref[0]
        up_mat = up_ref[0]
        down_mat = down_ref[0]
        column = lax.broadcasted_iota(jnp.int32, (TILE, LANES), 1)
        mine = lax.rem(column, EXPERTS) == first[0] + e
        gates = jnp.where(mine, x_ref[0, :, width : width + LANES].astype(jnp.float32), 0.0)
        weight = jnp.sum(gates, axis=1, keepdims=True)
        gate_pre = jnp.dot(x, gate_mat, preferred_element_type=jnp.float32)
        up_pre = jnp.dot(x, up_mat, preferred_element_type=jnp.float32)
        up_act = jnp.dot(c_ref[0], down_mat, preferred_element_type=jnp.float32)
        sig = 1.0 / (1.0 + jnp.exp(-gate_pre))
        silu = gate_pre * sig
        act = silu * up_pre
        gate_grad = jnp.sum(up_act * act, axis=1, keepdims=True)
        act_low = (act * weight).astype(jnp.bfloat16)
        act_grad = up_act * weight
        dgate = (act_grad * up_pre * sig * (1.0 + gate_pre * (1.0 - sig))).astype(jnp.bfloat16)
        dup = (act_grad * silu).astype(jnp.bfloat16)
        act_ref[0] = act_low
        dgate_ref[0] = dgate
        dup_ref[0] = dup
        y_ref[0] = contract(act_low, down_mat, 1, 1).astype(jnp.bfloat16)
        dx_ref[0, :, 0:width] = (
            contract(dgate, gate_mat, 1, 1) + contract(dup, up_mat, 1, 1)
        ).astype(jnp.bfloat16)
        dx_ref[0, :, width : width + LANES] = jnp.where(
            column == first[0] + e, gate_grad, 0.0
        ).astype(jnp.bfloat16)


def run_experts(x_rows, c_rows, w_gate, w_up, w_down, live, first):
    experts, rows, width = c_rows.shape
    hidden = w_gate.shape[2]

    def tile_map(e, t, live, first):
        return (e, t, 0)

    mat = pl.BlockSpec((1, width, hidden), lambda e, t, live, first: (e, 0, 0))
    wide = pl.BlockSpec((1, TILE, width + LANES), tile_map)
    plain = pl.BlockSpec((1, TILE, width), tile_map)
    inner = pl.BlockSpec((1, TILE, hidden), tile_map)
    b16 = jnp.bfloat16
    return pl.pallas_call(
        expert_kernel,
        grid_spec=pltpu.PrefetchScalarGridSpec(
            num_scalar_prefetch=2,
            grid=(experts, rows // TILE),
            in_specs=[wide, plain, mat, mat, mat],
            out_specs=[wide, plain, inner, inner, inner],
        ),
        out_shape=[
            jax.ShapeDtypeStruct(x_rows.shape, b16),
            jax.ShapeDtypeStruct(c_rows.shape, b16),
        ]
        + [jax.ShapeDtypeStruct((experts, rows, hidden), b16)] * 3,
        compiler_params=pltpu.CompilerParams(
            dimension_semantics=("arbitrary", "arbitrary"), vmem_limit_bytes=60 * 2**20
        ),
        cost_estimate=pl.CostEstimate(
            flops=12 * experts * rows * width * hidden,
            bytes_accessed=8 * experts * rows * width,
            transcendentals=experts * rows * hidden,
        ),
        name="experts",
    )(live, first, x_rows, c_rows, w_gate, w_up, w_down)


MESH = pl.DeviceIdType.MESH


class Place:
    def __init__(self, counts, fsdp_too):
        self.n_hi, self.n_lo, self.n_x, self.n_core = counts
        sp = lax.axis_index("sp")
        self.hi, self.lo = sp // self.n_lo, sp % self.n_lo
        if fsdp_too:
            fs = lax.axis_index("fsdp")
            self.x, self.core = fs // self.n_core, fs % self.n_core
        else:
            self.x, self.core = 0, 0

    def peer(self, dim, ahead):
        if dim == "core":
            return {"fsdp": self.x * self.n_core + (self.core + ahead) % self.n_core}
        if dim == "x":
            return {"fsdp": (self.x + ahead) % self.n_x * self.n_core + self.core}
        if dim == "lo":
            return {"sp": self.hi * self.n_lo + (self.lo + ahead) % self.n_lo}
        return {"sp": (self.hi + ahead) % self.n_hi * self.n_lo + self.lo}

    def sizes(self):
        return {"core": self.n_core, "x": self.n_x, "lo": self.n_lo, "hi": self.n_hi}

    def meet(self, other=None):
        barrier = pltpu.get_barrier_semaphore()
        met = 0
        for dim, size in self.sizes().items():
            for ahead in range(1, size):
                pl.semaphore_signal(
                    barrier, inc=1, device_id=self.peer(dim, ahead), device_id_type=MESH
                )
                met += 1
        for dim in ("x", "core") if other is not None else ():
            for ahead in range(1, other.sizes()[dim]):
                pl.semaphore_signal(
                    barrier, inc=1, device_id=other.peer(dim, ahead), device_id_type=MESH
                )
                met += 1
        pl.semaphore_wait(barrier, met)


def mesh_counts(sp_count, fs_count):
    low = 2
    while low * low < sp_count // 2:
        low *= 2
    low = min(low, sp_count)
    core = 2 if fs_count % 2 == 0 else 1
    return sp_count // low, low, fs_count // core, core


def scatter_kernel(
    counts, parts, fsdp_too, part_ref, out_ref, own, buf, first, second, third, own_sem, s0, r0,
    s1, r1, s2, r2, s3, r3, host=None, side=None,
):
    at = Place(counts, fsdp_too)
    n_hi, n_lo, n_x, n_core = counts
    rows = out_ref.shape[0] // parts
    pairs = parts // 2
    steps = n_hi * pairs
    lag = 1
    orders = [[d for d in o if at.sizes()[d] > 1] for o in (("x", "lo"), ("lo", "x"))]

    def remote(src, dst, send, recv, dim, ahead):
        return pltpu.make_async_remote_copy(
            src_ref=src, dst_ref=dst, send_sem=send, recv_sem=recv,
            device_id=at.peer(dim, ahead), device_id_type=MESH,
        )

    def where(t, v):
        return (at.hi + 1 + t // pairs) % n_hi, t % pairs * 2 + v

    def mine(t, v, core):
        hi, q = where(t, v)
        cut = pl.ds(pl.multiple_of(q * rows, 16), rows)
        if host is not None:
            return host.part.at[t // pairs % 2, :, core, :, cut, :]
        return part_ref.at[:, core, hi, :, cut, :]

    def load_own(t, v):
        place = own.at[t % 2, v] if n_core > 1 else buf.at[2 * t + v]
        return pltpu.make_async_copy(mine(t, v, at.core), place, own_sem.at[t % 2, v])

    def core_copy(t, v):
        return remote(
            mine(t, v, (at.core + 1) % 2), buf.at[2 * t + v], s0.at[2 * t + v], r0.at[2 * t + v],
            "core", 1,
        )

    def mid_copy(t, v, stage, ahead):
        u = 2 * t + v
        dim = orders[v][stage]
        size = at.sizes()[dim]
        to = ((at.x if dim == "x" else at.lo) + ahead) % size
        if stage == 0:
            src = buf.at[u, to] if dim == "x" else buf.at[u, :, to]
            dst = first.at[u, size - ahead - 1, pl.ds(0, n_lo if dim == "x" else n_x)]
            return remote(
                src, dst, s1.at[u, ahead - 1], r1.at[u, size - ahead - 1], dim, ahead
            )
        return remote(
            first.at[u, 0, to], second.at[u, size - ahead - 1],
            s2.at[u, ahead - 1], r2.at[u, size - ahead - 1], dim, ahead,
        )

    def wait_in(t, v, stage):
        size = at.sizes()[orders[v][stage]]
        for ahead in range(1, size):
            mid_copy(t, v, stage, ahead).wait_recv()

    def start_out(t, v, stage):
        size = at.sizes()[orders[v][stage]]
        for ahead in range(1, size):
            mid_copy(t, v, stage, ahead).start()

    def wide(ref):
        return ref[...].astype(jnp.float32)

    def result(t, v):
        u = 2 * t + v
        if len(orders[v]) == 2:
            return second.at[u, 0]
        if len(orders[v]) == 1:
            return first.at[u, 0, 0]
        return buf.at[u, 0, 0]

    def last_copy(t, v, ahead):
        _, q = where(t, v)
        return remote(
            result(t, v), third.at[n_hi - ahead - 1, q],
            s3.at[2 * t + v], r3.at[n_hi - ahead - 1, q], "hi", ahead,
        )

    def send_last(t, v):
        for k in range(n_hi - 1):

            @pl.when(t // pairs == k)
            def _(k=k):
                last_copy(t, v, k + 1).start()

    def stage_core(t, v):
        u = 2 * t + v
        if host is None:
            load_own(t, v).wait()
            own_part = own.at[t % 2, v]
        else:
            own_part = mine(t, v, at.core)
        if n_core > 1:
            core_copy(t, v).wait_recv()

            @pl.loop(0, n_x * n_lo)
            def _(j):
                x, lo = j // n_lo, j % n_lo
                place = buf.at[u, x, lo]
                place[...] = (wide(place) + wide(own_part.at[x, lo])).astype(jnp.bfloat16)

        if orders[v]:
            start_out(t, v, 0)
        else:
            send_last(t, v)

    def stage_mid(t, v, stage):
        u = 2 * t + v
        wait_in(t, v, stage)
        dim = orders[v][stage]
        size = at.sizes()[dim]
        if stage == 0:
            keep = n_lo if dim == "x" else n_x

            @pl.loop(0, keep)
            def _(j):
                base = buf.at[u, at.x, j] if dim == "x" else buf.at[u, j, at.lo]
                total = wide(base)
                for s in range(size - 1):
                    total = total + wide(first.at[u, s, j])
                first.at[u, 0, j][...] = total.astype(jnp.bfloat16)

        else:
            base = first.at[u, 0, at.x if dim == "x" else at.lo]
            total = wide(base)
            for s in range(size - 1):
                total = total + wide(second.at[u, s])
            second.at[u, 0][...] = total.astype(jnp.bfloat16)
        if stage + 1 < len(orders[v]):
            start_out(t, v, stage + 1)
        else:
            send_last(t, v)

    def each_core_copy(group, act):
        @pl.loop(0, pairs)
        def _(g):
            for v in range(2):
                act(core_copy(group * pairs + g, v))

    def make_group(group, piece, pieces):
        host.run(at, (at.hi + 1 + group) % n_hi, group % 2, piece, pieces)

    at.meet()
    if host is not None:
        make_group(0, 0, 2)
        each_core_copy(0, lambda c: c.start())
        make_group(0, 1, 2)
    else:
        if n_core > 1:

            @pl.loop(0, n_hi)
            def _(group):
                each_core_copy(group, lambda c: c.start())

        for v in range(2):
            load_own(0, v).start()

    depth = len(orders[0])

    @pl.loop(0, steps + depth * lag)
    def _(t):
        if host is None:

            @pl.when(t + 1 < steps)
            def _():
                for v in range(2):
                    load_own(t + 1, v).start()

        @pl.when(t < steps)
        def _():
            for v in range(2):
                stage_core(t, v)

        for stage in range(depth):
            back = (stage + 1) * lag

            @pl.when((t >= back) & (t < steps + back))
            def _(stage=stage, back=back):
                for v in range(2):
                    stage_mid(t - back, v, stage)

        if host is not None:

            @pl.when(t + pairs < steps)
            def _():
                group = t // pairs + 1

                @pl.when((t % pairs == 0) & (group >= 2))
                def _():
                    each_core_copy(group - 2, lambda c: c.wait_send())

                make_group(group, t % pairs, pairs)

                @pl.when(t % pairs == (pairs + 1) // 2 - 1)
                def _():
                    each_core_copy(group, lambda c: c.start())

        if side is not None:
            side.share(t, steps + depth * lag)

    for g in range(pairs):
        t = (n_hi - 1) * pairs + g
        for v in range(2):
            q = g * 2 + v
            total = wide(result(t, v))
            for s in range(n_hi - 1):
                last_copy(g, v, n_hi - 1 - s).wait_recv()
                total = total + wide(third.at[s, q])
            out_ref[pl.ds(q * rows, rows), :] = total.astype(out_ref.dtype)

    @pl.loop(0, steps)
    def _(t):
        for v in range(2):
            if host is None and n_core > 1:
                core_copy(t, v).wait_send()
            for stage in range(depth):
                for ahead in range(1, at.sizes()[orders[v][stage]]):
                    mid_copy(t, v, stage, ahead).wait_send()

            @pl.when(t // pairs < n_hi - 1)
            def _(v=v):
                last_copy(t, v, 1).wait_send()

    if host is not None:
        for group in range(max(n_hi - 2, 0), n_hi):
            each_core_copy(group, lambda c: c.wait_send())


class WeightGrads:
    def __init__(self, rows, grads, outs, row_bufs, grad_buf, acc, stage, in_sems, out_sems):
        self.rows, self.grads, self.outs = rows, grads, outs
        self.row_bufs, self.grad_buf, self.acc, self.stage = row_bufs, grad_buf, acc, stage
        self.in_sems, self.out_sems = in_sems, out_sems
        experts, total, _ = grads[0].shape
        self.depth = grad_buf.shape[2]
        self.each = total // self.depth
        self.jobs = experts * self.each

    def loads(self, j, slot):
        e = j // self.each
        rows = pl.ds(pl.multiple_of(j % self.each * self.depth, self.depth), self.depth)
        copies = []
        for k in range(2):
            width = self.row_bufs[k].shape[2]
            copies.append(
                pltpu.make_async_copy(
                    self.rows[k].at[e, rows, pl.ds(0, width)], self.row_bufs[k].at[slot],
                    self.in_sems.at[slot, k],
                )
            )
        for k in range(3):
            copies.append(
                pltpu.make_async_copy(
                    self.grads[k].at[e, rows], self.grad_buf.at[slot, k],
                    self.in_sems.at[slot, 2 + k],
                )
            )
        return copies

    def stores(self, e):
        return [
            pltpu.make_async_copy(self.stage.at[k], self.outs[k].at[e], self.out_sems.at[k])
            for k in range(3)
        ]

    def begin(self):
        for copy in self.loads(0, 0):
            copy.start()

    def share(self, t, turns):
        count = -(-self.jobs // turns)

        @pl.loop(0, count)
        def _(i):
            j = t * count + i

            @pl.when(j < self.jobs)
            def _():
                self.job(j)

    def job(self, j):
        slot = j % 2

        @pl.when(j + 1 < self.jobs)
        def _():
            for copy in self.loads(j + 1, 1 - slot):
                copy.start()

        for copy in self.loads(j, slot):
            copy.wait()

        @pl.when(j % self.each == 0)
        def _():
            self.acc[...] = jnp.zeros_like(self.acc)

        for k in range(3):
            rows = self.row_bufs[0 if k < 2 else 1]
            for start, size in column_spans(rows.shape[2]):
                cols = pl.ds(start, size)
                self.acc[k, :, cols] += contract(
                    self.grad_buf[slot, k], rows[slot, :, cols], 0, 0
                )

        @pl.when(j % self.each == self.each - 1)
        def _():
            e = j // self.each

            @pl.when(e > 0)
            def _():
                for copy in self.stores(e - 1):
                    copy.wait()

            for k in range(3):
                self.stage[k] = self.acc[k].T
            for copy in self.stores(e):
                copy.start()

    def finish(self):
        for copy in self.stores(self.jobs // self.each - 1):
            copy.wait()


def scatter_grads_kernel(
    counts, parts, part_ref, x_ref, c_ref, dgate_ref, dup_ref, act_ref, out_ref, gg_ref, gu_ref,
    gd_ref, x_buf, c_buf, grad_buf, acc, stage, in_sems, out_sems, own, *scratch,
):
    side = WeightGrads(
        (x_ref, c_ref), (dgate_ref, dup_ref, act_ref), (gg_ref, gu_ref, gd_ref), (x_buf, c_buf),
        grad_buf, acc, stage, in_sems, out_sems,
    )
    side.begin()
    scatter_kernel(counts, parts, False, part_ref, out_ref, own, *scratch, side=side)
    side.finish()


def scatter_and_grads(partial, counts, parts, x_rows, c_rows, grads, ident, name):
    n_hi, n_lo, n_x, n_core = counts
    rows, width = partial.shape[4:]
    experts, slots, hidden = grads[0].shape
    depth = 512
    b16 = jnp.bfloat16
    anywhere = pl.BlockSpec(memory_space=pl.ANY)
    weight = jax.ShapeDtypeStruct((experts, width, hidden), jnp.float32)
    return pl.pallas_call(
        functools.partial(scatter_grads_kernel, counts, parts),
        in_specs=[anywhere] * 6,
        out_specs=[pl.BlockSpec(memory_space=pltpu.VMEM)] + [anywhere] * 3,
        out_shape=[jax.ShapeDtypeStruct((rows, width), jnp.float32)] + [weight] * 3,
        scratch_shapes=[
            pltpu.VMEM((2, depth, width), b16),
            pltpu.VMEM((2, depth, width), b16),
            pltpu.VMEM((2, 3, depth, hidden), b16),
            pltpu.VMEM((3, hidden, width), jnp.float32),
            pltpu.VMEM((3, width, hidden), jnp.float32),
            pltpu.SemaphoreType.DMA((2, 5)),
            pltpu.SemaphoreType.DMA((3,)),
            pltpu.VMEM((1, 1, 1, 1, 16, 128), b16),
        ]
        + scatter_scratch(counts, parts, rows // parts, width),
        compiler_params=pltpu.CompilerParams(
            collective_id=ident, has_side_effects=True, vmem_limit_bytes=60 * 2**20
        ),
        cost_estimate=pl.CostEstimate(
            flops=6 * experts * slots * width * hidden,
            bytes_accessed=4 * experts * slots * width,
            transcendentals=0,
        ),
        name=name,
    )(partial, x_rows, c_rows, *grads)


class Combine:
    def __init__(self, rows_ref, rank_ref, part, held, sems, counts):
        self.rows_ref, self.rank_ref, self.part, self.held, self.sems = (
            rows_ref, rank_ref, part, held, sems,
        )
        self.n_hi, self.n_lo, self.n_x, self.n_core = counts

    def run(self, at, hi, slot, piece, pieces):
        total = self.n_x * self.n_core * self.n_lo
        count = total // pieces
        _, experts, slots, width = self.held.shape

        def spot(j):
            j = piece * count + j
            core = (at.core + 1 + j // (self.n_x * self.n_lo)) % self.n_core
            return j // self.n_lo % self.n_x, core, j % self.n_lo

        def block(j):
            x, core, lo = spot(j)
            return ((x * self.n_core + core) * self.n_hi + hi) * self.n_lo + lo

        def load(j, place):
            return pltpu.make_async_copy(
                self.rows_ref.at[:, block(j)], self.held.at[place], self.sems.at[place]
            )

        load(0, 0).start()

        @pl.loop(0, count)
        def _(j):
            place = j % 2

            @pl.when(j + 1 < count)
            def _():
                load(j + 1, 1 - place).start()

            load(j, place).wait()
            pick = pick_matrix(self.rank_ref[block(j)], slots)
            x, core, lo = spot(j)
            for start, size in column_spans(width):
                cols = pl.ds(start, size)
                found = self.held[place, :, :, cols].reshape(experts * slots, size)
                self.part[slot, x, core, lo, :, cols] = contract(pick, found, 0, 0).astype(
                    jnp.bfloat16
                )


def combine_scatter_kernel(
    counts, parts, rows_ref, rank_ref, out_ref, part, held, held_sem, *scratch
):
    host = Combine(rows_ref, rank_ref, part, held, held_sem, counts)
    scatter_kernel(counts, parts, True, None, out_ref, None, *scratch, host=host)


def scatter_scratch(counts, parts, r, width):
    n_hi, n_lo, n_x, _ = counts
    units = n_hi * parts
    keep = max(n_x, n_lo)
    peers = max(n_x, n_lo, 2) - 1
    b16 = jnp.bfloat16
    return [
        pltpu.VMEM((units, n_x, n_lo, r, width), b16),
        pltpu.VMEM((units, peers, keep, r, width), b16),
        pltpu.VMEM((units, peers, r, width), b16),
        pltpu.VMEM((max(n_hi - 1, 1), parts, r, width), b16),
        pltpu.SemaphoreType.DMA((2, 2)),
        pltpu.SemaphoreType.DMA((units,)),
        pltpu.SemaphoreType.DMA((units,)),
        pltpu.SemaphoreType.DMA((units, peers)),
        pltpu.SemaphoreType.DMA((units, peers)),
        pltpu.SemaphoreType.DMA((units, peers)),
        pltpu.SemaphoreType.DMA((units, peers)),
        pltpu.SemaphoreType.DMA((units,)),
        pltpu.SemaphoreType.DMA((max(n_hi - 1, 1), parts)),
    ]


def scatter_bytes(counts, parts, rows, width):
    n_hi, n_lo, n_x, _ = counts
    keep = max(n_x, n_lo)
    peers = max(n_x, n_lo, 2) - 1
    held = n_hi * (n_x * n_lo + peers * keep + peers) + max(n_hi - 1, 1)
    return (2 * held + 4) * rows * width


VMEM_ROOM = 58 * 2**20


def combine_sum(rows, rank, counts, parts, slots, ident, name):
    blocks, experts, block = rank.shape
    width = rows.shape[-1]
    _, n_lo, n_x, n_core = counts
    b16 = jnp.bfloat16
    return pl.pallas_call(
        functools.partial(combine_scatter_kernel, counts, parts),
        in_specs=[pl.BlockSpec(memory_space=pl.ANY), pl.BlockSpec(memory_space=pltpu.VMEM)],
        out_specs=pl.BlockSpec(memory_space=pltpu.VMEM),
        out_shape=jax.ShapeDtypeStruct((block, width), jnp.float32),
        scratch_shapes=[
            pltpu.VMEM((2, n_x, n_core, n_lo, block, width), b16),
            pltpu.VMEM((2, experts, slots, width), b16),
            pltpu.SemaphoreType.DMA((2,)),
        ]
        + scatter_scratch(counts, parts, block // parts, width),
        compiler_params=pltpu.CompilerParams(
            collective_id=ident, has_side_effects=True, vmem_limit_bytes=62 * 2**20
        ),
        cost_estimate=pl.CostEstimate(
            flops=2 * blocks * experts * slots * block * width,
            bytes_accessed=4 * blocks * block * width,
            transcendentals=0,
        ),
        name=name,
    )(rows.reshape(experts, blocks, slots, width), rank)


def scatter_sum(partial, counts, fsdp_too, parts, out_dtype, ident, name):
    _, n_lo, n_x, n_core = counts
    rows, width = partial.shape[4:]
    r = rows // parts
    own_shape = (2, 2, n_x, n_lo, r, width) if n_core > 1 else (1, 1, 1, 1, 16, 128)
    scratch = [pltpu.VMEM(own_shape, jnp.bfloat16)] + scatter_scratch(counts, parts, r, width)
    return pl.pallas_call(
        functools.partial(scatter_kernel, counts, parts, fsdp_too),
        in_specs=[pl.BlockSpec(memory_space=pl.ANY)],
        out_specs=pl.BlockSpec(memory_space=pltpu.VMEM),
        out_shape=jax.ShapeDtypeStruct((rows, width), out_dtype),
        scratch_shapes=scratch,
        compiler_params=pltpu.CompilerParams(
            collective_id=ident, has_side_effects=True, vmem_limit_bytes=60 * 2**20
        ),
        cost_estimate=pl.CostEstimate(
            flops=partial.size, bytes_accessed=2 * partial.size, transcendentals=0
        ),
        name=name,
    )(partial)


def gather_kernel(
    counts, parts, fsdp_too, in_ref, out_ref, own_sem, s0, r0, s1, r1, s2, r2, s3, r3, host=None,
    side=None,
):
    at = Place(counts, fsdp_too)
    n_hi, n_lo, n_x, n_core = counts
    rows = in_ref.shape[0] // parts
    pairs = parts // 2
    steps = n_hi * pairs
    orders = [[d for d in o if at.sizes()[d] > 1] for o in (("lo", "x"), ("x", "lo"))]
    depth = len(orders[0])

    def remote(src, dst, send, recv, dim, ahead):
        return pltpu.make_async_remote_copy(
            src_ref=src, dst_ref=dst, send_sem=send, recv_sem=recv,
            device_id=at.peer(dim, ahead), device_id_type=MESH,
        )

    def span(q):
        return pl.ds(pl.multiple_of(q * rows, 16), rows)

    def hi_copy(q, ahead):
        return remote(
            in_ref.at[span(q)], out_ref.at[at.x, at.core, at.hi, at.lo, span(q)],
            s0.at[ahead - 1, q], r0.at[n_hi - ahead - 1, q], "hi", ahead,
        )

    def where(t, v):
        return (at.hi + n_hi - t // pairs) % n_hi, t % pairs * 2 + v

    def mid_copy(t, v, stage, ahead):
        u = 2 * t + v
        hi, q = where(t, v)
        dim = orders[v][stage]
        size = at.sizes()[dim]
        if stage == 0:
            ref = out_ref.at[at.x, at.core, hi, at.lo, span(q)]
            if_own = in_ref.at[span(q)]
            del if_own
            return remote(
                ref, ref, s1.at[u, ahead - 1], r1.at[u, size - ahead - 1], dim, ahead
            )
        if dim == "x":
            ref = out_ref.at[at.x, at.core, hi, :, span(q)]
        else:
            ref = out_ref.at[:, at.core, hi, at.lo, span(q)]
        return remote(ref, ref, s2.at[u, ahead - 1], r2.at[u, size - ahead - 1], dim, ahead)

    def core_copy(t, v):
        u = 2 * t + v
        hi, q = where(t, v)
        ref = out_ref.at[:, at.core, hi, :, span(q)]
        return remote(ref, ref, s3.at[u], r3.at[u], "core", 1)

    def each_mid(t, v, stage, act):
        size = at.sizes()[orders[v][stage]]
        for ahead in range(1, size):
            act(mid_copy(t, v, stage, ahead))

    keep = pltpu.make_async_copy(
        in_ref, out_ref.at[at.x, at.core, at.hi, at.lo], own_sem
    )
    keep.start()
    at.meet(side.at if side is not None else None)
    if side is not None:
        side.begin()
    for ahead in range(1, n_hi):
        for q in range(parts):
            hi_copy(q, ahead).start()
    keep.wait()

    @pl.loop(0, steps + depth + (1 if host is not None and n_core > 1 else 0))
    def _(t):
        @pl.when(t < steps)
        def _():
            for v in range(2):
                _, q = where(t, v)
                for k in range(1, n_hi):

                    @pl.when(t // pairs == k)
                    def _(k=k, q=q):
                        hi_copy(q, k).wait_recv()

                if depth > 0:
                    each_mid(t, v, 0, lambda c: c.start())
                elif n_core > 1:
                    core_copy(t, v).start()

        for stage in range(depth):
            back = stage + 1

            @pl.when((t >= back) & (t < steps + back))
            def _(stage=stage, back=back):
                for v in range(2):
                    each_mid(t - back, v, stage, lambda c: c.wait_recv())
                    if stage + 1 < depth:
                        each_mid(t - back, v, stage + 1, lambda c: c.start())
                    elif n_core > 1:
                        core_copy(t - back, v).start()

        if side is not None:

            @pl.when(t == steps // 2 + 1)
            def _():
                side.middle()

        if host is not None:
            for origin_step in range(n_hi):
                done = (origin_step + 1) * pairs - 1 + depth
                hi = (at.hi + n_hi - origin_step) % n_hi

                @pl.when(t == done)
                def _(hi=hi):
                    host.blocks(at, at.core, hi)

                if n_core > 1:

                    @pl.when(t == done + 1)
                    def _(hi=hi, origin_step=origin_step):
                        for g in range(pairs):
                            for v in range(2):
                                core_copy(origin_step * pairs + g, v).wait_recv()
                        host.blocks(at, 1 - at.core, hi)

            host.others(t, steps + depth)

    @pl.loop(0, steps)
    def _(t):
        for v in range(2):
            if n_core > 1:
                if host is None:
                    core_copy(t, v).wait_recv()
                core_copy(t, v).wait_send()
            for stage in range(depth):
                each_mid(t, v, stage, lambda c: c.wait_send())

    for q in range(parts):
        for ahead in range(1, n_hi):
            hi_copy(q, ahead).wait_send()

    if side is not None:
        side.end()


class SideGather:
    def __init__(self, counts, in_ref, out_ref, own_sem, s_x, r_x, s_core, r_core):
        self.at = Place(counts, True)
        self.in_ref, self.out_ref, self.own_sem = in_ref, out_ref, own_sem
        self.s_x, self.r_x, self.s_core, self.r_core = s_x, r_x, s_core, r_core

    def own(self):
        at = self.at
        return pltpu.make_async_copy(self.in_ref, self.out_ref.at[at.x, at.core], self.own_sem)

    def x_copy(self, ahead):
        at = self.at
        return pltpu.make_async_remote_copy(
            src_ref=self.in_ref, dst_ref=self.out_ref.at[at.x, at.core],
            send_sem=self.s_x.at[ahead - 1], recv_sem=self.r_x.at[at.n_x - ahead - 1],
            device_id=at.peer("x", ahead), device_id_type=MESH,
        )

    def core_copy(self):
        ref = self.out_ref.at[:, self.at.core]
        return pltpu.make_async_remote_copy(
            src_ref=ref, dst_ref=ref, send_sem=self.s_core, recv_sem=self.r_core,
            device_id=self.at.peer("core", 1), device_id_type=MESH,
        )

    def begin(self):
        self.own().start()
        for ahead in range(1, self.at.n_x):
            self.x_copy(ahead).start()

    def middle(self):
        self.own().wait()
        for ahead in range(1, self.at.n_x):
            self.x_copy(ahead).wait_recv()
        if self.at.n_core > 1:
            self.core_copy().start()

    def end(self):
        for ahead in range(1, self.at.n_x):
            self.x_copy(ahead).wait_send()
        if self.at.n_core > 1:
            self.core_copy().wait()


def gather_two_kernel(
    counts, parts, side_counts, in_ref, side_in, out_ref, side_out, own_sem, s_x, r_x, s_core,
    r_core, *sems,
):
    side = SideGather(side_counts, side_in, side_out, own_sem, s_x, r_x, s_core, r_core)
    gather_kernel(counts, parts, False, in_ref, out_ref, *sems, side=side)


def gather_two(own, weight, counts, side_counts, parts, ident, name):
    n_hi, n_lo, _, _ = counts
    _, _, n_x, n_core = side_counts
    rows, width = own.shape
    anywhere = pl.BlockSpec(memory_space=pl.ANY)
    dma = pltpu.SemaphoreType.DMA
    out, side = pl.pallas_call(
        functools.partial(gather_two_kernel, counts, parts, side_counts),
        in_specs=[anywhere] * 2,
        out_specs=[anywhere] * 2,
        out_shape=[
            jax.ShapeDtypeStruct((1, 1, n_hi, n_lo, rows, width), own.dtype),
            jax.ShapeDtypeStruct((n_x, n_core) + weight.shape, weight.dtype),
        ],
        scratch_shapes=[dma, dma((max(n_x - 1, 1),)), dma((max(n_x - 1, 1),)), dma, dma]
        + gather_sems(counts, parts),
        compiler_params=pltpu.CompilerParams(collective_id=ident, has_side_effects=True),
        cost_estimate=pl.CostEstimate(
            flops=0, bytes_accessed=4 * n_hi * n_lo * rows * width, transcendentals=0
        ),
        name=name,
    )(own, weight)
    return out.reshape(-1, width), side.reshape(-1, weight.shape[1])


class Dispatch:
    def __init__(self, tables, rows, bufs, ins, outs, rank_ref, geometry):
        self.tables, self.rows, self.bufs, self.ins, self.outs = tables, rows, bufs, ins, outs
        self.rank_ref = rank_ref
        self.n_hi, self.n_lo, self.n_x, self.n_core = geometry

    def load(self, which, index, slot):
        held, _ = self.bufs[which]
        return pltpu.make_async_copy(
            self.tables[which].at[index + (slice(None), pl.ds(0, held.shape[2]))],
            held.at[slot], self.ins[which].at[slot],
        )

    def store(self, which, block, slot):
        _, found = self.bufs[which]
        return pltpu.make_async_copy(
            found.at[slot], self.rows[which].at[:, block], self.outs[which].at[slot]
        )

    def run(self, which, block_of, index_of, count):
        held, found = self.bufs[which]
        experts, slots, width = found.shape[1:]
        if held is not None:
            self.load(which, index_of(0), 0).start()

        @pl.loop(0, count)
        def _(j):
            slot = j % 2

            if held is not None:

                @pl.when(j + 1 < count)
                def _():
                    self.load(which, index_of(j + 1), 1 - slot).start()

            @pl.when(j >= 2)
            def _():
                self.store(which, block_of(j - 2), slot).wait()

            if held is not None:
                self.load(which, index_of(j), slot).wait()
                table = held.at[slot]
            else:
                table = self.tables[which].at[index_of(j)]
            pick = pick_matrix(self.rank_ref[block_of(j)], slots)
            for start, size in column_spans(width):
                cols = pl.ds(start, size)
                picked = jnp.dot(
                    pick, table[:, cols], preferred_element_type=jnp.float32
                ).astype(jnp.bfloat16)
                found[slot, :, :, cols] = picked.reshape(experts, slots, size)
            self.store(which, block_of(j), slot).start()

        for j in range(max(count - 2, 0), count):
            self.store(which, block_of(j), j % 2).wait()

    def blocks(self, at, core, hi):
        def spot(j):
            return j // self.n_lo, core, hi, j % self.n_lo

        def block_of(j):
            x, c, h, lo = spot(j)
            return ((x * self.n_core + c) * self.n_hi + h) * self.n_lo + lo

        self.run(0, block_of, spot, self.n_x * self.n_lo)

    def others(self, t, steps):
        total = self.n_x * self.n_core * self.n_hi * self.n_lo
        each = -(-total // steps)
        for step in range(steps):
            first = min(step * each, total)
            count = min(each, total - first)
            if count > 0:

                @pl.when(t == step)
                def _(first=first, count=count):
                    self.run(1, lambda j: first + j, lambda j: (first + j,), count)


def dispatch_kernel(
    counts, parts, in_ref, other_ref, rank_ref, rows_ref, other_rows_ref, *rest
):
    out_ref, held, found, other_held, other_found, in_sem, put_sem, other_in_sem, other_put_sem = (
        rest[:9]
    )
    sems = rest[9:]
    if len(out_ref.shape) == 6 and held.shape[0] == 1:
        held = None
    host = Dispatch(
        (out_ref, other_ref), (rows_ref, other_rows_ref),
        ((held, found), (other_held, other_found)), (in_sem, other_in_sem),
        (put_sem, other_put_sem), rank_ref, counts,
    )
    gather_kernel(counts, parts, True, in_ref, out_ref, *sems, host=host)


def gather_sems(counts, parts):
    n_hi, n_lo, n_x, n_core = counts
    units = n_hi * parts
    peers = max(n_x, n_lo, 2) - 1
    ahead = max(n_hi - 1, 1)
    sizes = [(ahead, parts)] * 2 + [(units, peers)] * 4 + [(units,)] * 2
    return [pltpu.SemaphoreType.DMA] + [pltpu.SemaphoreType.DMA(size) for size in sizes]


def gather_and_dispatch(own, other_all, other_width, rank, slots, sp_count, fs_count, ident, name):
    counts = mesh_counts(sp_count, fs_count)
    n_hi, n_lo, n_x, n_core = counts
    rows, width = own.shape
    blocks, experts, _ = rank.shape
    parts = 4 if rows % 64 == 0 else 2
    b16 = jnp.bfloat16
    anywhere = pl.BlockSpec(memory_space=pl.ANY)
    table = (n_x, n_core, n_hi, n_lo, rows, width)
    inside = 2 * blocks * rows * width <= 36 * 2**20
    scratch = [
        pltpu.VMEM((1, 16, LANES) if inside else (2, rows, width), b16),
        pltpu.VMEM((2, experts, slots, width), b16),
        pltpu.VMEM((2, rows, other_width), b16),
        pltpu.VMEM((2, experts, slots, other_width), b16),
    ] + [pltpu.SemaphoreType.DMA((2,))] * 4
    flops = 2 * blocks * experts * slots * rows * (width + other_width)
    results = [
        jax.ShapeDtypeStruct((experts, blocks, slots, width), b16),
        jax.ShapeDtypeStruct((experts, blocks, slots, other_width), b16),
    ]
    if inside:
        scratch = [pltpu.VMEM(table, b16)] + scratch
    else:
        results.append(jax.ShapeDtypeStruct(table, b16))
    picked, other_picked, *_ = pl.pallas_call(
        functools.partial(dispatch_kernel, counts, parts),
        in_specs=[anywhere, anywhere, pl.BlockSpec(memory_space=pltpu.VMEM)],
        out_specs=[anywhere] * len(results),
        out_shape=results,
        scratch_shapes=scratch + gather_sems(counts, parts),
        compiler_params=pltpu.CompilerParams(
            collective_id=ident, has_side_effects=True, vmem_limit_bytes=56 * 2**20
        ),
        cost_estimate=pl.CostEstimate(
            flops=flops, bytes_accessed=8 * blocks * rows * width, transcendentals=0
        ),
        name=name,
    )(own, other_all.reshape(blocks, rows, -1), rank)
    return picked.reshape(experts, -1, width), other_picked.reshape(experts, -1, other_width)


def gather_rows(own, counts, fsdp_too, parts, ident, name):
    n_hi, n_lo, n_x, n_core = counts
    rows, width = own.shape
    total = rows * n_hi * n_lo * n_x * n_core
    out = pl.pallas_call(
        functools.partial(gather_kernel, counts, parts, fsdp_too),
        in_specs=[pl.BlockSpec(memory_space=pl.ANY)],
        out_specs=pl.BlockSpec(memory_space=pl.ANY),
        out_shape=jax.ShapeDtypeStruct((n_x, n_core, n_hi, n_lo, rows, width), own.dtype),
        scratch_shapes=gather_sems(counts, parts),
        compiler_params=pltpu.CompilerParams(collective_id=ident, has_side_effects=True),
        cost_estimate=pl.CostEstimate(
            flops=0, bytes_accessed=4 * total * width, transcendentals=0
        ),
        name=name,
    )(own)
    return out.reshape(total, width)


def small_sum_kernel(counts, part_ref, out_ref, first, second, s0, r0, s1, r1):
    sp_count, fs_count = counts
    at = {"sp": lax.axis_index("sp"), "fsdp": lax.axis_index("fsdp")}

    def peer(dim, ahead, size):
        return {dim: (at[dim] + ahead) % size}

    barrier = pltpu.get_barrier_semaphore()
    for dim, size in (("sp", sp_count), ("fsdp", fs_count)):
        for ahead in range(1, size):
            pl.semaphore_signal(
                barrier, inc=1, device_id=peer(dim, ahead, size), device_id_type=MESH
            )
    pl.semaphore_wait(barrier, sp_count + fs_count - 2)

    def exchange(src, held, send, recv, dim, size):
        copies = [
            pltpu.make_async_remote_copy(
                src_ref=src, dst_ref=held.at[size - ahead - 1],
                send_sem=send.at[ahead - 1], recv_sem=recv.at[size - ahead - 1],
                device_id=peer(dim, ahead, size), device_id_type=MESH,
            )
            for ahead in range(1, size)
        ]
        for copy in copies:
            copy.start()
        total = src[...]
        for ahead, copy in enumerate(copies, 1):
            pltpu.make_async_remote_copy(
                src_ref=src, dst_ref=held.at[ahead - 1],
                send_sem=send.at[size - ahead - 1], recv_sem=recv.at[ahead - 1],
                device_id=peer(dim, size - ahead, size), device_id_type=MESH,
            ).wait_recv()
            total = total + held[ahead - 1]
        for copy in copies:
            copy.wait_send()
        return total

    total = exchange(part_ref, first, s0, r0, "sp", sp_count)
    out_ref[...] = total
    if fs_count > 1:
        total = exchange(out_ref, second, s1, r1, "fsdp", fs_count)
        out_ref[...] = total


def small_sum(part, sp_count, fs_count, ident, name):
    sems = [pltpu.SemaphoreType.DMA((max(n - 1, 1),)) for n in (sp_count, sp_count, fs_count, fs_count)]
    return pl.pallas_call(
        functools.partial(small_sum_kernel, (sp_count, fs_count)),
        in_specs=[pl.BlockSpec(memory_space=pltpu.VMEM)],
        out_specs=pl.BlockSpec(memory_space=pltpu.VMEM),
        out_shape=jax.ShapeDtypeStruct(part.shape, jnp.float32),
        scratch_shapes=[
            pltpu.VMEM((max(sp_count - 1, 1),) + part.shape, jnp.float32),
            pltpu.VMEM((max(fs_count - 1, 1),) + part.shape, jnp.float32),
        ]
        + sems,
        compiler_params=pltpu.CompilerParams(collective_id=ident, has_side_effects=True),
        name=name,
    )(part)


ROWS = 256


def window_scores(ends, count, q, k, first, top):
    scores = contract(q, k, 1, 1) * HEAD_DIM ** (-0.5)
    place = top + lax.broadcasted_iota(jnp.int32, (ROWS, 1), 0)
    oldest = jnp.maximum(place - (WINDOW - 1), 0)
    for n in range(count):
        oldest = jnp.maximum(oldest, jnp.where(place >= ends[n], ends[n], 0))
    other = first + lax.broadcasted_iota(jnp.int32, scores.shape, 1)
    return jnp.where((other >= oldest) & (other <= place), scores, masked_score)


def window_first(i, reach, total):
    return pl.multiple_of(jnp.clip(i * ROWS + ROWS - reach, 0, total - reach), ROWS)


def softmax_rows(scores):
    weights = jnp.exp(scores - jnp.max(scores, axis=-1, keepdims=True))
    return weights / jnp.sum(weights, axis=-1, keepdims=True)


def turn_pairs(values, cosine, sine):
    return values * cosine + pltpu.roll(values, HEAD_DIM // 2, 1) * sine


def attend_kernel(
    count, reach, ends, q_ref, k_ref, v_ref, scale_ref, gain_ref, cos_ref, sin_ref, o_ref, qo_ref,
    ko_ref, vo_ref,
):
    i = pl.program_id(1)
    first = window_first(i, reach, k_ref.shape[0])
    keys = pl.ds(first, reach)
    here = pl.ds(pl.multiple_of(i * ROWS, ROWS), ROWS)

    @pl.when(i == 0)
    def _():
        normed = k_ref[...] * scale_ref[:, 1:2] * gain_ref[1:2, :]
        ko_ref[...] = turn_pairs(normed, cos_ref[...], sin_ref[...]).astype(jnp.bfloat16)
        vo_ref[...] = v_ref[...].astype(jnp.bfloat16)

    normed = q_ref[...] * scale_ref[here, 0:1] * gain_ref[0:1, :]
    q = turn_pairs(normed, cos_ref[here, :], sin_ref[here, :]).astype(jnp.bfloat16)
    qo_ref[...] = q
    scores = window_scores(ends, count, q, ko_ref[keys, :], first, i * ROWS)
    probs = softmax_rows(scores).astype(jnp.bfloat16)
    o_ref[...] = jnp.dot(probs, vo_ref[keys, :], preferred_element_type=jnp.float32).astype(
        jnp.bfloat16
    )


def attend_back_kernel(
    count, reach, ends, q_ref, k_ref, v_ref, g_ref, cos_ref, sin_ref, dq_ref, dk_ref, dv_ref,
    dk_acc, dv_acc,
):
    i = pl.program_id(1)
    first = window_first(i, reach, k_ref.shape[0])
    keys = pl.ds(first, reach)
    here = pl.ds(pl.multiple_of(i * ROWS, ROWS), ROWS)
    scale = HEAD_DIM ** (-0.5)

    @pl.when(i == 0)
    def _():
        dk_acc[...] = jnp.zeros_like(dk_acc)
        dv_acc[...] = jnp.zeros_like(dv_acc)

    def turned_back(grad, cosine, sine):
        return turn_pairs(grad.astype(jnp.bfloat16).astype(jnp.float32), cosine, -sine)

    q = q_ref[...]
    k = k_ref[keys, :]
    grad = g_ref[...]
    probs = softmax_rows(window_scores(ends, count, q, k, first, i * ROWS))
    prob_grad = contract(grad, v_ref[keys, :], 1, 1)
    delta = jnp.sum(probs * prob_grad, axis=-1, keepdims=True)
    score_grad = (probs * (prob_grad - delta)).astype(jnp.bfloat16)
    dq = jnp.dot(score_grad, k, preferred_element_type=jnp.float32) * scale
    dq_ref[...] = turned_back(dq, cos_ref[here, :], sin_ref[here, :])
    dk_acc[keys, :] += contract(score_grad, q, 0, 0) * scale
    dv_acc[keys, :] += contract(probs.astype(jnp.bfloat16), grad, 0, 0)

    @pl.when(i == pl.num_programs(1) - 1)
    def _():
        dk_ref[...] = turned_back(dk_acc[...], cos_ref[...], sin_ref[...])
        dv_ref[...] = dv_acc[...].astype(jnp.bfloat16)


def attend(raw, scales, gains, lengths):
    seq_rows = raw.shape[0]
    span = raw.shape[1] // 3
    heads = span // HEAD_DIM
    reach = min(WINDOW + ROWS, seq_rows)
    count = lengths.shape[0]
    ends = jnp.cumsum(lengths)
    cosine, sine = rope_tables(jnp.arange(seq_rows, dtype=jnp.int32), HEAD_DIM)
    sign = jnp.where(jnp.arange(HEAD_DIM) < HEAD_DIM // 2, -1.0, 1.0)
    cosine, sine = cosine[:, 0], sine[:, 0] * sign

    def tile(group=0):
        return pl.BlockSpec((ROWS, HEAD_DIM), lambda h, i, ends: (i, group * heads + h))

    def whole(group=0):
        return pl.BlockSpec((seq_rows, HEAD_DIM), lambda h, i, ends: (0, group * heads + h))

    def fixed(array):
        return pl.BlockSpec(array.shape, lambda h, i, ends: (0, 0))

    pairs = seq_rows * heads * reach

    def call(kernel, ins, outs, types, scratch, name):
        return pl.pallas_call(
            kernel,
            grid_spec=pltpu.PrefetchScalarGridSpec(
                num_scalar_prefetch=1,
                grid=(heads, seq_rows // ROWS),
                in_specs=ins,
                out_specs=outs,
                scratch_shapes=scratch,
            ),
            out_shape=[jax.ShapeDtypeStruct((seq_rows, span), t) for t in types],
            compiler_params=pltpu.CompilerParams(
                dimension_semantics=("arbitrary", "arbitrary"), vmem_limit_bytes=56 * 2**20
            ),
            cost_estimate=pl.CostEstimate(
                flops=4 * len(outs) * pairs * HEAD_DIM,
                bytes_accessed=16 * seq_rows * span,
                transcendentals=pairs,
            ),
            name=name,
        )

    b16, f32 = jnp.bfloat16, jnp.float32
    tables = [fixed(cosine), fixed(sine)]
    row_scales = scales.T
    attended, query, key, value = call(
        functools.partial(attend_kernel, count, reach),
        [tile(0), whole(1), whole(2), fixed(row_scales)]
        + [pl.BlockSpec((2, HEAD_DIM), lambda h, i, ends: (0, h))]
        + tables,
        [tile(), tile(), whole(), whole()],
        [b16] * 4,
        [],
        "attend",
    )(ends, raw, raw, raw, row_scales, gains, cosine, sine)

    def back(grad):
        return call(
            functools.partial(attend_back_kernel, count, reach),
            [tile(), whole(), whole(), tile()] + tables,
            [tile(), whole(), whole()],
            [f32, f32, b16],
            [pltpu.VMEM((seq_rows, HEAD_DIM), f32)] * 2,
            "attend_back",
        )(ends, query, key, value, grad, cosine, sine)

    return attended, back


def scatter_over_all(partial, rows, sp_count, fs_count, ident, name):
    counts = mesh_counts(sp_count, fs_count)
    width = partial.shape[1]
    parts = 4 if rows % 64 == 0 else 2
    room = scatter_bytes(counts, parts, rows, width)
    room += 8 * counts[1] * counts[2] * rows // parts * width
    if room > VMEM_ROOM or rows % (parts * 16):
        part = lax.psum_scatter(partial, "fsdp", scatter_dimension=0, tiled=True)
        return lax.psum_scatter(part, "sp", scatter_dimension=0, tiled=True).astype(jnp.float32)
    n_hi, n_lo, n_x, n_core = counts
    shaped = partial.reshape(n_x, n_core, n_hi, n_lo, rows, width)
    return scatter_sum(shaped, counts, True, parts, jnp.float32, ident, name)


def combine_and_scatter(rows, rank, slots, sp_count, fs_count, ident, name):
    blocks, experts, block = rank.shape
    counts = mesh_counts(sp_count, fs_count)
    n_hi, n_lo, n_x, n_core = counts
    width = rows.shape[-1]
    parts = 4 if block % 64 == 0 else 2
    room = scatter_bytes(counts, parts, block, width)
    room += 4 * (n_x * n_core * n_lo * block + experts * slots) * width
    if n_core == 2 and room <= VMEM_ROOM and block % (parts * 16) == 0:
        return combine_sum(rows, rank, counts, parts, slots, ident, name)
    shaped = rows.reshape(experts, blocks, slots, -1)
    pick = (rank[:, :, None, :] == jnp.arange(slots)[None, None, :, None]).astype(jnp.bfloat16)
    partial = jnp.einsum("best,ebsw->btw", pick, shaped, preferred_element_type=jnp.float32)
    partial = partial.astype(jnp.bfloat16).reshape(blocks * block, -1)
    return scatter_over_all(partial, block, sp_count, fs_count, ident, name)


def scatter_over_fsdp(partial, rows, fs_count, ident, name):
    _, _, n_x, n_core = mesh_counts(1, fs_count)
    parts = 4 if rows % 64 == 0 else 2
    shaped = partial.reshape(n_x, n_core, 1, 1, rows, partial.shape[1])
    return scatter_sum(shaped, (1, 1, n_x, n_core), True, parts, jnp.float32, ident, name)


def gather_over_all(own, sp_count, fs_count, ident, name):
    parts = 4 if own.shape[0] % 64 == 0 else 2
    return gather_rows(own, mesh_counts(sp_count, fs_count), True, parts, ident, name)


def gather_over_sp(own, sp_count, ident, name):
    n_hi, n_lo, _, _ = mesh_counts(sp_count, 1)
    parts = 4 if own.shape[0] % 64 == 0 else 2
    return gather_rows(own, (n_hi, n_lo, 1, 1), False, parts, ident, name)


def sum_over_sp(rows, sp_count, ident, name):
    part = jnp.stack(rows)
    return small_sum(part.reshape(-1, 128), sp_count, 1, ident, name).reshape(part.shape)


def local(
    tokens,
    doc_lengths,
    expert_ids,
    norm_attn,
    norm_query,
    norm_key,
    norm_ffn,
    w_query,
    w_key,
    w_value,
    w_out,
    w_router,
    w_gate,
    w_up,
    w_down,
    cotangent,
):
    sp_count = lax.axis_size("sp")
    fs_count = lax.axis_size("fsdp")
    my_sp = lax.axis_index("sp")
    my_fs = lax.axis_index("fsdp")
    hidden_in = tokens[0].astype(jnp.float32)
    tok_rows, width = hidden_in.shape
    head_local = HEADS // sp_count
    seq_rows = tok_rows * sp_count
    span = head_local * HEAD_DIM
    expert_local = EXPERTS // sp_count
    first_expert = my_sp * expert_local
    gains = lax.all_gather(
        jnp.stack([norm_attn, norm_query, norm_key, norm_ffn]), "fsdp", axis=1, tiled=True
    ).astype(jnp.float32)
    gain_attn, gain_ffn = gains[0], gains[3]
    own_cols = lax.dynamic_slice_in_dim(gains, my_sp * span, span, axis=1)
    gain_query, gain_key = own_cols[1], own_cols[2]
    qkv_own = jnp.concatenate(
        [
            lax.dynamic_slice_in_dim(w, my_sp * span, span, axis=1)
            for w in (w_query, w_key, w_value)
        ],
        axis=1,
    )
    qkv_mat = lax.all_gather(qkv_own, "fsdp", axis=0, tiled=True)
    router_mat = lax.all_gather(w_router, "fsdp", axis=0, tiled=True)
    ids_own = jnp.pad(expert_ids[0].astype(jnp.bfloat16), ((0, 0), (0, LANES - TOPK)))
    cot_all = lax.all_gather(
        jnp.concatenate([cotangent[0], ids_own], axis=1), ("fsdp", "sp"), axis=0, tiled=True
    )
    ids_all = cot_all[:, width : width + TOPK].astype(jnp.int32)
    rank, live = route_plan(ids_all, tok_rows, sp_count)
    slots = 2 * tok_rows * TOPK // EXPERTS

    attn_normed, attn_pull = jax.vjp(rms_scale, hidden_in, gain_attn)
    n_hi, n_lo, n_x, n_core = mesh_counts(sp_count, fs_count)
    attn_in, out_mat = gather_two(
        attn_normed.astype(jnp.bfloat16), w_out, (n_hi, n_lo, 1, 1), (1, 1, n_x, n_core),
        4 if tok_rows % 64 == 0 else 2, 1, "gather_attn_in",
    )
    qkv_raw = jnp.dot(attn_in, qkv_mat, preferred_element_type=jnp.float32)
    raw = (qkv_raw[:, :span], qkv_raw[:, span : 2 * span])
    squares = sum_over_sp([jnp.sum(r * r, axis=-1) for r in raw], sp_count, 7, "sum_squares")
    scales = lax.rsqrt(squares / width + eps)
    attended_heads, attend_back = attend(qkv_raw, scales, own_cols[1:3], doc_lengths[0])
    scales = scales[:, :, None]
    attended_tok = lax.all_to_all(
        attended_heads, "sp", split_axis=0, concat_axis=1, tiled=True
    )
    after_attn = hidden_in + jnp.dot(attended_tok, out_mat, preferred_element_type=jnp.float32)
    ffn_normed, ffn_pull = jax.vjp(rms_scale, after_attn, gain_ffn)
    ffn_in = ffn_normed.astype(jnp.bfloat16)
    logits = jnp.dot(ffn_in, router_mat, preferred_element_type=jnp.float32)
    router = jax.nn.softmax(logits, axis=-1)
    router_high = router.astype(jnp.bfloat16)
    router_low = (router - router_high.astype(jnp.float32)).astype(jnp.bfloat16)
    ffn_rows, cot_rows = gather_and_dispatch(
        jnp.concatenate([ffn_in, router_high, router_low], axis=1),
        cot_all, width, rank, slots, sp_count, fs_count, 2, "gather_ffn_in",
    )
    in_grad_rows, out_rows, *inner_grads = run_experts(
        ffn_rows, cot_rows, w_gate, w_up, w_down, live, first_expert[None]
    )
    in_grad_sum = combine_and_scatter(
        in_grad_rows, rank, slots, sp_count, fs_count, 3, "scatter_grads"
    )
    moe_sum = combine_and_scatter(out_rows, rank, slots, sp_count, fs_count, 4, "scatter_outputs")
    mixed = (after_attn + moe_sum).astype(jnp.bfloat16)
    upstream = cotangent[0].astype(jnp.float32)
    ffn_in_grad = in_grad_sum[:, :width]
    router_grad = in_grad_sum[:, width : width + EXPERTS]
    logit_grad = (
        router * (router_grad - jnp.sum(router * router_grad, axis=-1, keepdims=True))
    ).astype(jnp.bfloat16)
    ffn_in_grad = ffn_in_grad + jnp.dot(
        logit_grad, router_mat.T, preferred_element_type=jnp.float32
    )
    ffn_hidden_grad, ffn_gain_term = ffn_pull(ffn_in_grad)
    after_grad = upstream + ffn_hidden_grad
    attn_out_grad = after_grad.astype(jnp.bfloat16)
    attended_grad = jnp.dot(attn_out_grad, out_mat.T, preferred_element_type=jnp.float32).astype(
        jnp.bfloat16
    )
    attended_grad_heads = lax.all_to_all(
        attended_grad, "sp", split_axis=1, concat_axis=0, tiled=True
    )
    row_terms = lax.dot_general(
        jnp.concatenate([attended_tok, ffn_in], axis=0),
        jnp.concatenate(
            [
                jnp.pad(attn_out_grad, ((0, 0), (0, LANES))),
                jnp.pad(logit_grad, ((0, 0), (width, LANES - EXPERTS))),
            ],
            axis=0,
        ),
        (((0,), (0,)), ((), ())),
        preferred_element_type=jnp.float32,
    ).astype(jnp.bfloat16)
    row_sums = scatter_over_all(
        row_terms, width // (sp_count * fs_count), sp_count, fs_count, 5, "scatter_out_rows"
    )
    attended_grad_heads, row_sums = lax.optimization_barrier((attended_grad_heads, row_sums))
    rows_every = lax.all_gather(row_sums.astype(jnp.bfloat16), "sp", axis=0, tiled=True)
    *normed_grads, value_low = attend_back(attended_grad_heads)
    scaled_grads = (normed_grads[0] * gain_query, normed_grads[1] * gain_key)
    products = sum_over_sp(
        [jnp.sum(g * r, axis=-1) for g, r in zip(scaled_grads, raw)], sp_count, 8, "sum_products"
    )[:, :, None]
    gain_terms = [
        jnp.sum(g * r * s, axis=0) for g, r, s in zip(normed_grads, raw, scales)
    ]
    raw_grads = [
        (g * s - r * (s * s * s) * (p / width)).astype(jnp.bfloat16)
        for g, r, s, p in zip(scaled_grads, raw, scales, products)
    ]
    qkv_low = jnp.concatenate(raw_grads + [value_low], axis=1)
    qkv_term = jnp.dot(attn_in.T, qkv_low, preferred_element_type=jnp.float32)
    qkv_sums = scatter_over_fsdp(
        qkv_term.astype(jnp.bfloat16), width // fs_count, fs_count, 11, "scatter_qkv"
    ).astype(jnp.bfloat16)
    qkv_every = lax.all_gather(qkv_sums, "sp", axis=0)
    attn_partial = lax.dot_general(
        qkv_low, qkv_mat, (((1,), (1,)), ((), ())), preferred_element_type=jnp.float32
    ).astype(jnp.bfloat16)
    attn_in_grad, grad_gate, grad_up, grad_down = scatter_and_grads(
        attn_partial.reshape(1, 1, n_hi, n_lo, tok_rows, width), (n_hi, n_lo, 1, 1),
        4 if tok_rows % 64 == 0 else 2, ffn_rows, cot_rows, inner_grads, 6, "scatter_attn_in",
    )
    attn_hidden_grad, attn_gain_term = attn_pull(attn_in_grad)
    grad_tokens = after_grad + attn_hidden_grad
    dense = [
        qkv_every[:, :, k * span : (k + 1) * span]
        .transpose(1, 0, 2)
        .reshape(-1, width)
        .astype(jnp.float32)
        for k in range(3)
    ]
    placed = [
        lax.dynamic_update_slice_in_dim(jnp.zeros((width,), jnp.float32), g, my_sp * span, 0)
        for g in gain_terms
    ]
    gain_sums = small_sum(
        jnp.stack([attn_gain_term, placed[0], placed[1], ffn_gain_term]).reshape(-1, 128),
        sp_count, fs_count, 9, "sum_gains",
    ).reshape(4, width)
    gain_sums = lax.dynamic_slice_in_dim(
        gain_sums, my_fs * (width // fs_count), width // fs_count, axis=1
    )
    return (
        mixed[None],
        grad_tokens[None],
        gain_sums[0],
        gain_sums[1],
        gain_sums[2],
        gain_sums[3],
        dense[0],
        dense[1],
        dense[2],
        rows_every[:, :width].astype(jnp.float32),
        rows_every[:, width : width + EXPERTS].astype(jnp.float32),
        grad_gate,
        grad_up,
        grad_down,
    )


def solution(mesh):
    in_specs = (
        P("fsdp", "sp", None),
        P("fsdp", None),
        P("fsdp", "sp", None),
        P("fsdp"),
        P("fsdp"),
        P("fsdp"),
        P("fsdp"),
        P("fsdp", None),
        P("fsdp", None),
        P("fsdp", None),
        P("fsdp", None),
        P("fsdp", None),
        P("sp", None, "fsdp"),
        P("sp", None, "fsdp"),
        P("sp", None, "fsdp"),
        P("fsdp", "sp", None),
    )
    out_specs = (
        P("fsdp", "sp", None),
        P("fsdp", "sp", None),
        P("fsdp"),
        P("fsdp"),
        P("fsdp"),
        P("fsdp"),
        P("fsdp", None),
        P("fsdp", None),
        P("fsdp", None),
        P("fsdp", None),
        P("fsdp", None),
        P("sp", None, "fsdp"),
        P("sp", None, "fsdp"),
        P("sp", None, "fsdp"),
    )
    return jax.shard_map(local, mesh=mesh, in_specs=in_specs, out_specs=out_specs, check_vma=False)
```

```python
import functools

import jax
import jax.numpy as jnp
from jax import lax
from jax.experimental import pallas as pl
from jax.experimental.pallas import tpu as pltpu
from jax.sharding import PartitionSpec as P

HEADS = 16
HEAD_DIM = 128
EXPERTS = 64
TOPK = 8
WINDOW = 1024


eps = 1e-05
rope_base = 10000.0
masked_score = -1e30


def rms_scale(values, gain_vec):
    return values * lax.rsqrt(jnp.mean(values * values, axis=-1, keepdims=True) + eps) * gain_vec


def rotate_pairs(values, cosine, sine):
    half_dim = values.shape[-1] // 2
    turned = jnp.concatenate([-values[..., half_dim:], values[..., :half_dim]], axis=-1)
    return values * cosine + turned * sine


def rope_tables(positions, head_size):
    inv_freq = rope_base ** (-jnp.arange(0, head_size, 2, dtype=jnp.float32) / head_size)
    phase_half = positions.astype(jnp.float32)[:, None] * inv_freq[None, :]
    phase_all = jnp.concatenate([phase_half, phase_half], axis=-1)
    return (jnp.cos(phase_all)[:, None, :], jnp.sin(phase_all)[:, None, :])


TILE = 1024
LANES = 128


def route_plan(ids, block, sp_count):
    local_experts = EXPERTS // sp_count
    blocks = ids.shape[0] // block
    capacity = 5 * ids.shape[0] * TOPK // (4 * EXPERTS)
    first = lax.axis_index("sp") * local_experts
    mine = first + jnp.arange(local_experts, dtype=jnp.int32)
    named = jnp.any(ids[:, None, :] == mine[None, :, None], axis=-1)
    named = named.reshape(blocks, block, local_experts)
    upto = (jnp.arange(block)[:, None] >= jnp.arange(block)[None, :]).astype(jnp.bfloat16)
    running = jnp.einsum(
        "ts,bse->bte", upto, named.astype(jnp.bfloat16), preferred_element_type=jnp.float32
    ).astype(jnp.int32)
    before = (jnp.arange(blocks)[:, None] > jnp.arange(blocks)[None, :]).astype(jnp.float32)
    earlier = jnp.dot(
        before, running[:, -1].astype(jnp.float32), precision=lax.Precision.HIGHEST
    ).astype(jnp.int32)
    keep = named & (earlier[:, None, :] + running - 1 < capacity)
    rank = jnp.where(keep, running - 1, -1).transpose(0, 2, 1)
    slots = 2 * block * TOPK // EXPERTS
    some = jnp.any(keep, axis=1).reshape(-1, TILE // slots, local_experts)
    live = jnp.any(some, axis=1).astype(jnp.int32).T.reshape(-1)
    return rank, live


def pick_matrix(rank, slots):
    experts, block = rank.shape
    slot = lax.broadcasted_iota(jnp.int32, (slots, block), 0)
    return jnp.concatenate(
        [(slot == rank[e : e + 1, :]).astype(jnp.bfloat16) for e in range(experts)], axis=0
    )


def column_spans(width):
    return [(done, min(512, width - done)) for done in range(0, width, 512)]


def contract(left, right, left_dim, right_dim):
    return lax.dot_general(
        left, right, (((left_dim,), (right_dim,)), ((), ())), preferred_element_type=jnp.float32
    )


def expert_kernel(
    live, first, x_ref, c_ref, gate_ref, up_ref, down_ref, dx_ref, y_ref, dgate_ref, dup_ref,
    act_ref,
):
    e = pl.program_id(0)
    t = pl.program_id(1)
    width = c_ref.shape[2]

    @pl.when(live[e * pl.num_programs(1) + t] == 0)
    def _():
        for ref in (dx_ref, y_ref, dgate_ref, dup_ref, act_ref):
            ref[...] = jnp.zeros_like(ref)

    @pl.when(live[e * pl.num_programs(1) + t] > 0)
    def _():
        x = x_ref[0, :, 0:width]
        gate_mat = gate_ref[0]
        up_mat = up_ref[0]
        down_mat = down_ref[0]
        column = lax.broadcasted_iota(jnp.int32, (TILE, LANES), 1)
        mine = lax.rem(column, EXPERTS) == first[0] + e
        gates = jnp.where(mine, x_ref[0, :, width : width + LANES].astype(jnp.float32), 0.0)
        weight = jnp.sum(gates, axis=1, keepdims=True)
        gate_pre = jnp.dot(x, gate_mat, preferred_element_type=jnp.float32)
        up_pre = jnp.dot(x, up_mat, preferred_element_type=jnp.float32)
        up_act = jnp.dot(c_ref[0], down_mat, preferred_element_type=jnp.float32)
        sig = 1.0 / (1.0 + jnp.exp(-gate_pre))
        silu = gate_pre * sig
        act = silu * up_pre
        gate_grad = jnp.sum(up_act * act, axis=1, keepdims=True)
        act_low = (act * weight).astype(jnp.bfloat16)
        act_grad = up_act * weight
        dgate = (act_grad * up_pre * sig * (1.0 + gate_pre * (1.0 - sig))).astype(jnp.bfloat16)
        dup = (act_grad * silu).astype(jnp.bfloat16)
        act_ref[0] = act_low
        dgate_ref[0] = dgate
        dup_ref[0] = dup
        y_ref[0] = contract(act_low, down_mat, 1, 1).astype(jnp.bfloat16)
        dx_ref[0, :, 0:width] = (
            contract(dgate, gate_mat, 1, 1) + contract(dup, up_mat, 1, 1)
        ).astype(jnp.bfloat16)
        dx_ref[0, :, width : width + LANES] = jnp.where(
            column == first[0] + e, gate_grad, 0.0
        ).astype(jnp.bfloat16)


def run_experts(x_rows, c_rows, w_gate, w_up, w_down, live, first):
    experts, rows, width = c_rows.shape
    hidden = w_gate.shape[2]

    def tile_map(e, t, live, first):
        return (e, t, 0)

    mat = pl.BlockSpec((1, width, hidden), lambda e, t, live, first: (e, 0, 0))
    wide = pl.BlockSpec((1, TILE, width + LANES), tile_map)
    plain = pl.BlockSpec((1, TILE, width), tile_map)
    inner = pl.BlockSpec((1, TILE, hidden), tile_map)
    b16 = jnp.bfloat16
    return pl.pallas_call(
        expert_kernel,
        grid_spec=pltpu.PrefetchScalarGridSpec(
            num_scalar_prefetch=2,
            grid=(experts, rows // TILE),
            in_specs=[wide, plain, mat, mat, mat],
            out_specs=[wide, plain, inner, inner, inner],
        ),
        out_shape=[
            jax.ShapeDtypeStruct(x_rows.shape, b16),
            jax.ShapeDtypeStruct(c_rows.shape, b16),
        ]
        + [jax.ShapeDtypeStruct((experts, rows, hidden), b16)] * 3,
        compiler_params=pltpu.CompilerParams(
            dimension_semantics=("arbitrary", "arbitrary"), vmem_limit_bytes=60 * 2**20
        ),
        cost_estimate=pl.CostEstimate(
            flops=12 * experts * rows * width * hidden,
            bytes_accessed=8 * experts * rows * width,
            transcendentals=experts * rows * hidden,
        ),
        name="experts",
    )(live, first, x_rows, c_rows, w_gate, w_up, w_down)


MESH = pl.DeviceIdType.MESH


class Place:
    def __init__(self, counts, fsdp_too):
        self.n_hi, self.n_lo, self.n_x, self.n_core = counts
        sp = lax.axis_index("sp")
        self.hi, self.lo = sp // self.n_lo, sp % self.n_lo
        if fsdp_too:
            fs = lax.axis_index("fsdp")
            self.x, self.core = fs // self.n_core, fs % self.n_core
        else:
            self.x, self.core = 0, 0

    def peer(self, dim, ahead):
        if dim == "core":
            return {"fsdp": self.x * self.n_core + (self.core + ahead) % self.n_core}
        if dim == "x":
            return {"fsdp": (self.x + ahead) % self.n_x * self.n_core + self.core}
        if dim == "lo":
            return {"sp": self.hi * self.n_lo + (self.lo + ahead) % self.n_lo}
        return {"sp": (self.hi + ahead) % self.n_hi * self.n_lo + self.lo}

    def sizes(self):
        return {"core": self.n_core, "x": self.n_x, "lo": self.n_lo, "hi": self.n_hi}

    def meet(self, other=None):
        barrier = pltpu.get_barrier_semaphore()
        met = 0
        for dim, size in self.sizes().items():
            for ahead in range(1, size):
                pl.semaphore_signal(
                    barrier, inc=1, device_id=self.peer(dim, ahead), device_id_type=MESH
                )
                met += 1
        for dim in ("x", "core") if other is not None else ():
            for ahead in range(1, other.sizes()[dim]):
                pl.semaphore_signal(
                    barrier, inc=1, device_id=other.peer(dim, ahead), device_id_type=MESH
                )
                met += 1
        pl.semaphore_wait(barrier, met)


def mesh_counts(sp_count, fs_count):
    low = 2
    while low * low < sp_count // 2:
        low *= 2
    low = min(low, sp_count)
    core = 2 if fs_count % 2 == 0 else 1
    return sp_count // low, low, fs_count // core, core


def scatter_kernel(
    counts, parts, fsdp_too, part_ref, out_ref, own, buf, first, second, third, own_sem, s0, r0,
    s1, r1, s2, r2, s3, r3, host=None, side=None,
):
    at = Place(counts, fsdp_too)
    n_hi, n_lo, n_x, n_core = counts
    rows = out_ref.shape[0] // parts
    pairs = parts // 2
    steps = n_hi * pairs
    lag = 1
    orders = [[d for d in o if at.sizes()[d] > 1] for o in (("x", "lo"), ("lo", "x"))]

    def remote(src, dst, send, recv, dim, ahead):
        return pltpu.make_async_remote_copy(
            src_ref=src, dst_ref=dst, send_sem=send, recv_sem=recv,
            device_id=at.peer(dim, ahead), device_id_type=MESH,
        )

    def where(t, v):
        return (at.hi + 1 + t // pairs) % n_hi, t % pairs * 2 + v

    def mine(t, v, core):
        hi, q = where(t, v)
        cut = pl.ds(pl.multiple_of(q * rows, 16), rows)
        if host is not None:
            return host.part.at[t // pairs % 2, :, core, :, cut, :]
        return part_ref.at[:, core, hi, :, cut, :]

    def load_own(t, v):
        place = own.at[t % 2, v] if n_core > 1 else buf.at[2 * t + v]
        return pltpu.make_async_copy(mine(t, v, at.core), place, own_sem.at[t % 2, v])

    def core_copy(t, v):
        return remote(
            mine(t, v, (at.core + 1) % 2), buf.at[2 * t + v], s0.at[2 * t + v], r0.at[2 * t + v],
            "core", 1,
        )

    def mid_copy(t, v, stage, ahead):
        u = 2 * t + v
        dim = orders[v][stage]
        size = at.sizes()[dim]
        to = ((at.x if dim == "x" else at.lo) + ahead) % size
        if stage == 0:
            src = buf.at[u, to] if dim == "x" else buf.at[u, :, to]
            dst = first.at[u, size - ahead - 1, pl.ds(0, n_lo if dim == "x" else n_x)]
            return remote(
                src, dst, s1.at[u, ahead - 1], r1.at[u, size - ahead - 1], dim, ahead
            )
        return remote(
            first.at[u, 0, to], second.at[u, size - ahead - 1],
            s2.at[u, ahead - 1], r2.at[u, size - ahead - 1], dim, ahead,
        )

    def wait_in(t, v, stage):
        size = at.sizes()[orders[v][stage]]
        for ahead in range(1, size):
            mid_copy(t, v, stage, ahead).wait_recv()

    def start_out(t, v, stage):
        size = at.sizes()[orders[v][stage]]
        for ahead in range(1, size):
            mid_copy(t, v, stage, ahead).start()

    def wide(ref):
        return ref[...].astype(jnp.float32)

    def result(t, v):
        u = 2 * t + v
        if len(orders[v]) == 2:
            return second.at[u, 0]
        if len(orders[v]) == 1:
            return first.at[u, 0, 0]
        return buf.at[u, 0, 0]

    def last_copy(t, v, ahead):
        _, q = where(t, v)
        return remote(
            result(t, v), third.at[n_hi - ahead - 1, q],
            s3.at[2 * t + v], r3.at[n_hi - ahead - 1, q], "hi", ahead,
        )

    def send_last(t, v):
        for k in range(n_hi - 1):

            @pl.when(t // pairs == k)
            def _(k=k):
                last_copy(t, v, k + 1).start()

    def stage_core(t, v):
        u = 2 * t + v
        if host is None:
            load_own(t, v).wait()
            own_part = own.at[t % 2, v]
        else:
            own_part = mine(t, v, at.core)
        if n_core > 1:
            core_copy(t, v).wait_recv()

            @pl.loop(0, n_x * n_lo)
            def _(j):
                x, lo = j // n_lo, j % n_lo
                place = buf.at[u, x, lo]
                place[...] = (wide(place) + wide(own_part.at[x, lo])).astype(jnp.bfloat16)

        if orders[v]:
            start_out(t, v, 0)
        else:
            send_last(t, v)

    def stage_mid(t, v, stage):
        u = 2 * t + v
        wait_in(t, v, stage)
        dim = orders[v][stage]
        size = at.sizes()[dim]
        if stage == 0:
            keep = n_lo if dim == "x" else n_x

            @pl.loop(0, keep)
            def _(j):
                base = buf.at[u, at.x, j] if dim == "x" else buf.at[u, j, at.lo]
                total = wide(base)
                for s in range(size - 1):
                    total = total + wide(first.at[u, s, j])
                first.at[u, 0, j][...] = total.astype(jnp.bfloat16)

        else:
            base = first.at[u, 0, at.x if dim == "x" else at.lo]
            total = wide(base)
            for s in range(size - 1):
                total = total + wide(second.at[u, s])
            second.at[u, 0][...] = total.astype(jnp.bfloat16)
        if stage + 1 < len(orders[v]):
            start_out(t, v, stage + 1)
        else:
            send_last(t, v)

    def each_core_copy(group, act):
        @pl.loop(0, pairs)
        def _(g):
            for v in range(2):
                act(core_copy(group * pairs + g, v))

    def make_group(group, piece, pieces):
        host.run(at, (at.hi + 1 + group) % n_hi, group % 2, piece, pieces)

    at.meet()
    if host is not None:
        make_group(0, 0, 2)
        each_core_copy(0, lambda c: c.start())
        make_group(0, 1, 2)
    else:
        if n_core > 1:

            @pl.loop(0, n_hi)
            def _(group):
                each_core_copy(group, lambda c: c.start())

        for v in range(2):
            load_own(0, v).start()

    depth = len(orders[0])

    @pl.loop(0, steps + depth * lag)
    def _(t):
        if host is None:

            @pl.when(t + 1 < steps)
            def _():
                for v in range(2):
                    load_own(t + 1, v).start()

        @pl.when(t < steps)
        def _():
            for v in range(2):
                stage_core(t, v)

        for stage in range(depth):
            back = (stage + 1) * lag

            @pl.when((t >= back) & (t < steps + back))
            def _(stage=stage, back=back):
                for v in range(2):
                    stage_mid(t - back, v, stage)

        if host is not None:

            @pl.when(t + pairs < steps)
            def _():
                group = t // pairs + 1

                @pl.when((t % pairs == 0) & (group >= 2))
                def _():
                    each_core_copy(group - 2, lambda c: c.wait_send())

                make_group(group, t % pairs, pairs)

                @pl.when(t % pairs == (pairs + 1) // 2 - 1)
                def _():
                    each_core_copy(group, lambda c: c.start())

        if side is not None:
            side.share(t, steps + depth * lag)

    for g in range(pairs):
        t = (n_hi - 1) * pairs + g
        for v in range(2):
            q = g * 2 + v
            total = wide(result(t, v))
            for s in range(n_hi - 1):
                last_copy(g, v, n_hi - 1 - s).wait_recv()
                total = total + wide(third.at[s, q])
            out_ref[pl.ds(q * rows, rows), :] = total.astype(out_ref.dtype)

    @pl.loop(0, steps)
    def _(t):
        for v in range(2):
            if host is None and n_core > 1:
                core_copy(t, v).wait_send()
            for stage in range(depth):
                for ahead in range(1, at.sizes()[orders[v][stage]]):
                    mid_copy(t, v, stage, ahead).wait_send()

            @pl.when(t // pairs < n_hi - 1)
            def _(v=v):
                last_copy(t, v, 1).wait_send()

    if host is not None:
        for group in range(max(n_hi - 2, 0), n_hi):
            each_core_copy(group, lambda c: c.wait_send())


class WeightGrads:
    def __init__(self, rows, grads, outs, row_bufs, grad_buf, acc, stage, in_sems, out_sems):
        self.rows, self.grads, self.outs = rows, grads, outs
        self.row_bufs, self.grad_buf, self.acc, self.stage = row_bufs, grad_buf, acc, stage
        self.in_sems, self.out_sems = in_sems, out_sems
        experts, total, _ = grads[0].shape
        self.depth = grad_buf.shape[2]
        self.each = total // self.depth
        self.jobs = experts * self.each

    def loads(self, j, slot):
        e = j // self.each
        rows = pl.ds(pl.multiple_of(j % self.each * self.depth, self.depth), self.depth)
        copies = []
        for k in range(2):
            width = self.row_bufs[k].shape[2]
            copies.append(
                pltpu.make_async_copy(
                    self.rows[k].at[e, rows, pl.ds(0, width)], self.row_bufs[k].at[slot],
                    self.in_sems.at[slot, k],
                )
            )
        for k in range(3):
            copies.append(
                pltpu.make_async_copy(
                    self.grads[k].at[e, rows], self.grad_buf.at[slot, k],
                    self.in_sems.at[slot, 2 + k],
                )
            )
        return copies

    def stores(self, e):
        return [
            pltpu.make_async_copy(self.stage.at[k], self.outs[k].at[e], self.out_sems.at[k])
            for k in range(3)
        ]

    def begin(self):
        for copy in self.loads(0, 0):
            copy.start()

    def share(self, t, turns):
        count = -(-self.jobs // turns)

        @pl.loop(0, count)
        def _(i):
            j = t * count + i

            @pl.when(j < self.jobs)
            def _():
                self.job(j)

    def job(self, j):
        slot = j % 2

        @pl.when(j + 1 < self.jobs)
        def _():
            for copy in self.loads(j + 1, 1 - slot):
                copy.start()

        for copy in self.loads(j, slot):
            copy.wait()

        @pl.when(j % self.each == 0)
        def _():
            self.acc[...] = jnp.zeros_like(self.acc)

        for k in range(3):
            rows = self.row_bufs[0 if k < 2 else 1]
            for start, size in column_spans(rows.shape[2]):
                cols = pl.ds(start, size)
                self.acc[k, :, cols] += contract(
                    self.grad_buf[slot, k], rows[slot, :, cols], 0, 0
                )

        @pl.when(j % self.each == self.each - 1)
        def _():
            e = j // self.each

            @pl.when(e > 0)
            def _():
                for copy in self.stores(e - 1):
                    copy.wait()

            for k in range(3):
                self.stage[k] = self.acc[k].T.astype(self.stage.dtype)
            for copy in self.stores(e):
                copy.start()

    def finish(self):
        for copy in self.stores(self.jobs // self.each - 1):
            copy.wait()


def scatter_grads_kernel(
    counts, parts, part_ref, x_ref, c_ref, dgate_ref, dup_ref, act_ref, out_ref, gg_ref, gu_ref,
    gd_ref, x_buf, c_buf, grad_buf, acc, stage, in_sems, out_sems, own, *scratch,
):
    side = WeightGrads(
        (x_ref, c_ref), (dgate_ref, dup_ref, act_ref), (gg_ref, gu_ref, gd_ref), (x_buf, c_buf),
        grad_buf, acc, stage, in_sems, out_sems,
    )
    side.begin()
    scatter_kernel(counts, parts, False, part_ref, out_ref, own, *scratch, side=side)
    side.finish()


def scatter_and_grads(partial, counts, parts, x_rows, c_rows, grads, ident, name):
    n_hi, n_lo, n_x, n_core = counts
    rows, width = partial.shape[4:]
    experts, slots, hidden = grads[0].shape
    depth = 512
    b16 = jnp.bfloat16
    anywhere = pl.BlockSpec(memory_space=pl.ANY)
    weight = jax.ShapeDtypeStruct((experts, width, hidden), b16)
    return pl.pallas_call(
        functools.partial(scatter_grads_kernel, counts, parts),
        in_specs=[anywhere] * 6,
        out_specs=[pl.BlockSpec(memory_space=pltpu.VMEM)] + [anywhere] * 3,
        out_shape=[jax.ShapeDtypeStruct((rows, width), jnp.float32)] + [weight] * 3,
        scratch_shapes=[
            pltpu.VMEM((2, depth, width), b16),
            pltpu.VMEM((2, depth, width), b16),
            pltpu.VMEM((2, 3, depth, hidden), b16),
            pltpu.VMEM((3, hidden, width), jnp.float32),
            pltpu.VMEM((3, width, hidden), b16),
            pltpu.SemaphoreType.DMA((2, 5)),
            pltpu.SemaphoreType.DMA((3,)),
            pltpu.VMEM((1, 1, 1, 1, 16, 128), b16),
        ]
        + scatter_scratch(counts, parts, rows // parts, width),
        compiler_params=pltpu.CompilerParams(
            collective_id=ident, has_side_effects=True, vmem_limit_bytes=60 * 2**20
        ),
        cost_estimate=pl.CostEstimate(
            flops=6 * experts * slots * width * hidden,
            bytes_accessed=4 * experts * slots * width,
            transcendentals=0,
        ),
        name=name,
    )(partial, x_rows, c_rows, *grads)


class Combine:
    def __init__(self, rows_ref, rank_ref, part, held, sems, counts):
        self.rows_ref, self.rank_ref, self.part, self.held, self.sems = (
            rows_ref, rank_ref, part, held, sems,
        )
        self.n_hi, self.n_lo, self.n_x, self.n_core = counts

    def run(self, at, hi, slot, piece, pieces):
        total = self.n_x * self.n_core * self.n_lo
        count = total // pieces
        _, experts, slots, width = self.held.shape

        def spot(j):
            j = piece * count + j
            core = (at.core + 1 + j // (self.n_x * self.n_lo)) % self.n_core
            return j // self.n_lo % self.n_x, core, j % self.n_lo

        def block(j):
            x, core, lo = spot(j)
            return ((x * self.n_core + core) * self.n_hi + hi) * self.n_lo + lo

        def load(j, place):
            return pltpu.make_async_copy(
                self.rows_ref.at[:, block(j)], self.held.at[place], self.sems.at[place]
            )

        load(0, 0).start()

        @pl.loop(0, count)
        def _(j):
            place = j % 2

            @pl.when(j + 1 < count)
            def _():
                load(j + 1, 1 - place).start()

            load(j, place).wait()
            pick = pick_matrix(self.rank_ref[block(j)], slots)
            x, core, lo = spot(j)
            for start, size in column_spans(width):
                cols = pl.ds(start, size)
                found = self.held[place, :, :, cols].reshape(experts * slots, size)
                self.part[slot, x, core, lo, :, cols] = contract(pick, found, 0, 0).astype(
                    jnp.bfloat16
                )


def combine_scatter_kernel(
    counts, parts, rows_ref, rank_ref, out_ref, part, held, held_sem, *scratch
):
    host = Combine(rows_ref, rank_ref, part, held, held_sem, counts)
    scatter_kernel(counts, parts, True, None, out_ref, None, *scratch, host=host)


def scatter_scratch(counts, parts, r, width):
    n_hi, n_lo, n_x, _ = counts
    units = n_hi * parts
    keep = max(n_x, n_lo)
    peers = max(n_x, n_lo, 2) - 1
    b16 = jnp.bfloat16
    return [
        pltpu.VMEM((units, n_x, n_lo, r, width), b16),
        pltpu.VMEM((units, peers, keep, r, width), b16),
        pltpu.VMEM((units, peers, r, width), b16),
        pltpu.VMEM((max(n_hi - 1, 1), parts, r, width), b16),
        pltpu.SemaphoreType.DMA((2, 2)),
        pltpu.SemaphoreType.DMA((units,)),
        pltpu.SemaphoreType.DMA((units,)),
        pltpu.SemaphoreType.DMA((units, peers)),
        pltpu.SemaphoreType.DMA((units, peers)),
        pltpu.SemaphoreType.DMA((units, peers)),
        pltpu.SemaphoreType.DMA((units, peers)),
        pltpu.SemaphoreType.DMA((units,)),
        pltpu.SemaphoreType.DMA((max(n_hi - 1, 1), parts)),
    ]


def scatter_bytes(counts, parts, rows, width):
    n_hi, n_lo, n_x, _ = counts
    keep = max(n_x, n_lo)
    peers = max(n_x, n_lo, 2) - 1
    held = n_hi * (n_x * n_lo + peers * keep + peers) + max(n_hi - 1, 1)
    return (2 * held + 4) * rows * width


VMEM_ROOM = 58 * 2**20


def combine_sum(rows, rank, counts, parts, slots, ident, name):
    blocks, experts, block = rank.shape
    width = rows.shape[-1]
    _, n_lo, n_x, n_core = counts
    b16 = jnp.bfloat16
    return pl.pallas_call(
        functools.partial(combine_scatter_kernel, counts, parts),
        in_specs=[pl.BlockSpec(memory_space=pl.ANY), pl.BlockSpec(memory_space=pltpu.VMEM)],
        out_specs=pl.BlockSpec(memory_space=pltpu.VMEM),
        out_shape=jax.ShapeDtypeStruct((block, width), jnp.float32),
        scratch_shapes=[
            pltpu.VMEM((2, n_x, n_core, n_lo, block, width), b16),
            pltpu.VMEM((2, experts, slots, width), b16),
            pltpu.SemaphoreType.DMA((2,)),
        ]
        + scatter_scratch(counts, parts, block // parts, width),
        compiler_params=pltpu.CompilerParams(
            collective_id=ident, has_side_effects=True, vmem_limit_bytes=62 * 2**20
        ),
        cost_estimate=pl.CostEstimate(
            flops=2 * blocks * experts * slots * block * width,
            bytes_accessed=4 * blocks * block * width,
            transcendentals=0,
        ),
        name=name,
    )(rows.reshape(experts, blocks, slots, width), rank)


def scatter_sum(partial, counts, fsdp_too, parts, out_dtype, ident, name):
    _, n_lo, n_x, n_core = counts
    rows, width = partial.shape[4:]
    r = rows // parts
    own_shape = (2, 2, n_x, n_lo, r, width) if n_core > 1 else (1, 1, 1, 1, 16, 128)
    scratch = [pltpu.VMEM(own_shape, jnp.bfloat16)] + scatter_scratch(counts, parts, r, width)
    return pl.pallas_call(
        functools.partial(scatter_kernel, counts, parts, fsdp_too),
        in_specs=[pl.BlockSpec(memory_space=pl.ANY)],
        out_specs=pl.BlockSpec(memory_space=pltpu.VMEM),
        out_shape=jax.ShapeDtypeStruct((rows, width), out_dtype),
        scratch_shapes=scratch,
        compiler_params=pltpu.CompilerParams(
            collective_id=ident, has_side_effects=True, vmem_limit_bytes=60 * 2**20
        ),
        cost_estimate=pl.CostEstimate(
            flops=partial.size, bytes_accessed=2 * partial.size, transcendentals=0
        ),
        name=name,
    )(partial)


def gather_kernel(
    counts, parts, fsdp_too, in_ref, out_ref, own_sem, s0, r0, s1, r1, s2, r2, s3, r3, host=None,
    side=None,
):
    at = Place(counts, fsdp_too)
    n_hi, n_lo, n_x, n_core = counts
    rows = in_ref.shape[0] // parts
    pairs = parts // 2
    steps = n_hi * pairs
    orders = [[d for d in o if at.sizes()[d] > 1] for o in (("lo", "x"), ("x", "lo"))]
    depth = len(orders[0])

    def remote(src, dst, send, recv, dim, ahead):
        return pltpu.make_async_remote_copy(
            src_ref=src, dst_ref=dst, send_sem=send, recv_sem=recv,
            device_id=at.peer(dim, ahead), device_id_type=MESH,
        )

    def span(q):
        return pl.ds(pl.multiple_of(q * rows, 16), rows)

    def hi_copy(q, ahead):
        return remote(
            in_ref.at[span(q)], out_ref.at[at.x, at.core, at.hi, at.lo, span(q)],
            s0.at[ahead - 1, q], r0.at[n_hi - ahead - 1, q], "hi", ahead,
        )

    def where(t, v):
        return (at.hi + n_hi - t // pairs) % n_hi, t % pairs * 2 + v

    def mid_copy(t, v, stage, ahead):
        u = 2 * t + v
        hi, q = where(t, v)
        dim = orders[v][stage]
        size = at.sizes()[dim]
        if stage == 0:
            ref = out_ref.at[at.x, at.core, hi, at.lo, span(q)]
            if_own = in_ref.at[span(q)]
            del if_own
            return remote(
                ref, ref, s1.at[u, ahead - 1], r1.at[u, size - ahead - 1], dim, ahead
            )
        if dim == "x":
            ref = out_ref.at[at.x, at.core, hi, :, span(q)]
        else:
            ref = out_ref.at[:, at.core, hi, at.lo, span(q)]
        return remote(ref, ref, s2.at[u, ahead - 1], r2.at[u, size - ahead - 1], dim, ahead)

    def core_copy(t, v):
        u = 2 * t + v
        hi, q = where(t, v)
        ref = out_ref.at[:, at.core, hi, :, span(q)]
        return remote(ref, ref, s3.at[u], r3.at[u], "core", 1)

    def each_mid(t, v, stage, act):
        size = at.sizes()[orders[v][stage]]
        for ahead in range(1, size):
            act(mid_copy(t, v, stage, ahead))

    keep = pltpu.make_async_copy(
        in_ref, out_ref.at[at.x, at.core, at.hi, at.lo], own_sem
    )
    keep.start()
    at.meet(side.at if side is not None else None)
    if side is not None:
        side.begin()
    for ahead in range(1, n_hi):
        for q in range(parts):
            hi_copy(q, ahead).start()
    keep.wait()

    @pl.loop(0, steps + depth + (1 if host is not None and n_core > 1 else 0))
    def _(t):
        @pl.when(t < steps)
        def _():
            for v in range(2):
                _, q = where(t, v)
                for k in range(1, n_hi):

                    @pl.when(t // pairs == k)
                    def _(k=k, q=q):
                        hi_copy(q, k).wait_recv()

                if depth > 0:
                    each_mid(t, v, 0, lambda c: c.start())
                elif n_core > 1:
                    core_copy(t, v).start()

        for stage in range(depth):
            back = stage + 1

            @pl.when((t >= back) & (t < steps + back))
            def _(stage=stage, back=back):
                for v in range(2):
                    each_mid(t - back, v, stage, lambda c: c.wait_recv())
                    if stage + 1 < depth:
                        each_mid(t - back, v, stage + 1, lambda c: c.start())
                    elif n_core > 1:
                        core_copy(t - back, v).start()

        if side is not None:

            @pl.when(t == steps // 2 + 1)
            def _():
                side.middle()

        if host is not None:
            for origin_step in range(n_hi):
                done = (origin_step + 1) * pairs - 1 + depth
                hi = (at.hi + n_hi - origin_step) % n_hi

                @pl.when(t == done)
                def _(hi=hi):
                    host.blocks(at, at.core, hi)

                if n_core > 1:

                    @pl.when(t == done + 1)
                    def _(hi=hi, origin_step=origin_step):
                        for g in range(pairs):
                            for v in range(2):
                                core_copy(origin_step * pairs + g, v).wait_recv()
                        host.blocks(at, 1 - at.core, hi)

            host.others(t, steps + depth)

    @pl.loop(0, steps)
    def _(t):
        for v in range(2):
            if n_core > 1:
                if host is None:
                    core_copy(t, v).wait_recv()
                core_copy(t, v).wait_send()
            for stage in range(depth):
                each_mid(t, v, stage, lambda c: c.wait_send())

    for q in range(parts):
        for ahead in range(1, n_hi):
            hi_copy(q, ahead).wait_send()

    if side is not None:
        side.end()


class SideGather:
    def __init__(self, counts, in_ref, out_ref, own_sem, s_x, r_x, s_core, r_core):
        self.at = Place(counts, True)
        self.in_ref, self.out_ref, self.own_sem = in_ref, out_ref, own_sem
        self.s_x, self.r_x, self.s_core, self.r_core = s_x, r_x, s_core, r_core

    def own(self):
        at = self.at
        return pltpu.make_async_copy(self.in_ref, self.out_ref.at[at.x, at.core], self.own_sem)

    def x_copy(self, ahead):
        at = self.at
        return pltpu.make_async_remote_copy(
            src_ref=self.in_ref, dst_ref=self.out_ref.at[at.x, at.core],
            send_sem=self.s_x.at[ahead - 1], recv_sem=self.r_x.at[at.n_x - ahead - 1],
            device_id=at.peer("x", ahead), device_id_type=MESH,
        )

    def core_copy(self):
        ref = self.out_ref.at[:, self.at.core]
        return pltpu.make_async_remote_copy(
            src_ref=ref, dst_ref=ref, send_sem=self.s_core, recv_sem=self.r_core,
            device_id=self.at.peer("core", 1), device_id_type=MESH,
        )

    def begin(self):
        self.own().start()
        for ahead in range(1, self.at.n_x):
            self.x_copy(ahead).start()

    def middle(self):
        self.own().wait()
        for ahead in range(1, self.at.n_x):
            self.x_copy(ahead).wait_recv()
        if self.at.n_core > 1:
            self.core_copy().start()

    def end(self):
        for ahead in range(1, self.at.n_x):
            self.x_copy(ahead).wait_send()
        if self.at.n_core > 1:
            self.core_copy().wait()


def gather_two_kernel(
    counts, parts, side_counts, in_ref, side_in, out_ref, side_out, own_sem, s_x, r_x, s_core,
    r_core, *sems,
):
    side = SideGather(side_counts, side_in, side_out, own_sem, s_x, r_x, s_core, r_core)
    gather_kernel(counts, parts, False, in_ref, out_ref, *sems, side=side)


def gather_two(own, weight, counts, side_counts, parts, ident, name):
    n_hi, n_lo, _, _ = counts
    _, _, n_x, n_core = side_counts
    rows, width = own.shape
    anywhere = pl.BlockSpec(memory_space=pl.ANY)
    dma = pltpu.SemaphoreType.DMA
    out, side = pl.pallas_call(
        functools.partial(gather_two_kernel, counts, parts, side_counts),
        in_specs=[anywhere] * 2,
        out_specs=[anywhere] * 2,
        out_shape=[
            jax.ShapeDtypeStruct((1, 1, n_hi, n_lo, rows, width), own.dtype),
            jax.ShapeDtypeStruct((n_x, n_core) + weight.shape, weight.dtype),
        ],
        scratch_shapes=[dma, dma((max(n_x - 1, 1),)), dma((max(n_x - 1, 1),)), dma, dma]
        + gather_sems(counts, parts),
        compiler_params=pltpu.CompilerParams(collective_id=ident, has_side_effects=True),
        cost_estimate=pl.CostEstimate(
            flops=0, bytes_accessed=4 * n_hi * n_lo * rows * width, transcendentals=0
        ),
        name=name,
    )(own, weight)
    return out.reshape(-1, width), side.reshape(-1, weight.shape[1])


class Dispatch:
    def __init__(self, tables, rows, bufs, ins, outs, rank_ref, geometry):
        self.tables, self.rows, self.bufs, self.ins, self.outs = tables, rows, bufs, ins, outs
        self.rank_ref = rank_ref
        self.n_hi, self.n_lo, self.n_x, self.n_core = geometry

    def load(self, which, index, slot):
        held, _ = self.bufs[which]
        return pltpu.make_async_copy(
            self.tables[which].at[index + (slice(None), pl.ds(0, held.shape[2]))],
            held.at[slot], self.ins[which].at[slot],
        )

    def store(self, which, block, slot):
        _, found = self.bufs[which]
        return pltpu.make_async_copy(
            found.at[slot], self.rows[which].at[:, block], self.outs[which].at[slot]
        )

    def run(self, which, block_of, index_of, count):
        held, found = self.bufs[which]
        experts, slots, width = found.shape[1:]
        if held is not None:
            self.load(which, index_of(0), 0).start()

        @pl.loop(0, count)
        def _(j):
            slot = j % 2

            if held is not None:

                @pl.when(j + 1 < count)
                def _():
                    self.load(which, index_of(j + 1), 1 - slot).start()

            @pl.when(j >= 2)
            def _():
                self.store(which, block_of(j - 2), slot).wait()

            if held is not None:
                self.load(which, index_of(j), slot).wait()
                table = held.at[slot]
            else:
                table = self.tables[which].at[index_of(j)]
            pick = pick_matrix(self.rank_ref[block_of(j)], slots)
            for start, size in column_spans(width):
                cols = pl.ds(start, size)
                picked = jnp.dot(
                    pick, table[:, cols], preferred_element_type=jnp.float32
                ).astype(jnp.bfloat16)
                found[slot, :, :, cols] = picked.reshape(experts, slots, size)
            self.store(which, block_of(j), slot).start()

        for j in range(max(count - 2, 0), count):
            self.store(which, block_of(j), j % 2).wait()

    def blocks(self, at, core, hi):
        def spot(j):
            return j // self.n_lo, core, hi, j % self.n_lo

        def block_of(j):
            x, c, h, lo = spot(j)
            return ((x * self.n_core + c) * self.n_hi + h) * self.n_lo + lo

        self.run(0, block_of, spot, self.n_x * self.n_lo)

    def others(self, t, steps):
        total = self.n_x * self.n_core * self.n_hi * self.n_lo
        each = -(-total // steps)
        for step in range(steps):
            first = min(step * each, total)
            count = min(each, total - first)
            if count > 0:

                @pl.when(t == step)
                def _(first=first, count=count):
                    self.run(1, lambda j: first + j, lambda j: (first + j,), count)


def dispatch_kernel(
    counts, parts, in_ref, other_ref, rank_ref, rows_ref, other_rows_ref, *rest
):
    out_ref, held, found, other_held, other_found, in_sem, put_sem, other_in_sem, other_put_sem = (
        rest[:9]
    )
    sems = rest[9:]
    if len(out_ref.shape) == 6 and held.shape[0] == 1:
        held = None
    host = Dispatch(
        (out_ref, other_ref), (rows_ref, other_rows_ref),
        ((held, found), (other_held, other_found)), (in_sem, other_in_sem),
        (put_sem, other_put_sem), rank_ref, counts,
    )
    gather_kernel(counts, parts, True, in_ref, out_ref, *sems, host=host)


def gather_sems(counts, parts):
    n_hi, n_lo, n_x, n_core = counts
    units = n_hi * parts
    peers = max(n_x, n_lo, 2) - 1
    ahead = max(n_hi - 1, 1)
    sizes = [(ahead, parts)] * 2 + [(units, peers)] * 4 + [(units,)] * 2
    return [pltpu.SemaphoreType.DMA] + [pltpu.SemaphoreType.DMA(size) for size in sizes]


def gather_and_dispatch(own, other_all, other_width, rank, slots, sp_count, fs_count, ident, name):
    counts = mesh_counts(sp_count, fs_count)
    n_hi, n_lo, n_x, n_core = counts
    rows, width = own.shape
    blocks, experts, _ = rank.shape
    parts = 4 if rows % 64 == 0 else 2
    b16 = jnp.bfloat16
    anywhere = pl.BlockSpec(memory_space=pl.ANY)
    table = (n_x, n_core, n_hi, n_lo, rows, width)
    inside = 2 * blocks * rows * width <= 36 * 2**20
    scratch = [
        pltpu.VMEM((1, 16, LANES) if inside else (2, rows, width), b16),
        pltpu.VMEM((2, experts, slots, width), b16),
        pltpu.VMEM((2, rows, other_width), b16),
        pltpu.VMEM((2, experts, slots, other_width), b16),
    ] + [pltpu.SemaphoreType.DMA((2,))] * 4
    flops = 2 * blocks * experts * slots * rows * (width + other_width)
    results = [
        jax.ShapeDtypeStruct((experts, blocks, slots, width), b16),
        jax.ShapeDtypeStruct((experts, blocks, slots, other_width), b16),
    ]
    if inside:
        scratch = [pltpu.VMEM(table, b16)] + scratch
    else:
        results.append(jax.ShapeDtypeStruct(table, b16))
    picked, other_picked, *_ = pl.pallas_call(
        functools.partial(dispatch_kernel, counts, parts),
        in_specs=[anywhere, anywhere, pl.BlockSpec(memory_space=pltpu.VMEM)],
        out_specs=[anywhere] * len(results),
        out_shape=results,
        scratch_shapes=scratch + gather_sems(counts, parts),
        compiler_params=pltpu.CompilerParams(
            collective_id=ident, has_side_effects=True, vmem_limit_bytes=56 * 2**20
        ),
        cost_estimate=pl.CostEstimate(
            flops=flops, bytes_accessed=8 * blocks * rows * width, transcendentals=0
        ),
        name=name,
    )(own, other_all.reshape(blocks, rows, -1), rank)
    return picked.reshape(experts, -1, width), other_picked.reshape(experts, -1, other_width)


def gather_rows(own, counts, fsdp_too, parts, ident, name):
    n_hi, n_lo, n_x, n_core = counts
    rows, width = own.shape
    total = rows * n_hi * n_lo * n_x * n_core
    out = pl.pallas_call(
        functools.partial(gather_kernel, counts, parts, fsdp_too),
        in_specs=[pl.BlockSpec(memory_space=pl.ANY)],
        out_specs=pl.BlockSpec(memory_space=pl.ANY),
        out_shape=jax.ShapeDtypeStruct((n_x, n_core, n_hi, n_lo, rows, width), own.dtype),
        scratch_shapes=gather_sems(counts, parts),
        compiler_params=pltpu.CompilerParams(collective_id=ident, has_side_effects=True),
        cost_estimate=pl.CostEstimate(
            flops=0, bytes_accessed=4 * total * width, transcendentals=0
        ),
        name=name,
    )(own)
    return out.reshape(total, width)


def small_sum_kernel(counts, part_ref, out_ref, first, second, s0, r0, s1, r1):
    sp_count, fs_count = counts
    at = {"sp": lax.axis_index("sp"), "fsdp": lax.axis_index("fsdp")}

    def peer(dim, ahead, size):
        return {dim: (at[dim] + ahead) % size}

    barrier = pltpu.get_barrier_semaphore()
    for dim, size in (("sp", sp_count), ("fsdp", fs_count)):
        for ahead in range(1, size):
            pl.semaphore_signal(
                barrier, inc=1, device_id=peer(dim, ahead, size), device_id_type=MESH
            )
    pl.semaphore_wait(barrier, sp_count + fs_count - 2)

    def exchange(src, held, send, recv, dim, size):
        copies = [
            pltpu.make_async_remote_copy(
                src_ref=src, dst_ref=held.at[size - ahead - 1],
                send_sem=send.at[ahead - 1], recv_sem=recv.at[size - ahead - 1],
                device_id=peer(dim, ahead, size), device_id_type=MESH,
            )
            for ahead in range(1, size)
        ]
        for copy in copies:
            copy.start()
        total = src[...]
        for ahead, copy in enumerate(copies, 1):
            pltpu.make_async_remote_copy(
                src_ref=src, dst_ref=held.at[ahead - 1],
                send_sem=send.at[size - ahead - 1], recv_sem=recv.at[ahead - 1],
                device_id=peer(dim, size - ahead, size), device_id_type=MESH,
            ).wait_recv()
            total = total + held[ahead - 1]
        for copy in copies:
            copy.wait_send()
        return total

    total = exchange(part_ref, first, s0, r0, "sp", sp_count)
    out_ref[...] = total
    if fs_count > 1:
        total = exchange(out_ref, second, s1, r1, "fsdp", fs_count)
        out_ref[...] = total


def small_sum(part, sp_count, fs_count, ident, name):
    sems = [pltpu.SemaphoreType.DMA((max(n - 1, 1),)) for n in (sp_count, sp_count, fs_count, fs_count)]
    return pl.pallas_call(
        functools.partial(small_sum_kernel, (sp_count, fs_count)),
        in_specs=[pl.BlockSpec(memory_space=pltpu.VMEM)],
        out_specs=pl.BlockSpec(memory_space=pltpu.VMEM),
        out_shape=jax.ShapeDtypeStruct(part.shape, jnp.float32),
        scratch_shapes=[
            pltpu.VMEM((max(sp_count - 1, 1),) + part.shape, jnp.float32),
            pltpu.VMEM((max(fs_count - 1, 1),) + part.shape, jnp.float32),
        ]
        + sems,
        compiler_params=pltpu.CompilerParams(collective_id=ident, has_side_effects=True),
        name=name,
    )(part)


ROWS = 256


def window_scores(ends, count, q, k, first, top):
    scores = contract(q, k, 1, 1) * HEAD_DIM ** (-0.5)
    place = top + lax.broadcasted_iota(jnp.int32, (ROWS, 1), 0)
    oldest = jnp.maximum(place - (WINDOW - 1), 0)
    for n in range(count):
        oldest = jnp.maximum(oldest, jnp.where(place >= ends[n], ends[n], 0))
    other = first + lax.broadcasted_iota(jnp.int32, scores.shape, 1)
    return jnp.where((other >= oldest) & (other <= place), scores, masked_score)


def window_first(i, reach, total):
    return pl.multiple_of(jnp.clip(i * ROWS + ROWS - reach, 0, total - reach), ROWS)


def softmax_rows(scores):
    weights = jnp.exp(scores - jnp.max(scores, axis=-1, keepdims=True))
    return weights / jnp.sum(weights, axis=-1, keepdims=True)


def turn_pairs(values, cosine, sine):
    return values * cosine + pltpu.roll(values, HEAD_DIM // 2, 1) * sine


def attend_kernel(
    count, reach, ends, q_ref, k_ref, v_ref, scale_ref, gain_ref, cos_ref, sin_ref, o_ref, qo_ref,
    ko_ref, vo_ref,
):
    i = pl.program_id(1)
    first = window_first(i, reach, k_ref.shape[0])
    keys = pl.ds(first, reach)
    here = pl.ds(pl.multiple_of(i * ROWS, ROWS), ROWS)

    @pl.when(i == 0)
    def _():
        normed = k_ref[...] * scale_ref[:, 1:2] * gain_ref[1:2, :]
        ko_ref[...] = turn_pairs(normed, cos_ref[...], sin_ref[...]).astype(jnp.bfloat16)
        vo_ref[...] = v_ref[...].astype(jnp.bfloat16)

    normed = q_ref[...] * scale_ref[here, 0:1] * gain_ref[0:1, :]
    q = turn_pairs(normed, cos_ref[here, :], sin_ref[here, :]).astype(jnp.bfloat16)
    qo_ref[...] = q
    scores = window_scores(ends, count, q, ko_ref[keys, :], first, i * ROWS)
    probs = softmax_rows(scores).astype(jnp.bfloat16)
    o_ref[...] = jnp.dot(probs, vo_ref[keys, :], preferred_element_type=jnp.float32).astype(
        jnp.bfloat16
    )


def attend_back_kernel(
    count, reach, ends, q_ref, k_ref, v_ref, g_ref, cos_ref, sin_ref, dq_ref, dk_ref, dv_ref,
    dk_acc, dv_acc,
):
    i = pl.program_id(1)
    first = window_first(i, reach, k_ref.shape[0])
    keys = pl.ds(first, reach)
    here = pl.ds(pl.multiple_of(i * ROWS, ROWS), ROWS)
    scale = HEAD_DIM ** (-0.5)

    @pl.when(i == 0)
    def _():
        dk_acc[...] = jnp.zeros_like(dk_acc)
        dv_acc[...] = jnp.zeros_like(dv_acc)

    def turned_back(grad, cosine, sine):
        return turn_pairs(grad.astype(jnp.bfloat16).astype(jnp.float32), cosine, -sine)

    q = q_ref[...]
    k = k_ref[keys, :]
    grad = g_ref[...]
    probs = softmax_rows(window_scores(ends, count, q, k, first, i * ROWS))
    prob_grad = contract(grad, v_ref[keys, :], 1, 1)
    delta = jnp.sum(probs * prob_grad, axis=-1, keepdims=True)
    score_grad = (probs * (prob_grad - delta)).astype(jnp.bfloat16)
    dq = jnp.dot(score_grad, k, preferred_element_type=jnp.float32) * scale
    dq_ref[...] = turned_back(dq, cos_ref[here, :], sin_ref[here, :])
    dk_acc[keys, :] += contract(score_grad, q, 0, 0) * scale
    dv_acc[keys, :] += contract(probs.astype(jnp.bfloat16), grad, 0, 0)

    @pl.when(i == pl.num_programs(1) - 1)
    def _():
        dk_ref[...] = turned_back(dk_acc[...], cos_ref[...], sin_ref[...])
        dv_ref[...] = dv_acc[...].astype(jnp.bfloat16)


def attend(raw, scales, gains, lengths):
    seq_rows = raw.shape[0]
    span = raw.shape[1] // 3
    heads = span // HEAD_DIM
    reach = min(WINDOW + ROWS, seq_rows)
    count = lengths.shape[0]
    ends = jnp.cumsum(lengths)
    cosine, sine = rope_tables(jnp.arange(seq_rows, dtype=jnp.int32), HEAD_DIM)
    sign = jnp.where(jnp.arange(HEAD_DIM) < HEAD_DIM // 2, -1.0, 1.0)
    cosine, sine = cosine[:, 0], sine[:, 0] * sign

    def tile(group=0):
        return pl.BlockSpec((ROWS, HEAD_DIM), lambda h, i, ends: (i, group * heads + h))

    def whole(group=0):
        return pl.BlockSpec((seq_rows, HEAD_DIM), lambda h, i, ends: (0, group * heads + h))

    def fixed(array):
        return pl.BlockSpec(array.shape, lambda h, i, ends: (0, 0))

    pairs = seq_rows * heads * reach

    def call(kernel, ins, outs, types, scratch, name):
        return pl.pallas_call(
            kernel,
            grid_spec=pltpu.PrefetchScalarGridSpec(
                num_scalar_prefetch=1,
                grid=(heads, seq_rows // ROWS),
                in_specs=ins,
                out_specs=outs,
                scratch_shapes=scratch,
            ),
            out_shape=[jax.ShapeDtypeStruct((seq_rows, span), t) for t in types],
            compiler_params=pltpu.CompilerParams(
                dimension_semantics=("arbitrary", "arbitrary"), vmem_limit_bytes=56 * 2**20
            ),
            cost_estimate=pl.CostEstimate(
                flops=4 * len(outs) * pairs * HEAD_DIM,
                bytes_accessed=16 * seq_rows * span,
                transcendentals=pairs,
            ),
            name=name,
        )

    b16, f32 = jnp.bfloat16, jnp.float32
    tables = [fixed(cosine), fixed(sine)]
    row_scales = scales.T
    attended, query, key, value = call(
        functools.partial(attend_kernel, count, reach),
        [tile(0), whole(1), whole(2), fixed(row_scales)]
        + [pl.BlockSpec((2, HEAD_DIM), lambda h, i, ends: (0, h))]
        + tables,
        [tile(), tile(), whole(), whole()],
        [b16] * 4,
        [],
        "attend",
    )(ends, raw, raw, raw, row_scales, gains, cosine, sine)

    def back(grad):
        return call(
            functools.partial(attend_back_kernel, count, reach),
            [tile(), whole(), whole(), tile()] + tables,
            [tile(), whole(), whole()],
            [f32, f32, b16],
            [pltpu.VMEM((seq_rows, HEAD_DIM), f32)] * 2,
            "attend_back",
        )(ends, query, key, value, grad, cosine, sine)

    return attended, back


def scatter_over_all(partial, rows, sp_count, fs_count, ident, name):
    counts = mesh_counts(sp_count, fs_count)
    width = partial.shape[1]
    parts = 4 if rows % 64 == 0 else 2
    room = scatter_bytes(counts, parts, rows, width)
    room += 8 * counts[1] * counts[2] * rows // parts * width
    if room > VMEM_ROOM or rows % (parts * 16):
        part = lax.psum_scatter(partial, "fsdp", scatter_dimension=0, tiled=True)
        return lax.psum_scatter(part, "sp", scatter_dimension=0, tiled=True).astype(jnp.float32)
    n_hi, n_lo, n_x, n_core = counts
    shaped = partial.reshape(n_x, n_core, n_hi, n_lo, rows, width)
    return scatter_sum(shaped, counts, True, parts, jnp.float32, ident, name)


def combine_and_scatter(rows, rank, slots, sp_count, fs_count, ident, name):
    blocks, experts, block = rank.shape
    counts = mesh_counts(sp_count, fs_count)
    n_hi, n_lo, n_x, n_core = counts
    width = rows.shape[-1]
    parts = 4 if block % 64 == 0 else 2
    room = scatter_bytes(counts, parts, block, width)
    room += 4 * (n_x * n_core * n_lo * block + experts * slots) * width
    if n_core == 2 and room <= VMEM_ROOM and block % (parts * 16) == 0:
        return combine_sum(rows, rank, counts, parts, slots, ident, name)
    shaped = rows.reshape(experts, blocks, slots, -1)
    pick = (rank[:, :, None, :] == jnp.arange(slots)[None, None, :, None]).astype(jnp.bfloat16)
    partial = jnp.einsum("best,ebsw->btw", pick, shaped, preferred_element_type=jnp.float32)
    partial = partial.astype(jnp.bfloat16).reshape(blocks * block, -1)
    return scatter_over_all(partial, block, sp_count, fs_count, ident, name)


def scatter_over_fsdp(partial, rows, fs_count, ident, name):
    _, _, n_x, n_core = mesh_counts(1, fs_count)
    parts = 4 if rows % 64 == 0 else 2
    shaped = partial.reshape(n_x, n_core, 1, 1, rows, partial.shape[1])
    return scatter_sum(shaped, (1, 1, n_x, n_core), True, parts, jnp.float32, ident, name)


def gather_over_all(own, sp_count, fs_count, ident, name):
    parts = 4 if own.shape[0] % 64 == 0 else 2
    return gather_rows(own, mesh_counts(sp_count, fs_count), True, parts, ident, name)


def gather_over_sp(own, sp_count, ident, name):
    n_hi, n_lo, _, _ = mesh_counts(sp_count, 1)
    parts = 4 if own.shape[0] % 64 == 0 else 2
    return gather_rows(own, (n_hi, n_lo, 1, 1), False, parts, ident, name)


def sum_over_sp(rows, sp_count, ident, name):
    part = jnp.stack(rows)
    return small_sum(part.reshape(-1, 128), sp_count, 1, ident, name).reshape(part.shape)


def local(
    tokens,
    doc_lengths,
    expert_ids,
    norm_attn,
    norm_query,
    norm_key,
    norm_ffn,
    w_query,
    w_key,
    w_value,
    w_out,
    w_router,
    w_gate,
    w_up,
    w_down,
    cotangent,
):
    sp_count = lax.axis_size("sp")
    fs_count = lax.axis_size("fsdp")
    my_sp = lax.axis_index("sp")
    my_fs = lax.axis_index("fsdp")
    hidden_in = tokens[0].astype(jnp.float32)
    tok_rows, width = hidden_in.shape
    head_local = HEADS // sp_count
    seq_rows = tok_rows * sp_count
    span = head_local * HEAD_DIM
    expert_local = EXPERTS // sp_count
    first_expert = my_sp * expert_local
    gains = lax.all_gather(
        jnp.stack([norm_attn, norm_query, norm_key, norm_ffn]), "fsdp", axis=1, tiled=True
    ).astype(jnp.float32)
    gain_attn, gain_ffn = gains[0], gains[3]
    own_cols = lax.dynamic_slice_in_dim(gains, my_sp * span, span, axis=1)
    gain_query, gain_key = own_cols[1], own_cols[2]
    qkv_own = jnp.concatenate(
        [
            lax.dynamic_slice_in_dim(w, my_sp * span, span, axis=1)
            for w in (w_query, w_key, w_value)
        ],
        axis=1,
    )
    qkv_mat = lax.all_gather(qkv_own, "fsdp", axis=0, tiled=True)
    router_mat = lax.all_gather(w_router, "fsdp", axis=0, tiled=True)
    ids_own = jnp.pad(expert_ids[0].astype(jnp.bfloat16), ((0, 0), (0, LANES - TOPK)))
    cot_all = lax.all_gather(
        jnp.concatenate([cotangent[0], ids_own], axis=1), ("fsdp", "sp"), axis=0, tiled=True
    )
    ids_all = cot_all[:, width : width + TOPK].astype(jnp.int32)
    rank, live = route_plan(ids_all, tok_rows, sp_count)
    slots = 2 * tok_rows * TOPK // EXPERTS

    attn_normed, attn_pull = jax.vjp(rms_scale, hidden_in, gain_attn)
    n_hi, n_lo, n_x, n_core = mesh_counts(sp_count, fs_count)
    attn_in, out_mat = gather_two(
        attn_normed.astype(jnp.bfloat16), w_out, (n_hi, n_lo, 1, 1), (1, 1, n_x, n_core),
        4 if tok_rows % 64 == 0 else 2, 1, "gather_attn_in",
    )
    qkv_raw = jnp.dot(attn_in, qkv_mat, preferred_element_type=jnp.float32)
    raw = (qkv_raw[:, :span], qkv_raw[:, span : 2 * span])
    squares = sum_over_sp([jnp.sum(r * r, axis=-1) for r in raw], sp_count, 7, "sum_squares")
    scales = lax.rsqrt(squares / width + eps)
    attended_heads, attend_back = attend(qkv_raw, scales, own_cols[1:3], doc_lengths[0])
    scales = scales[:, :, None]
    attended_tok = lax.all_to_all(
        attended_heads, "sp", split_axis=0, concat_axis=1, tiled=True
    )
    after_attn = hidden_in + jnp.dot(attended_tok, out_mat, preferred_element_type=jnp.float32)
    ffn_normed, ffn_pull = jax.vjp(rms_scale, after_attn, gain_ffn)
    ffn_in = ffn_normed.astype(jnp.bfloat16)
    logits = jnp.dot(ffn_in, router_mat, preferred_element_type=jnp.float32)
    router = jax.nn.softmax(logits, axis=-1)
    router_high = router.astype(jnp.bfloat16)
    router_low = (router - router_high.astype(jnp.float32)).astype(jnp.bfloat16)
    ffn_rows, cot_rows = gather_and_dispatch(
        jnp.concatenate([ffn_in, router_high, router_low], axis=1),
        cot_all, width, rank, slots, sp_count, fs_count, 2, "gather_ffn_in",
    )
    in_grad_rows, out_rows, *inner_grads = run_experts(
        ffn_rows, cot_rows, w_gate, w_up, w_down, live, first_expert[None]
    )
    in_grad_sum = combine_and_scatter(
        in_grad_rows, rank, slots, sp_count, fs_count, 3, "scatter_grads"
    )
    moe_sum = combine_and_scatter(out_rows, rank, slots, sp_count, fs_count, 4, "scatter_outputs")
    mixed = (after_attn + moe_sum).astype(jnp.bfloat16)
    upstream = cotangent[0].astype(jnp.float32)
    ffn_in_grad = in_grad_sum[:, :width]
    router_grad = in_grad_sum[:, width : width + EXPERTS]
    logit_grad = (
        router * (router_grad - jnp.sum(router * router_grad, axis=-1, keepdims=True))
    ).astype(jnp.bfloat16)
    ffn_in_grad = ffn_in_grad + jnp.dot(
        logit_grad, router_mat.T, preferred_element_type=jnp.float32
    )
    ffn_hidden_grad, ffn_gain_term = ffn_pull(ffn_in_grad)
    after_grad = upstream + ffn_hidden_grad
    attn_out_grad = after_grad.astype(jnp.bfloat16)
    attended_grad = jnp.dot(attn_out_grad, out_mat.T, preferred_element_type=jnp.float32).astype(
        jnp.bfloat16
    )
    attended_grad_heads = lax.all_to_all(
        attended_grad, "sp", split_axis=1, concat_axis=0, tiled=True
    )
    row_terms = lax.dot_general(
        jnp.concatenate([attended_tok, ffn_in], axis=0),
        jnp.concatenate(
            [
                jnp.pad(attn_out_grad, ((0, 0), (0, LANES))),
                jnp.pad(logit_grad, ((0, 0), (width, LANES - EXPERTS))),
            ],
            axis=0,
        ),
        (((0,), (0,)), ((), ())),
        preferred_element_type=jnp.float32,
    ).astype(jnp.bfloat16)
    row_sums = scatter_over_all(
        row_terms, width // (sp_count * fs_count), sp_count, fs_count, 5, "scatter_out_rows"
    )
    attended_grad_heads, row_sums = lax.optimization_barrier((attended_grad_heads, row_sums))
    rows_every = lax.all_gather(row_sums.astype(jnp.bfloat16), "sp", axis=0, tiled=True)
    *normed_grads, value_low = attend_back(attended_grad_heads)
    scaled_grads = (normed_grads[0] * gain_query, normed_grads[1] * gain_key)
    products = sum_over_sp(
        [jnp.sum(g * r, axis=-1) for g, r in zip(scaled_grads, raw)], sp_count, 8, "sum_products"
    )[:, :, None]
    gain_terms = [
        jnp.sum(g * r * s, axis=0) for g, r, s in zip(normed_grads, raw, scales)
    ]
    raw_grads = [
        (g * s - r * (s * s * s) * (p / width)).astype(jnp.bfloat16)
        for g, r, s, p in zip(scaled_grads, raw, scales, products)
    ]
    qkv_low = jnp.concatenate(raw_grads + [value_low], axis=1)
    qkv_term = jnp.dot(attn_in.T, qkv_low, preferred_element_type=jnp.float32)
    qkv_sums = scatter_over_fsdp(
        qkv_term.astype(jnp.bfloat16), width // fs_count, fs_count, 11, "scatter_qkv"
    ).astype(jnp.bfloat16)
    qkv_every = lax.all_gather(qkv_sums, "sp", axis=0)
    attn_partial = lax.dot_general(
        qkv_low, qkv_mat, (((1,), (1,)), ((), ())), preferred_element_type=jnp.float32
    ).astype(jnp.bfloat16)
    attn_in_grad, grad_gate, grad_up, grad_down = scatter_and_grads(
        attn_partial.reshape(1, 1, n_hi, n_lo, tok_rows, width), (n_hi, n_lo, 1, 1),
        4 if tok_rows % 64 == 0 else 2, ffn_rows, cot_rows, inner_grads, 6, "scatter_attn_in",
    )
    attn_hidden_grad, attn_gain_term = attn_pull(attn_in_grad)
    grad_tokens = after_grad + attn_hidden_grad
    dense = [
        qkv_every[:, :, k * span : (k + 1) * span]
        .transpose(1, 0, 2)
        .reshape(-1, width)
        .astype(jnp.float32)
        for k in range(3)
    ]
    placed = [
        lax.dynamic_update_slice_in_dim(jnp.zeros((width,), jnp.float32), g, my_sp * span, 0)
        for g in gain_terms
    ]
    gain_sums = small_sum(
        jnp.stack([attn_gain_term, placed[0], placed[1], ffn_gain_term]).reshape(-1, 128),
        sp_count, fs_count, 9, "sum_gains",
    ).reshape(4, width)
    gain_sums = lax.dynamic_slice_in_dim(
        gain_sums, my_fs * (width // fs_count), width // fs_count, axis=1
    )
    return (
        mixed[None],
        grad_tokens[None],
        gain_sums[0],
        gain_sums[1],
        gain_sums[2],
        gain_sums[3],
        dense[0],
        dense[1],
        dense[2],
        rows_every[:, :width].astype(jnp.float32),
        rows_every[:, width : width + EXPERTS].astype(jnp.float32),
        grad_gate.astype(jnp.float32),
        grad_up.astype(jnp.float32),
        grad_down.astype(jnp.float32),
    )


def solution(mesh):
    in_specs = (
        P("fsdp", "sp", None),
        P("fsdp", None),
        P("fsdp", "sp", None),
        P("fsdp"),
        P("fsdp"),
        P("fsdp"),
        P("fsdp"),
        P("fsdp", None),
        P("fsdp", None),
        P("fsdp", None),
        P("fsdp", None),
        P("fsdp", None),
        P("sp", None, "fsdp"),
        P("sp", None, "fsdp"),
        P("sp", None, "fsdp"),
        P("fsdp", "sp", None),
    )
    out_specs = (
        P("fsdp", "sp", None),
        P("fsdp", "sp", None),
        P("fsdp"),
        P("fsdp"),
        P("fsdp"),
        P("fsdp"),
        P("fsdp", None),
        P("fsdp", None),
        P("fsdp", None),
        P("fsdp", None),
        P("fsdp", None),
        P("sp", None, "fsdp"),
        P("sp", None, "fsdp"),
        P("sp", None, "fsdp"),
    )
    return jax.shard_map(local, mesh=mesh, in_specs=in_specs, out_specs=out_specs, check_vma=False)
```
